32 devices in a mesh: row: 8 (over y, x, core), seg: 4 (over z).
Axes of the slice: x: 2, y: 2, z: 4, core: 2. Of those that a mesh axis runs over, the one named last changes fastest.
Arguments:
- tokens: bfloat16 [64, 1024, 768], P('row', 'seg'), may hold values from -6 to 6
- doc_ids: int32 [64, 8], P('row'), may hold values from 0 to 7, as said below
- w_qkv: bfloat16 [2, 768, 2304], replicated, may hold values from -0.21875 to 0.21875
- w_out: bfloat16 [2, 768, 768], replicated, may hold values from -0.875 to 0.875
- w_up: bfloat16 [2, 768, 3072], replicated, may hold values from -0.21875 to 0.21875
- w_down: bfloat16 [2, 3072, 768], replicated, may hold values from -0.109375 to 0.109375
- biases: bfloat16 [2, 6, 768], replicated, may hold values from -1 to 1
- gains: bfloat16 [2, 2, 768], replicated, may hold values from 0.5 to 1.5
- b_up: bfloat16 [2, 3072], replicated, may hold values from -1 to 1
- pos_table: bfloat16 [8, 768], replicated, may hold values from -3 to 3
- cotangent: bfloat16 [64, 1024, 768], P('row', 'seg'), may hold values from -6 to 6
Outputs:
- output: bfloat16 [64, 1024, 768], P('row', 'seg')
- grad_tokens: float32 [64, 1024, 768], P('row', 'seg')
- grad_w_qkv: float32 [1536, 2304], P(('row', 'seg'))
- grad_w_out: float32 [1536, 768], P(('row', 'seg'))
- grad_w_up: float32 [1536, 3072], P(('row', 'seg'))
- grad_w_down: float32 [6144, 768], P(('row', 'seg'))
- grad_biases: float32 [9216], P(('row', 'seg'))
- grad_gains: float32 [3072], P(('row', 'seg'))
- grad_b_up: float32 [6144], P(('row', 'seg'))
- grad_pos_table: float32 [6144], P(('row', 'seg'))
The draws below stay inside these ranges and needn't reach their ends.
Inputs may be any that keep to these rules, and one draw needn't show every extreme that they name: `doc_ids`: in each row the ids start at 0 and rise by 0 or 1 from one segment to the next; among rows 8 * g to 8 * g + 7 at least one row is a single document; where 8 is 2 or more, some row among the first 8 rows has every segment in a document of its own.
All inputs are finite; a program needn't handle non-finite values.
Results may differ from the reference program's by a relative error of at most 0.02.
Values may be sent and summed in bfloat16 or wider, within the bound.
A program may use at most 256 MiB of HBM per device.

```python
import jax
import jax.numpy as jnp
from jax import lax

D = 768
HDIM = 64
FF = 3072
SEGLEN = 128
ROWS_DEV = 8
ROWS = 64
SEGS = 8
LENGTH = 1024


def draw_doc_ids(key, part):
    key = jax.random.fold_in(key, 11)
    flag_key = jax.random.fold_in(key, 1)
    pick_key = jax.random.fold_in(key, 2)
    flags = (jax.random.randint(flag_key, (ROWS, SEGS), 0, 4) == 0).astype(jnp.int32)
    groups = ROWS // ROWS_DEV
    chosen = jnp.arange(groups) * ROWS_DEV + jax.random.randint(pick_key, (groups,), 0, ROWS_DEV)
    split_row = (chosen[0] + 1) % ROWS_DEV
    flags = jnp.where((jnp.arange(ROWS) == split_row)[:, None], 1, flags)
    single = jnp.any(jnp.arange(ROWS)[:, None] == chosen[None, :], axis=1)
    flags = jnp.where(single[:, None], 0, flags)
    flags = flags.at[:, 0].set(0)
    return jnp.cumsum(flags, axis=1).astype(jnp.int32)


def level_of(key, extent, cuts, low, top_value):
    factor_of, own = 1.0, jax.random.fold_in(key, 6)
    for dim, blocks in cuts:
        draws = jnp.exp(jax.random.uniform(jax.random.fold_in(own, dim), (blocks,), jnp.float32, low / len(cuts), top_value / len(cuts)))
        factor_of = factor_of * jnp.repeat(draws, extent[dim] // blocks).reshape([-1 if axis == dim else 1 for axis in range(len(extent))])
    return factor_of


def scatter_about(key, shape, scale, most, shards=(), held_as=jnp.bfloat16):
    values = scale * jax.random.normal(key, shape, jnp.float32)
    if shards:
        values = values * level_of(key, shape, shards, -0.22, 0.18)
    return jnp.clip(values, -most, most).astype(held_as)


def setup_inputs(seed: int = 0) -> dict:
    splits = jax.random.split(jax.random.key(seed), 12)
    return {
        "tokens": scatter_about(splits[0], (ROWS, LENGTH, D), 1.0, 6.0, ((0, 8), (1, 4))),
        "doc_ids": draw_doc_ids(jax.random.fold_in(splits[11], 71), 0),
        "w_qkv": scatter_about(splits[2], (2, D, 3 * D), D ** -0.5, 0.21875),
        "w_out": scatter_about(splits[3], (2, D, D), (D // 16) ** -0.5, 0.875),
        "w_up": scatter_about(splits[4], (2, D, FF), D ** -0.5, 0.21875),
        "w_down": scatter_about(splits[5], (2, FF, D), FF ** -0.5, 0.109375),
        "biases": scatter_about(splits[6], (2, 6, D), 0.2, 1.0),
        "gains": jnp.clip(1.0 + 0.1 * jax.random.normal(splits[7], (2, 2, D), jnp.float32), 0.5, 1.5).astype(jnp.bfloat16),
        "b_up": scatter_about(splits[8], (2, FF), 0.2, 1.0),
        "pos_table": scatter_about(splits[9], (SEGS, D), 0.5, 3.0),
        "cotangent": scatter_about(splits[10], (ROWS, LENGTH, D), 1.0, 6.0, ((0, 8), (1, 4))),
    }


@jax.custom_vjp
def low(v):
    return lax.optimization_barrier(v.astype(jnp.bfloat16)).astype(jnp.float32)

@jax.custom_vjp
def low_back(v):
    return v

def low_keep(v):
    return (low(v), None)

def low_pass(kept, grad):
    return (grad,)

def back_keep(v):
    return (v, None)

def back_low(kept, grad):
    return (low(grad),)
low.defvjp(low_keep, low_pass)
low_back.defvjp(back_keep, back_low)
NEGATIVE = -1000000000.0
EPSILON = 1e-05

def layer_norm(values, gain, shift):
    centered = values - lax.optimization_barrier(jnp.mean(values, axis=-1, keepdims=True))
    variance = lax.optimization_barrier(jnp.mean(centered * centered, axis=-1, keepdims=True))
    return centered * lax.rsqrt(variance + EPSILON) * gain + shift

def matmul(values, matrix):
    return jnp.einsum('...i,ij->...j', values, matrix, precision=lax.Precision.HIGHEST)

def attention(proj_qkv, allowed):
    batch, number, triple = proj_qkv.shape
    model_width = triple // 3
    heads = model_width // HDIM
    split = proj_qkv.reshape(batch, number, 3, heads, HDIM)
    query, keys, values = (split[:, :, 0], split[:, :, 1], split[:, :, 2])
    scores = jnp.einsum('bqhd,bkhd->bhqk', query, keys, precision=lax.Precision.HIGHEST) * HDIM ** (-0.5)
    if allowed is not None:
        scores = jnp.where(allowed[:, None], scores, NEGATIVE)
    scores = low_back(scores)
    attn_probs = low(jax.nn.softmax(scores, axis=-1))
    mixed = jnp.einsum('bhqk,bkhd->bqhd', attn_probs, values, precision=lax.Precision.HIGHEST)
    return low(low_back(mixed.reshape(batch, number, model_width)))

def block(rows, index, allowed, weights):
    w_qkv, w_out, w_up, w_down, biases, gains, b_up = weights
    bias = biases[index]
    gain = gains[index]
    qkv_bias = jnp.concatenate([bias[0], jnp.zeros_like(bias[0]), bias[1]])
    proj_qkv = low(low_back(matmul(rows, w_qkv[index]) + qkv_bias))
    mixed = attention(proj_qkv, allowed)
    branch = low_back(matmul(mixed, w_out[index]) + bias[2])
    first = low(layer_norm(rows + branch, gain[0], bias[3]))
    inner = low_back(matmul(first, w_up[index]) + b_up[index])
    hidden = low(jax.nn.gelu(inner))
    second = low_back(matmul(hidden, w_down[index]) + bias[4])
    return low(layer_norm(first + second, gain[1], bias[5]))

def forward(tokens, doc_ids, w_qkv, w_out, w_up, w_down, biases, gains, b_up, pos_table):
    weights = (w_qkv, w_out, w_up, w_down, biases, gains, b_up)
    row_count, length, model_width = tokens.shape
    segments = length // SEGLEN
    seg_out = block(tokens.reshape(row_count * segments, SEGLEN, model_width), 0, None, weights)
    seg_out = seg_out.reshape(row_count, segments, SEGLEN, model_width)
    seg_place = jnp.arange(segments)
    same_doc = doc_ids[:, :, None] == doc_ids[:, None, :]
    doc_start = lax.optimization_barrier(jnp.min(jnp.where(same_doc, seg_place[None, None, :], segments), axis=2))
    position = seg_place[None, :] - doc_start
    cls_in = low(seg_out[:, :, 0] + pos_table[position])
    cls_out = block(cls_in, 1, same_doc, weights)
    return seg_out.at[:, :, 0].set(cls_out).reshape(row_count, length, model_width)

def reference(tokens, doc_ids, w_qkv, w_out, w_up, w_down, biases, gains, b_up, pos_table, cotangent):
    params = tuple((array_in.astype(jnp.float32) for array_in in (w_qkv, w_out, w_up, w_down, biases, gains, b_up, pos_table)))
    groups = ROWS // ROWS_DEV

    def one_group(summed, pieces):
        group_tokens, group_docs, group_cot = pieces

        def run_forward(values, *weights):
            return forward(values, group_docs, *weights)
        result, pullback = jax.vjp(run_forward, group_tokens.astype(jnp.float32), *params)
        gradients = pullback(group_cot.astype(jnp.float32))
        summed = tuple((before + after for before, after in zip(summed, gradients[1:])))
        return (summed, (result.astype(jnp.bfloat16), gradients[0]))
    initial = tuple((jnp.zeros_like(array_in) for array_in in params))
    summed, (output, grad_tokens) = lax.scan(one_group, initial, (tokens.reshape(groups, ROWS_DEV, LENGTH, D), doc_ids.reshape(groups, ROWS_DEV, SEGS), cotangent.reshape(groups, ROWS_DEV, LENGTH, D)))
    return (output.reshape(ROWS, LENGTH, D), grad_tokens.reshape(ROWS, LENGTH, D), summed[0].reshape(2 * D, 3 * D), summed[1].reshape(2 * D, D), summed[2].reshape(2 * D, FF), summed[3].reshape(2 * FF, D), summed[4].reshape(12 * D), summed[5].reshape(4 * D), summed[6].reshape(2 * FF), summed[7].reshape(SEGS * D))
```

```python
import functools

import jax
import jax.numpy as jnp
from jax import lax
from jax.experimental import pallas as pl
from jax.experimental.pallas import tpu as pltpu
from jax.sharding import PartitionSpec as P


HDIM = 64
SEGLEN = 128
LANES = 128
EPSILON = 1e-05
GELU_A = 0.7978845608028654
GELU_B = 0.044715 * GELU_A
F32, BF16 = jnp.float32, jnp.bfloat16


def mm(a, b):
    return lax.dot_general(a, b, (((1,), (0,)), ((), ())), preferred_element_type=F32)


def mm_nt(a, b):
    return lax.dot_general(a, b, (((1,), (1,)), ((), ())), preferred_element_type=F32)


def mm_tn(a, b):
    return lax.dot_general(a, b, (((0,), (0,)), ((), ())), preferred_element_type=F32)


def low_lanes(shape):
    return lax.broadcasted_iota(jnp.int32, shape, 1) < HDIM


def stack_heads(pair):
    keep = low_lanes(pair.shape)
    zero = jnp.zeros_like(pair)
    return jnp.concatenate([jnp.where(keep, pair, zero), jnp.where(keep, zero, pair)], axis=0)


def norm_stats(values):
    centered = values - jnp.mean(values, axis=-1, keepdims=True)
    variance = jnp.mean(centered * centered, axis=-1, keepdims=True)
    rstd = lax.rsqrt(variance + EPSILON)
    return centered * rstd, rstd


def gelu_both(u):
    square = u * u
    t = jnp.tanh(u * (GELU_A + GELU_B * square))
    half = 0.5 * u
    hidden = half + half * t
    slope = 0.5 + 0.5 * t + half * (1.0 - t * t) * (GELU_A + (3.0 * GELU_B) * square)
    return hidden, slope


def forward_kernel(
    x_ref, wqkv_hbm, wout_hbm, wup_hbm, wdown_hbm, bias_ref, gain_ref, bup_ref,
    qkv_ref, probs_ref, n1_ref, r1_ref, slope_ref, n2_ref, r2_ref, y_ref, cls_ref, xt_ref, mixedt_ref, firstt_ref, hiddent_ref,
    wqkv, wout, wup, wdown, mixed_ref, sems, *, ff_chunk,
):
    step = pl.program_id(0)
    copies = [
        pltpu.make_async_copy(src.at[0], dst, sems.at[i])
        for i, (src, dst) in enumerate(
            ((wqkv_hbm, wqkv), (wout_hbm, wout), (wup_hbm, wup), (wdown_hbm, wdown))
        )
    ]

    @pl.when(step == 0)
    def _():
        for copy in copies:
            copy.start()
        copies[0].wait()

    rows, width = x_ref.shape
    bias = bias_ref[...].astype(F32)
    gain = gain_ref[...].astype(F32)
    x = x_ref[...]
    xt_ref[...] = x.T
    for part in range(3):
        cols = slice(part * width, (part + 1) * width)
        out = mm(x, wqkv[:, cols])
        if part == 0:
            out = out + bias[0:1]
        if part == 2:
            out = out + bias[1:2]
        qkv_ref[:, cols] = out.astype(BF16)
    for seg in range(rows // SEGLEN):
        at = slice(seg * SEGLEN, (seg + 1) * SEGLEN)
        for pair in range(width // LANES):
            q = qkv_ref[at, pair * LANES : (pair + 1) * LANES]
            k = qkv_ref[at, width + pair * LANES : width + (pair + 1) * LANES]
            v = qkv_ref[at, 2 * width + pair * LANES : 2 * width + (pair + 1) * LANES]
            scores = mm_nt(k, stack_heads(q * HDIM**-0.5))
            e = jnp.exp(scores - jnp.max(scores, axis=0, keepdims=True))
            p = (e * (1.0 / jnp.sum(e, axis=0, keepdims=True))).astype(BF16)
            probs_ref[seg, pair] = p
            pt = jnp.concatenate([p[:, :SEGLEN].T, p[:, SEGLEN:].T], axis=1)
            mixed_ref[at, pair * LANES : (pair + 1) * LANES] = mm(pt, stack_heads(v)).astype(BF16)

    @pl.when(step == 0)
    def _():
        for copy in copies[1:]:
            copy.wait()

    mixed = mixed_ref[...]
    mixedt_ref[...] = mixed.T
    resid = x.astype(F32) + mm(mixed, wout[...]) + bias[2:3]
    n1, r1 = norm_stats(resid)
    n1_ref[...] = n1.astype(BF16)
    r1_ref[...] = jnp.broadcast_to(r1, r1_ref.shape)
    first = (n1 * gain[0:1] + bias[3:4]).astype(BF16)
    firstt_ref[...] = first.T
    total = first.astype(F32) + bias[4:5]
    inners = wup.shape[1]
    for c in range(inners // ff_chunk):
        cols = slice(c * ff_chunk, (c + 1) * ff_chunk)
        inner = mm(first, wup[:, cols]) + bup_ref[:, cols].astype(F32)
        hidden, slope = gelu_both(inner)
        hidden = hidden.astype(BF16)
        hiddent_ref[cols, :] = hidden.T
        slope_ref[:, cols] = slope.astype(BF16)
        total = total + mm(hidden, wdown[cols, :])
    n2, r2 = norm_stats(total)
    n2_ref[...] = n2.astype(BF16)
    r2_ref[...] = jnp.broadcast_to(r2, r2_ref.shape)
    y = (n2 * gain[1:2] + bias[5:6]).astype(BF16)
    y_ref[...] = y
    for seg in range(rows // SEGLEN):
        cls_ref[pl.ds(step * (rows // SEGLEN) + seg, 1), :] = y[seg * SEGLEN : seg * SEGLEN + 8].astype(F32)[0:1]


def forward_block(x, w_qkv, w_out, w_up, w_down, bias, gain, bup, tile=256, ff_chunk=768):
    total, width = x.shape
    inners = w_up.shape[-1]
    segs = tile // SEGLEN
    pairs = width // LANES
    any_spec = pl.BlockSpec(memory_space=pl.ANY)

    def rows_of(cols):
        return pl.BlockSpec((tile, cols), lambda i: (i, 0))

    def whole(a):
        return pl.BlockSpec(a.shape, lambda i: (0,) * a.ndim)

    def cols_of(rows):
        return pl.BlockSpec((rows, tile), lambda i: (0, i))

    outs = [
        ((total, 3 * width), BF16, rows_of(3 * width)),
        ((total // SEGLEN, pairs, SEGLEN, 2 * SEGLEN), BF16, pl.BlockSpec((segs, pairs, SEGLEN, 2 * SEGLEN), lambda i: (i, 0, 0, 0))),
        ((total, width), BF16, rows_of(width)),
        ((total, LANES), F32, rows_of(LANES)),
        ((total, inners), BF16, rows_of(inners)),
        ((total, width), BF16, rows_of(width)),
        ((total, LANES), F32, rows_of(LANES)),
        ((total, width), BF16, rows_of(width)),
        ((total // SEGLEN, width), F32, pl.BlockSpec((total // SEGLEN, width), lambda i: (0, 0))),
        ((width, total), BF16, cols_of(width)),
        ((width, total), BF16, cols_of(width)),
        ((width, total), BF16, cols_of(width)),
        ((inners, total), BF16, cols_of(inners)),
    ]
    return pl.pallas_call(
        functools.partial(forward_kernel, ff_chunk=ff_chunk),
        grid=(total // tile,),
        in_specs=[rows_of(width), any_spec, any_spec, any_spec, any_spec, whole(bias), whole(gain), whole(bup)],
        out_specs=[o[2] for o in outs],
        out_shape=[jax.ShapeDtypeStruct(o[0], o[1]) for o in outs],
        scratch_shapes=[
            pltpu.VMEM(w_qkv.shape[1:], BF16),
            pltpu.VMEM(w_out.shape[1:], BF16),
            pltpu.VMEM(w_up.shape[1:], BF16),
            pltpu.VMEM(w_down.shape[1:], BF16),
            pltpu.VMEM((tile, width), BF16),
            pltpu.SemaphoreType.DMA((4,)),
        ],
        compiler_params=pltpu.CompilerParams(vmem_limit_bytes=60 * 2**20),
        name="segment_forward",
    )(x, w_qkv, w_out, w_up, w_down, bias, gain, bup)

def fold_rows(values):
    rows, cols = values.shape
    return jnp.sum(values.reshape(rows // 8, 8, cols), axis=0)


def norm_back(grad, gain, normal, rstd):
    scaled = grad * gain
    a = jnp.mean(scaled, axis=-1, keepdims=True)
    b = jnp.mean(scaled * normal, axis=-1, keepdims=True)
    return (scaled - a - normal * b) * rstd


def backward_kernel(
    gcls_ref, ccls_ref, cot_ref, y_ref, n2_ref, r2_ref, slope_ref, n1_ref, r1_ref, qkv_ref, probs_ref,
    wqkv_hbm, wout_hbm, wup_hbm, wdown_hbm, gain_ref,
    out_ref, gsecond_ref, ginner_ref, gbranch_ref, gqkv_ref, gx_ref, sums_ref, bsums_ref,
    wqkv, wout, wup, wdown, sems, *, ff_chunk,
):
    step = pl.program_id(0)
    copies = [
        pltpu.make_async_copy(src.at[0], dst, sems.at[i])
        for i, (src, dst) in enumerate(
            ((wdown_hbm, wdown), (wup_hbm, wup), (wout_hbm, wout), (wqkv_hbm, wqkv))
        )
    ]

    @pl.when(step == 0)
    def _():
        for copy in copies:
            copy.start()
        sums_ref[...] = jnp.zeros_like(sums_ref)
        bsums_ref[...] = jnp.zeros_like(bsums_ref)
        for copy in copies[:2]:
            copy.wait()

    rows, width = cot_ref.shape
    segs = rows // SEGLEN
    inners = wup.shape[1]
    gain = gain_ref[...].astype(F32)
    place = lax.broadcasted_iota(jnp.int32, (rows, width), 0)
    gy = cot_ref[...].astype(F32)
    y = y_ref[...].astype(F32)
    for seg in range(segs):
        at = pl.ds(step * segs + seg, 1)
        gy = jnp.where(place == seg * SEGLEN, gcls_ref[at, :], gy)
        y = jnp.where(place == seg * SEGLEN, ccls_ref[at, :], y)
    out_ref[...] = y.astype(BF16)
    n2 = n2_ref[...].astype(F32)
    sums_ref[0] += fold_rows(gy * n2)
    sums_ref[1] += fold_rows(gy)
    g_two = norm_back(gy, gain[1:2], n2, r2_ref[:, 0:1])
    g_second = g_two.astype(BF16)
    gsecond_ref[...] = g_second
    sums_ref[2] += fold_rows(g_second.astype(F32))
    g_first = g_two
    for c in range(inners // ff_chunk):
        cols = slice(c * ff_chunk, (c + 1) * ff_chunk)
        g_inner = mm_nt(g_second, wdown[cols, :]) * slope_ref[:, cols].astype(F32)
        g_low = g_inner.astype(BF16)
        ginner_ref[:, cols] = g_low
        bsums_ref[:, cols] += fold_rows(g_low.astype(F32))
        g_first = g_first + mm_nt(g_low, wup[:, cols])
    n1 = n1_ref[...].astype(F32)
    sums_ref[3] += fold_rows(g_first * n1)
    sums_ref[4] += fold_rows(g_first)
    g_one = norm_back(g_first, gain[0:1], n1, r1_ref[:, 0:1])
    g_branch = g_one.astype(BF16)
    gbranch_ref[...] = g_branch
    sums_ref[5] += fold_rows(g_branch.astype(F32))

    @pl.when(step == 0)
    def _():
        for copy in copies[2:]:
            copy.wait()

    g_mixed = mm_nt(g_branch, wout[...]).astype(BF16)
    for seg in range(segs):
        at = slice(seg * SEGLEN, (seg + 1) * SEGLEN)
        for pair in range(width // LANES):
            lanes = [slice(part * width + pair * LANES, part * width + (pair + 1) * LANES) for part in range(3)]
            q = qkv_ref[at, lanes[0]] * HDIM**-0.5
            k = qkv_ref[at, lanes[1]]
            v = qkv_ref[at, lanes[2]]
            p_low = probs_ref[seg, pair]
            p = p_low.astype(F32)
            g_out = stack_heads(g_mixed[at, lanes[0]])
            g_p = mm_nt(v, g_out)
            inner_sum = jnp.sum(g_p * p, axis=0, keepdims=True)
            g_s = (p * (g_p - inner_sum)).astype(BF16)
            g_v = mm(p_low, g_out)
            g_k = mm(g_s, stack_heads(q))
            g_st = jnp.concatenate([g_s[:, :SEGLEN].T, g_s[:, SEGLEN:].T], axis=1)
            g_q = mm(g_st, stack_heads(k)) * HDIM**-0.5
            gqkv_ref[at, lanes[0]] = g_q.astype(BF16)
            gqkv_ref[at, lanes[1]] = g_k.astype(BF16)
            gqkv_ref[at, lanes[2]] = g_v.astype(BF16)
    g_qkv = gqkv_ref[...]
    sums_ref[6] += fold_rows(g_qkv[:, :width].astype(F32))
    sums_ref[7] += fold_rows(g_qkv[:, 2 * width :].astype(F32))
    gx_ref[...] = g_one + mm_nt(g_qkv, wqkv[...])


def backward_block(gcls, ccls, cot, y, n2, r2, slope, n1, r1, qkv, probs, w_qkv, w_out, w_up, w_down, gain, tile=256, ff_chunk=768):
    total, width = cot.shape
    inners = w_up.shape[-1]
    segs = tile // SEGLEN
    pairs = width // LANES
    any_spec = pl.BlockSpec(memory_space=pl.ANY)

    def rows_of(cols):
        return pl.BlockSpec((tile, cols), lambda i: (i, 0))

    def whole(a):
        return pl.BlockSpec(a.shape, lambda i: (0,) * len(a.shape))

    outs = [
        ((total, width), BF16, rows_of(width)),
        ((total, width), BF16, rows_of(width)),
        ((total, inners), BF16, rows_of(inners)),
        ((total, width), BF16, rows_of(width)),
        ((total, 3 * width), BF16, rows_of(3 * width)),
        ((total, width), F32, rows_of(width)),
        ((8, 8, width), F32, pl.BlockSpec((8, 8, width), lambda i: (0, 0, 0))),
        ((8, inners), F32, pl.BlockSpec((8, inners), lambda i: (0, 0))),
    ]
    return pl.pallas_call(
        functools.partial(backward_kernel, ff_chunk=ff_chunk),
        grid=(total // tile,),
        in_specs=[whole(gcls), whole(ccls), rows_of(width), rows_of(width), rows_of(width), rows_of(LANES), rows_of(inners),
                  rows_of(width), rows_of(LANES), rows_of(3 * width),
                  pl.BlockSpec((segs, pairs, SEGLEN, 2 * SEGLEN), lambda i: (i, 0, 0, 0)),
                  any_spec, any_spec, any_spec, any_spec, whole(gain)],
        out_specs=[o[2] for o in outs],
        out_shape=[jax.ShapeDtypeStruct(o[0], o[1]) for o in outs],
        scratch_shapes=[
            pltpu.VMEM(w_qkv.shape[1:], BF16),
            pltpu.VMEM(w_out.shape[1:], BF16),
            pltpu.VMEM(w_up.shape[1:], BF16),
            pltpu.VMEM(w_down.shape[1:], BF16),
            pltpu.SemaphoreType.DMA((4,)),
        ],
        compiler_params=pltpu.CompilerParams(vmem_limit_bytes=60 * 2**20),
        name="segment_backward",
    )(gcls, ccls, cot, y, n2, r2, slope, n1, r1, qkv, probs, w_qkv, w_out, w_up, w_down, gain)

NEGATIVE = -1000000000.0
MESH = pl.DeviceIdType.MESH


def turned(values):
    return values.astype(F32).T.astype(BF16)


def cross_kernel(
    cls_ref, cot_ref, place_ref, keycol_ref, keyrow_ref, table_ref, wqkv_hbm, wout_hbm, wup_hbm, wdown_hbm, bias_ref, gain_ref, bup_ref,
    ccls_ref, gcls_ref, sums_ref, bsums_ref, gpos_ref, xt_ref, mixedt_ref, firstt_ref, hiddent_ref, gqkv_ref, gbranch_ref, ginner_ref, gsecond_ref,
    wqkv, wout, wup, wdown, packed, gathered, qkv_ref, probs_ref, mixed_ref, slope_ref, whole_ref, sems, send_sems, recv_sems, *, ff_chunk, devices,
):
    copies = [
        pltpu.make_async_copy(src.at[1], dst, sems.at[i])
        for i, (src, dst) in enumerate(
            ((wqkv_hbm, wqkv), (wout_hbm, wout), (wup_hbm, wup), (wdown_hbm, wdown))
        )
    ]
    for copy in copies:
        copy.start()
    own, width = cls_ref.shape
    rows = own * devices
    inners = wup.shape[1]
    me = lax.axis_index("seg")
    line = lax.axis_index("row")
    barrier = pltpu.get_barrier_semaphore()
    for hop in range(1, devices):
        pl.semaphore_signal(barrier, inc=1, device_id=(line, lax.rem(me + hop, devices)), device_id_type=MESH)
    packed[0:own, :] = cls_ref[...].astype(BF16)
    packed[own:, :] = cot_ref[...]
    pl.semaphore_wait(barrier, devices - 1)
    sends = []
    for hop in range(1, devices):
        send = pltpu.make_async_remote_copy(
            src_ref=packed, dst_ref=gathered.at[hop], send_sem=send_sems.at[hop], recv_sem=recv_sems.at[hop],
            device_id=(line, lax.rem(me + hop, devices)), device_id_type=MESH,
        )
        send.start()
        sends.append(send)
    bias = bias_ref[...].astype(F32)
    gain = gain_ref[...].astype(F32)
    onehot = (place_ref[...] == lax.broadcasted_iota(jnp.int32, (rows, table_ref.shape[0]), 1)).astype(F32)
    embed = mm(onehot.astype(BF16), table_ref[...])
    allowed = keycol_ref[...] == keyrow_ref[...]
    gathered[0] = packed[...]
    for send in sends:
        send.wait()
    for hop in range(devices):
        at = pl.ds(pl.multiple_of(lax.rem(me - hop + devices, devices) * own, own), own)
        block = gathered[hop].astype(F32)
        whole_ref[0, at, :] = block[:own]
        whole_ref[1, at, :] = block[own:]
    x = (whole_ref[0] + embed).astype(BF16)
    gy = whole_ref[1]
    xt_ref[...] = turned(x)
    copies[0].wait()
    for part in range(3):
        cols = slice(part * width, (part + 1) * width)
        out = mm(x, wqkv[:, cols])
        if part == 0:
            out = out + bias[0:1]
        if part == 2:
            out = out + bias[1:2]
        qkv_ref[:, cols] = out.astype(BF16)
    for pair in range(width // LANES):
        q, k, v = (qkv_ref[:, part * width + pair * LANES : part * width + (pair + 1) * LANES] for part in range(3))
        scores = jnp.where(allowed, mm_nt(k, stack_heads(q * HDIM**-0.5)), NEGATIVE)
        e = jnp.exp(scores - jnp.max(scores, axis=0, keepdims=True))
        p = e * (1.0 / jnp.sum(e, axis=0, keepdims=True))
        probs_ref[pair] = p
        pt = p.T.astype(BF16)
        low = low_lanes((rows, LANES))
        mixed = jnp.where(low, mm(pt[:rows], v), mm(pt[rows:], v))
        mixed_ref[:, pair * LANES : (pair + 1) * LANES] = mixed.astype(BF16)
    copies[1].wait()
    mixed = mixed_ref[...]
    mixedt_ref[...] = turned(mixed)
    n1, r1 = norm_stats(x.astype(F32) + mm(mixed, wout[...]) + bias[2:3])
    first = (n1 * gain[0:1] + bias[3:4]).astype(BF16)
    firstt_ref[...] = turned(first)
    copies[2].wait()
    copies[3].wait()
    total = first.astype(F32) + bias[4:5]
    for c in range(inners // ff_chunk):
        cols = slice(c * ff_chunk, (c + 1) * ff_chunk)
        hidden, slope = gelu_both(mm(first, wup[:, cols]) + bup_ref[:, cols].astype(F32))
        hidden = hidden.astype(BF16)
        hiddent_ref[cols, :] = turned(hidden)
        slope_ref[:, cols] = slope
        total = total + mm(hidden, wdown[cols, :])
    n2, r2 = norm_stats(total)
    mine = pl.ds(pl.multiple_of(me * own, own), own)
    whole_ref[0] = (n2 * gain[1:2] + bias[5:6]).astype(BF16).astype(F32)
    ccls_ref[...] = whole_ref[0, mine, :]

    def row_sum(values):
        return jnp.sum(values.astype(F32), axis=0, keepdims=True)

    sums_ref[0:1, :] = row_sum(gy * n2)
    sums_ref[1:2, :] = row_sum(gy)
    g_two = norm_back(gy, gain[1:2], n2, r2)
    g_second = g_two.astype(BF16)
    gsecond_ref[...] = g_second
    sums_ref[2:3, :] = row_sum(g_second)
    g_first = g_two
    for c in range(inners // ff_chunk):
        cols = slice(c * ff_chunk, (c + 1) * ff_chunk)
        g_inner = (mm_nt(g_second, wdown[cols, :]) * slope_ref[:, cols]).astype(BF16)
        ginner_ref[:, cols] = g_inner
        bsums_ref[:, cols] = row_sum(g_inner)
        g_first = g_first + mm_nt(g_inner, wup[:, cols])
    sums_ref[3:4, :] = row_sum(g_first * n1)
    sums_ref[4:5, :] = row_sum(g_first)
    g_one = norm_back(g_first, gain[0:1], n1, r1)
    g_branch = g_one.astype(BF16)
    gbranch_ref[...] = g_branch
    sums_ref[5:6, :] = row_sum(g_branch)
    g_mixed = mm_nt(g_branch, wout[...]).astype(BF16)
    for pair in range(width // LANES):
        lanes = [slice(part * width + pair * LANES, part * width + (pair + 1) * LANES) for part in range(3)]
        q, k, v = (qkv_ref[:, at] for at in lanes)
        p = probs_ref[pair]
        g_out = stack_heads(g_mixed[:, lanes[0]])
        g_p = mm_nt(v, g_out)
        g_s = p * (g_p - jnp.sum(g_p * p, axis=0, keepdims=True))
        g_st = g_s.T.astype(BF16)
        g_s = g_s.astype(BF16)
        low = low_lanes((rows, LANES))
        g_q = jnp.where(low, mm(g_st[:rows], k), mm(g_st[rows:], k)) * HDIM**-0.5
        gqkv_ref[:, lanes[0]] = g_q.astype(BF16)
        gqkv_ref[:, lanes[1]] = mm(g_s, stack_heads(q * HDIM**-0.5)).astype(BF16)
        gqkv_ref[:, lanes[2]] = mm(p.astype(BF16), g_out).astype(BF16)
    g_qkv = gqkv_ref[...]
    sums_ref[6:7, :] = row_sum(g_qkv[:, :width])
    sums_ref[7:8, :] = row_sum(g_qkv[:, 2 * width :])
    g_x = g_one + mm_nt(g_qkv, wqkv[...])
    whole_ref[1] = g_x
    gcls_ref[...] = whole_ref[1, mine, :]
    gpos_ref[...] = lax.dot_general(onehot, g_x, (((0,), (0,)), ((), ())), preferred_element_type=F32, precision=lax.Precision.HIGHEST)


def cross_block(cls, cot, place, keys, table, w_qkv, w_out, w_up, w_down, bias, gain, bup, devices, ff_chunk=768):
    own, width = cls.shape
    rows = own * devices
    inners = w_up.shape[-1]
    vmem = pl.BlockSpec(memory_space=pltpu.VMEM)
    any_spec = pl.BlockSpec(memory_space=pl.ANY)
    outs = [
        ((own, width), F32), ((own, width), F32), ((8, width), F32), ((1, inners), F32), (table.shape, F32),
        ((width, rows), BF16), ((width, rows), BF16), ((width, rows), BF16), ((inners, rows), BF16),
        ((rows, 3 * width), BF16), ((rows, width), BF16), ((rows, inners), BF16), ((rows, width), BF16),
    ]
    return pl.pallas_call(
        functools.partial(cross_kernel, ff_chunk=ff_chunk, devices=devices),
        in_specs=[vmem] * 6 + [any_spec] * 4 + [vmem] * 3,
        out_specs=[vmem] * len(outs),
        out_shape=[jax.ShapeDtypeStruct(*o) for o in outs],
        scratch_shapes=[
            pltpu.VMEM(w_qkv.shape[1:], BF16),
            pltpu.VMEM(w_out.shape[1:], BF16),
            pltpu.VMEM(w_up.shape[1:], BF16),
            pltpu.VMEM(w_down.shape[1:], BF16),
            pltpu.VMEM((2 * own, width), BF16),
            pltpu.VMEM((devices, 2 * own, width), BF16),
            pltpu.VMEM((rows, 3 * width), BF16),
            pltpu.VMEM((width // LANES, rows, 2 * rows), F32),
            pltpu.VMEM((rows, width), BF16),
            pltpu.VMEM((rows, inners), F32),
            pltpu.VMEM((2, rows, width), F32),
            pltpu.SemaphoreType.DMA((4,)),
            pltpu.SemaphoreType.DMA((devices,)),
            pltpu.SemaphoreType.DMA((devices,)),
        ],
        compiler_params=pltpu.CompilerParams(vmem_limit_bytes=50 * 2**20, collective_id=0, has_side_effects=True),
        name="cross_block",
    )(cls, cot, place, keys, jnp.tile(keys.reshape(1, rows), (1, 2)), table, w_qkv, w_out, w_up, w_down, bias, gain, bup)

def small_grads(sums, bsums, csums, cbsums, gpos, cross_share):
    seg_rows = jnp.sum(sums, axis=1)
    cross_rows = csums * cross_share
    seg_up = jnp.sum(bsums, axis=0)
    order = jnp.array([6, 7, 5, 4, 2, 1])
    biases = jnp.stack([seg_rows[order], cross_rows[order]])
    gains = jnp.stack([seg_rows[jnp.array([3, 0])], cross_rows[jnp.array([3, 0])]])
    ups = jnp.stack([seg_up, cbsums[0] * cross_share])
    return biases.reshape(-1), gains.reshape(-1), ups.reshape(-1), (gpos * cross_share).reshape(-1)


def per_device(
    tokens, doc_ids, w_qkv, w_out, w_up, w_down, biases, gains, b_up, pos_table, cotangent, *, sizes
):
    lines, planes = sizes
    row_count, local_length, width = tokens.shape
    seg_here = local_length // SEGLEN
    segments = doc_ids.shape[1]
    total = row_count * local_length
    own = row_count * seg_here
    me = lax.axis_index("seg")
    axes = ("row", "seg")

    seg_place = jnp.arange(segments)
    same_doc = doc_ids[:, :, None] == doc_ids[:, None, :]
    doc_start = jnp.min(jnp.where(same_doc, seg_place[None, None, :], segments), axis=2)

    def by_device(values):
        return values.reshape(row_count, planes, seg_here).transpose(1, 0, 2).reshape(-1, 1)

    place = by_device(seg_place[None, :] - doc_start)
    keys = by_device(doc_ids + segments * jnp.arange(row_count)[:, None])

    cot = cotangent.reshape(total, width)
    cot_cls = cotangent.reshape(own, SEGLEN, width)[:, 0]
    qkv, probs, n1, r1, slope, n2, r2, y, cls, xt, mixedt, firstt, hiddent = forward_block(
        tokens.reshape(total, width), w_qkv, w_out, w_up, w_down, biases[0], gains[0], b_up[0:1]
    )
    (ccls, gcls, csums, cbsums, gpos, cxt, cmixedt, cfirstt, chiddent, cgqkv, cgbranch, cginner, cgsecond) = cross_block(
        cls, cot_cls, place, keys, pos_table, w_qkv, w_out, w_up, w_down, biases[1], gains[1], b_up[1:2], planes
    )
    output, gsecond, ginner, gbranch, gqkv, gx, sums, bsums = backward_block(
        gcls, ccls, cot, y, n2, r2, slope, n1, r1, qkv, probs, w_qkv, w_out, w_up, w_down, gains[0]
    )
    small = small_grads(sums, bsums, csums, cbsums, gpos, 1.0 / planes)
    small = [lax.psum_scatter(part, axes, scatter_dimension=0, tiled=True) for part in small]

    def mine(values, dim):
        return lax.dynamic_slice_in_dim(values, me * own, own, dim)

    big = []
    for seg_a, seg_b, cross_a, cross_b in (
        (xt, gqkv, cxt, cgqkv), (mixedt, gbranch, cmixedt, cgbranch), (firstt, ginner, cfirstt, cginner), (hiddent, gsecond, chiddent, cgsecond)
    ):
        both = jnp.concatenate([mm(seg_a, seg_b), mm(mine(cross_a, 1), mine(cross_b, 0))], axis=0)
        big.append(lax.psum_scatter(both, axes, scatter_dimension=0, tiled=True))
    return (output.reshape(tokens.shape), gx.reshape(tokens.shape), *big, *small)


def solution(mesh):
    sizes = (mesh.shape["row"], mesh.shape["seg"])
    tokens_at = P("row", "seg", None)
    return jax.shard_map(
        functools.partial(per_device, sizes=sizes),
        mesh=mesh,
        in_specs=(tokens_at, P("row", None)) + (P(),) * 8 + (tokens_at,),
        out_specs=(tokens_at, tokens_at) + (P(("row", "seg"), None),) * 4 + (P(("row", "seg")),) * 4,
        check_vma=False,
    )
```

```python
import functools

import jax
import jax.numpy as jnp
from jax import lax
from jax.experimental import pallas as pl
from jax.experimental.pallas import tpu as pltpu
from jax.sharding import PartitionSpec as P


HDIM = 64
SEGLEN = 128
LANES = 128
EPSILON = 1e-05
GELU_A = 0.7978845608028654
GELU_B = 0.044715 * GELU_A
F32, BF16 = jnp.float32, jnp.bfloat16


def mm(a, b):
    return lax.dot_general(a, b, (((1,), (0,)), ((), ())), preferred_element_type=F32)


def mm_nt(a, b):
    return lax.dot_general(a, b, (((1,), (1,)), ((), ())), preferred_element_type=F32)


def mm_tn(a, b):
    return lax.dot_general(a, b, (((0,), (0,)), ((), ())), preferred_element_type=F32)


def low_lanes(shape):
    return lax.broadcasted_iota(jnp.int32, shape, 1) < HDIM


def stack_heads(pair):
    keep = low_lanes(pair.shape)
    zero = jnp.zeros_like(pair)
    return jnp.concatenate([jnp.where(keep, pair, zero), jnp.where(keep, zero, pair)], axis=0)


def norm_stats(values):
    centered = values - jnp.mean(values, axis=-1, keepdims=True)
    variance = jnp.mean(centered * centered, axis=-1, keepdims=True)
    rstd = lax.rsqrt(variance + EPSILON)
    return centered * rstd, rstd


def gelu_both(u):
    square = u * u
    t = jnp.tanh(u * (GELU_A + GELU_B * square))
    half = 0.5 * u
    hidden = half + half * t
    slope = 0.5 + 0.5 * t + half * (1.0 - t * t) * (GELU_A + (3.0 * GELU_B) * square)
    return hidden, slope


def forward_kernel(
    x_ref, wqkv_hbm, wout_hbm, wup_hbm, wdown_hbm, bias_ref, gain_ref, bup_ref,
    qkv_ref, probs_ref, n1_ref, r1_ref, slope_ref, n2_ref, r2_ref, y_ref, cls_ref, xt_ref, mixedt_ref, firstt_ref, hiddent_ref,
    wqkv, wout, wup, wdown, mixed_ref, sems, *, ff_chunk,
):
    step = pl.program_id(0)
    copies = [
        pltpu.make_async_copy(src.at[0], dst, sems.at[i])
        for i, (src, dst) in enumerate(
            ((wqkv_hbm, wqkv), (wout_hbm, wout), (wup_hbm, wup), (wdown_hbm, wdown))
        )
    ]

    @pl.when(step == 0)
    def _():
        for copy in copies:
            copy.start()
        copies[0].wait()

    rows, width = x_ref.shape
    bias = bias_ref[...].astype(F32)
    gain = gain_ref[...].astype(F32)
    x = x_ref[...]
    xt_ref[...] = x.T
    for part in range(3):
        cols = slice(part * width, (part + 1) * width)
        out = mm(x, wqkv[:, cols])
        if part == 0:
            out = out + bias[0:1]
        if part == 2:
            out = out + bias[1:2]
        qkv_ref[:, cols] = out.astype(BF16)
    for seg in range(rows // SEGLEN):
        at = slice(seg * SEGLEN, (seg + 1) * SEGLEN)
        for pair in range(width // LANES):
            q = qkv_ref[at, pair * LANES : (pair + 1) * LANES]
            k = qkv_ref[at, width + pair * LANES : width + (pair + 1) * LANES]
            v = qkv_ref[at, 2 * width + pair * LANES : 2 * width + (pair + 1) * LANES]
            scores = mm_nt(k, stack_heads(q * HDIM**-0.5))
            e = jnp.exp(scores - jnp.max(scores, axis=0, keepdims=True))
            p = (e * (1.0 / jnp.sum(e, axis=0, keepdims=True))).astype(BF16)
            probs_ref[seg, pair] = p
            pt = jnp.concatenate([p[:, :SEGLEN].T, p[:, SEGLEN:].T], axis=1)
            mixed_ref[at, pair * LANES : (pair + 1) * LANES] = mm(pt, stack_heads(v)).astype(BF16)

    @pl.when(step == 0)
    def _():
        for copy in copies[1:]:
            copy.wait()

    mixed = mixed_ref[...]
    mixedt_ref[...] = mixed.T
    resid = x.astype(F32) + mm(mixed, wout[...]) + bias[2:3]
    n1, r1 = norm_stats(resid)
    n1_ref[...] = n1.astype(BF16)
    r1_ref[...] = jnp.broadcast_to(r1, r1_ref.shape)
    first = (n1 * gain[0:1] + bias[3:4]).astype(BF16)
    firstt_ref[...] = first.T
    total = first.astype(F32) + bias[4:5]
    inners = wup.shape[1]
    for c in range(inners // ff_chunk):
        cols = slice(c * ff_chunk, (c + 1) * ff_chunk)
        inner = mm(first, wup[:, cols]) + bup_ref[:, cols].astype(F32)
        hidden, slope = gelu_both(inner)
        hidden = hidden.astype(BF16)
        hiddent_ref[cols, :] = hidden.T
        slope_ref[:, cols] = slope.astype(BF16)
        total = total + mm(hidden, wdown[cols, :])
    n2, r2 = norm_stats(total)
    n2_ref[...] = n2.astype(BF16)
    r2_ref[...] = jnp.broadcast_to(r2, r2_ref.shape)
    y = (n2 * gain[1:2] + bias[5:6]).astype(BF16)
    y_ref[...] = y
    for seg in range(rows // SEGLEN):
        cls_ref[pl.ds(step * (rows // SEGLEN) + seg, 1), :] = y[seg * SEGLEN : seg * SEGLEN + 8].astype(F32)[0:1]


def forward_block(x, w_qkv, w_out, w_up, w_down, bias, gain, bup, tile=256, ff_chunk=768):
    total, width = x.shape
    inners = w_up.shape[-1]
    segs = tile // SEGLEN
    pairs = width // LANES
    any_spec = pl.BlockSpec(memory_space=pl.ANY)

    def rows_of(cols):
        return pl.BlockSpec((tile, cols), lambda i: (i, 0))

    def whole(a):
        return pl.BlockSpec(a.shape, lambda i: (0,) * a.ndim)

    def cols_of(rows):
        return pl.BlockSpec((rows, tile), lambda i: (0, i))

    outs = [
        ((total, 3 * width), BF16, rows_of(3 * width)),
        ((total // SEGLEN, pairs, SEGLEN, 2 * SEGLEN), BF16, pl.BlockSpec((segs, pairs, SEGLEN, 2 * SEGLEN), lambda i: (i, 0, 0, 0))),
        ((total, width), BF16, rows_of(width)),
        ((total, LANES), F32, rows_of(LANES)),
        ((total, inners), BF16, rows_of(inners)),
        ((total, width), BF16, rows_of(width)),
        ((total, LANES), F32, rows_of(LANES)),
        ((total, width), BF16, rows_of(width)),
        ((total // SEGLEN, width), F32, pl.BlockSpec((total // SEGLEN, width), lambda i: (0, 0))),
        ((width, total), BF16, cols_of(width)),
        ((width, total), BF16, cols_of(width)),
        ((width, total), BF16, cols_of(width)),
        ((inners, total), BF16, cols_of(inners)),
    ]
    return pl.pallas_call(
        functools.partial(forward_kernel, ff_chunk=ff_chunk),
        grid=(total // tile,),
        in_specs=[rows_of(width), any_spec, any_spec, any_spec, any_spec, whole(bias), whole(gain), whole(bup)],
        out_specs=[o[2] for o in outs],
        out_shape=[jax.ShapeDtypeStruct(o[0], o[1]) for o in outs],
        scratch_shapes=[
            pltpu.VMEM(w_qkv.shape[1:], BF16),
            pltpu.VMEM(w_out.shape[1:], BF16),
            pltpu.VMEM(w_up.shape[1:], BF16),
            pltpu.VMEM(w_down.shape[1:], BF16),
            pltpu.VMEM((tile, width), BF16),
            pltpu.SemaphoreType.DMA((4,)),
        ],
        compiler_params=pltpu.CompilerParams(vmem_limit_bytes=60 * 2**20),
        name="segment_forward",
    )(x, w_qkv, w_out, w_up, w_down, bias, gain, bup)

def fold_rows(values):
    rows, cols = values.shape
    return jnp.sum(values.reshape(rows // 8, 8, cols), axis=0)


def norm_back(grad, gain, normal, rstd):
    scaled = grad * gain
    a = jnp.mean(scaled, axis=-1, keepdims=True)
    b = jnp.mean(scaled * normal, axis=-1, keepdims=True)
    return (scaled - a - normal * b) * rstd


def backward_kernel(
    gcls_ref, ccls_ref, cot_ref, y_ref, n2_ref, r2_ref, slope_ref, n1_ref, r1_ref, qkv_ref, probs_ref,
    wqkv_hbm, wout_hbm, wup_hbm, wdown_hbm, gain_ref,
    out_ref, gsecond_ref, ginner_ref, gbranch_ref, gqkv_ref, gx_ref, sums_ref, bsums_ref,
    wqkv, wout, wup, wdown, sems, *, ff_chunk,
):
    step = pl.program_id(0)
    copies = [
        pltpu.make_async_copy(src.at[0], dst, sems.at[i])
        for i, (src, dst) in enumerate(
            ((wdown_hbm, wdown), (wup_hbm, wup), (wout_hbm, wout), (wqkv_hbm, wqkv))
        )
    ]

    @pl.when(step == 0)
    def _():
        for copy in copies:
            copy.start()
        sums_ref[...] = jnp.zeros_like(sums_ref)
        bsums_ref[...] = jnp.zeros_like(bsums_ref)
        for copy in copies[:2]:
            copy.wait()

    rows, width = cot_ref.shape
    segs = rows // SEGLEN
    inners = wup.shape[1]
    gain = gain_ref[...].astype(F32)
    place = lax.broadcasted_iota(jnp.int32, (rows, width), 0)
    gy = cot_ref[...].astype(F32)
    y = y_ref[...].astype(F32)
    for seg in range(segs):
        at = pl.ds(step * segs + seg, 1)
        gy = jnp.where(place == seg * SEGLEN, gcls_ref[at, :], gy)
        y = jnp.where(place == seg * SEGLEN, ccls_ref[at, :], y)
    out_ref[...] = y.astype(BF16)
    n2 = n2_ref[...].astype(F32)
    sums_ref[0] += fold_rows(gy * n2)
    sums_ref[1] += fold_rows(gy)
    g_two = norm_back(gy, gain[1:2], n2, r2_ref[:, 0:1])
    g_second = g_two.astype(BF16)
    gsecond_ref[...] = g_second
    sums_ref[2] += fold_rows(g_second.astype(F32))
    g_first = g_two
    for c in range(inners // ff_chunk):
        cols = slice(c * ff_chunk, (c + 1) * ff_chunk)
        g_inner = mm_nt(g_second, wdown[cols, :]) * slope_ref[:, cols].astype(F32)
        g_low = g_inner.astype(BF16)
        ginner_ref[:, cols] = g_low
        bsums_ref[:, cols] += fold_rows(g_low.astype(F32))
        g_first = g_first + mm_nt(g_low, wup[:, cols])
    n1 = n1_ref[...].astype(F32)
    sums_ref[3] += fold_rows(g_first * n1)
    sums_ref[4] += fold_rows(g_first)
    g_one = norm_back(g_first, gain[0:1], n1, r1_ref[:, 0:1])
    g_branch = g_one.astype(BF16)
    gbranch_ref[...] = g_branch
    sums_ref[5] += fold_rows(g_branch.astype(F32))

    @pl.when(step == 0)
    def _():
        for copy in copies[2:]:
            copy.wait()

    g_mixed = mm_nt(g_branch, wout[...]).astype(BF16)
    for seg in range(segs):
        at = slice(seg * SEGLEN, (seg + 1) * SEGLEN)
        for pair in range(width // LANES):
            lanes = [slice(part * width + pair * LANES, part * width + (pair + 1) * LANES) for part in range(3)]
            q = qkv_ref[at, lanes[0]] * HDIM**-0.5
            k = qkv_ref[at, lanes[1]]
            v = qkv_ref[at, lanes[2]]
            p_low = probs_ref[seg, pair]
            p = p_low.astype(F32)
            g_out = stack_heads(g_mixed[at, lanes[0]])
            g_p = mm_nt(v, g_out)
            inner_sum = jnp.sum(g_p * p, axis=0, keepdims=True)
            g_s = (p * (g_p - inner_sum)).astype(BF16)
            g_v = mm(p_low, g_out)
            g_k = mm(g_s, stack_heads(q))
            g_st = jnp.concatenate([g_s[:, :SEGLEN].T, g_s[:, SEGLEN:].T], axis=1)
            g_q = mm(g_st, stack_heads(k)) * HDIM**-0.5
            gqkv_ref[at, lanes[0]] = g_q.astype(BF16)
            gqkv_ref[at, lanes[1]] = g_k.astype(BF16)
            gqkv_ref[at, lanes[2]] = g_v.astype(BF16)
    g_qkv = gqkv_ref[...]
    sums_ref[6] += fold_rows(g_qkv[:, :width].astype(F32))
    sums_ref[7] += fold_rows(g_qkv[:, 2 * width :].astype(F32))
    gx_ref[...] = g_one + mm_nt(g_qkv, wqkv[...])


def backward_block(gcls, ccls, cot, y, n2, r2, slope, n1, r1, qkv, probs, w_qkv, w_out, w_up, w_down, gain, tile=256, ff_chunk=768):
    total, width = cot.shape
    inners = w_up.shape[-1]
    segs = tile // SEGLEN
    pairs = width // LANES
    any_spec = pl.BlockSpec(memory_space=pl.ANY)

    def rows_of(cols):
        return pl.BlockSpec((tile, cols), lambda i: (i, 0))

    def whole(a):
        return pl.BlockSpec(a.shape, lambda i: (0,) * len(a.shape))

    outs = [
        ((total, width), BF16, rows_of(width)),
        ((total, width), BF16, rows_of(width)),
        ((total, inners), BF16, rows_of(inners)),
        ((total, width), BF16, rows_of(width)),
        ((total, 3 * width), BF16, rows_of(3 * width)),
        ((total, width), F32, rows_of(width)),
        ((8, 8, width), F32, pl.BlockSpec((8, 8, width), lambda i: (0, 0, 0))),
        ((8, inners), F32, pl.BlockSpec((8, inners), lambda i: (0, 0))),
    ]
    return pl.pallas_call(
        functools.partial(backward_kernel, ff_chunk=ff_chunk),
        grid=(total // tile,),
        in_specs=[whole(gcls), whole(ccls), rows_of(width), rows_of(width), rows_of(width), rows_of(LANES), rows_of(inners),
                  rows_of(width), rows_of(LANES), rows_of(3 * width),
                  pl.BlockSpec((segs, pairs, SEGLEN, 2 * SEGLEN), lambda i: (i, 0, 0, 0)),
                  any_spec, any_spec, any_spec, any_spec, whole(gain)],
        out_specs=[o[2] for o in outs],
        out_shape=[jax.ShapeDtypeStruct(o[0], o[1]) for o in outs],
        scratch_shapes=[
            pltpu.VMEM(w_qkv.shape[1:], BF16),
            pltpu.VMEM(w_out.shape[1:], BF16),
            pltpu.VMEM(w_up.shape[1:], BF16),
            pltpu.VMEM(w_down.shape[1:], BF16),
            pltpu.SemaphoreType.DMA((4,)),
        ],
        compiler_params=pltpu.CompilerParams(vmem_limit_bytes=60 * 2**20),
        name="segment_backward",
    )(gcls, ccls, cot, y, n2, r2, slope, n1, r1, qkv, probs, w_qkv, w_out, w_up, w_down, gain)

NEGATIVE = -1000000000.0
MESH = pl.DeviceIdType.MESH


def turned(values):
    return values.astype(F32).T.astype(BF16)


def cross_kernel(
    cls_ref, cot_ref, place_ref, keycol_ref, keyrow_ref, table_ref, wqkv_hbm, wout_hbm, wup_hbm, wdown_hbm, bias_ref, gain_ref, bup_ref,
    ccls_ref, gcls_ref, sums_ref, bsums_ref, gpos_ref, xt_ref, mixedt_ref, firstt_ref, hiddent_ref, gqkv_ref, gbranch_ref, ginner_ref, gsecond_ref,
    wqkv, wout, wup, wdown, packed, gathered, qkv_ref, probs_ref, mixed_ref, slope_ref, whole_ref, sems, send_sems, recv_sems, *, ff_chunk, devices,
):
    copies = [
        pltpu.make_async_copy(src.at[1], dst, sems.at[i])
        for i, (src, dst) in enumerate(
            ((wqkv_hbm, wqkv), (wout_hbm, wout), (wup_hbm, wup), (wdown_hbm, wdown))
        )
    ]
    for copy in copies:
        copy.start()
    own, width = cls_ref.shape
    rows = own * devices
    inners = wup.shape[1]
    me = lax.axis_index("seg")
    line = lax.axis_index("row")
    barrier = pltpu.get_barrier_semaphore()
    for hop in range(1, devices):
        pl.semaphore_signal(barrier, inc=1, device_id=(line, lax.rem(me + hop, devices)), device_id_type=MESH)
    packed[0:own, :] = cls_ref[...].astype(BF16)
    packed[own:, :] = cot_ref[...]
    pl.semaphore_wait(barrier, devices - 1)
    sends = []
    for hop in range(1, devices):
        send = pltpu.make_async_remote_copy(
            src_ref=packed, dst_ref=gathered.at[hop], send_sem=send_sems.at[hop], recv_sem=recv_sems.at[hop],
            device_id=(line, lax.rem(me + hop, devices)), device_id_type=MESH,
        )
        send.start()
        sends.append(send)
    bias = bias_ref[...].astype(F32)
    gain = gain_ref[...].astype(F32)
    onehot = (place_ref[...] == lax.broadcasted_iota(jnp.int32, (rows, table_ref.shape[0]), 1)).astype(F32)
    embed = mm(onehot.astype(BF16), table_ref[...])
    allowed = keycol_ref[...] == keyrow_ref[...]
    gathered[0] = packed[...]
    for send in sends:
        send.wait()
    for hop in range(devices):
        at = pl.ds(pl.multiple_of(lax.rem(me - hop + devices, devices) * own, own), own)
        block = gathered[hop].astype(F32)
        whole_ref[0, at, :] = block[:own]
        whole_ref[1, at, :] = block[own:]
    x = (whole_ref[0] + embed).astype(BF16)
    gy = whole_ref[1]
    xt_ref[...] = turned(x)
    copies[0].wait()
    for part in range(3):
        cols = slice(part * width, (part + 1) * width)
        out = mm(x, wqkv[:, cols])
        if part == 0:
            out = out + bias[0:1]
        if part == 2:
            out = out + bias[1:2]
        qkv_ref[:, cols] = out.astype(BF16)
    for pair in range(width // LANES):
        q, k, v = (qkv_ref[:, part * width + pair * LANES : part * width + (pair + 1) * LANES] for part in range(3))
        scores = jnp.where(allowed, mm_nt(k, stack_heads(q * HDIM**-0.5)), NEGATIVE)
        e = jnp.exp(scores - jnp.max(scores, axis=0, keepdims=True))
        p = e * (1.0 / jnp.sum(e, axis=0, keepdims=True))
        probs_ref[pair] = p
        pt = p.T.astype(BF16)
        low = low_lanes((rows, LANES))
        mixed = jnp.where(low, mm(pt[:rows], v), mm(pt[rows:], v))
        mixed_ref[:, pair * LANES : (pair + 1) * LANES] = mixed.astype(BF16)
    copies[1].wait()
    mixed = mixed_ref[...]
    mixedt_ref[...] = turned(mixed)
    n1, r1 = norm_stats(x.astype(F32) + mm(mixed, wout[...]) + bias[2:3])
    first = (n1 * gain[0:1] + bias[3:4]).astype(BF16)
    firstt_ref[...] = turned(first)
    copies[2].wait()
    copies[3].wait()
    total = first.astype(F32) + bias[4:5]
    for c in range(inners // ff_chunk):
        cols = slice(c * ff_chunk, (c + 1) * ff_chunk)
        hidden, slope = gelu_both(mm(first, wup[:, cols]) + bup_ref[:, cols].astype(F32))
        hidden = hidden.astype(BF16)
        hiddent_ref[cols, :] = turned(hidden)
        slope_ref[:, cols] = slope
        total = total + mm(hidden, wdown[cols, :])
    n2, r2 = norm_stats(total)
    mine = pl.ds(pl.multiple_of(me * own, own), own)
    whole_ref[0] = (n2 * gain[1:2] + bias[5:6]).astype(BF16).astype(F32)
    ccls_ref[...] = whole_ref[0, mine, :]

    def row_sum(values):
        return jnp.sum(values.astype(F32), axis=0, keepdims=True)

    sums_ref[0:1, :] = row_sum(gy * n2)
    sums_ref[1:2, :] = row_sum(gy)
    g_two = norm_back(gy, gain[1:2], n2, r2)
    g_second = g_two.astype(BF16)
    gsecond_ref[...] = g_second
    sums_ref[2:3, :] = row_sum(g_second)
    g_first = g_two
    for c in range(inners // ff_chunk):
        cols = slice(c * ff_chunk, (c + 1) * ff_chunk)
        g_inner = (mm_nt(g_second, wdown[cols, :]) * slope_ref[:, cols]).astype(BF16)
        ginner_ref[:, cols] = g_inner
        bsums_ref[:, cols] = row_sum(g_inner)
        g_first = g_first + mm_nt(g_inner, wup[:, cols])
    sums_ref[3:4, :] = row_sum(g_first * n1)
    sums_ref[4:5, :] = row_sum(g_first)
    g_one = norm_back(g_first, gain[0:1], n1, r1)
    g_branch = g_one.astype(BF16)
    gbranch_ref[...] = g_branch
    sums_ref[5:6, :] = row_sum(g_branch)
    g_mixed = mm_nt(g_branch, wout[...]).astype(BF16)
    for pair in range(width // LANES):
        lanes = [slice(part * width + pair * LANES, part * width + (pair + 1) * LANES) for part in range(3)]
        q, k, v = (qkv_ref[:, at] for at in lanes)
        p = probs_ref[pair]
        g_out = stack_heads(g_mixed[:, lanes[0]])
        g_p = mm_nt(v, g_out)
        g_s = p * (g_p - jnp.sum(g_p * p, axis=0, keepdims=True))
        g_st = g_s.T.astype(BF16)
        g_s = g_s.astype(BF16)
        low = low_lanes((rows, LANES))
        g_q = jnp.where(low, mm(g_st[:rows], k), mm(g_st[rows:], k)) * HDIM**-0.5
        gqkv_ref[:, lanes[0]] = g_q.astype(BF16)
        gqkv_ref[:, lanes[1]] = mm(g_s, stack_heads(q * HDIM**-0.5)).astype(BF16)
        gqkv_ref[:, lanes[2]] = mm(p.astype(BF16), g_out).astype(BF16)
    g_qkv = gqkv_ref[...]
    sums_ref[6:7, :] = row_sum(g_qkv[:, :width])
    sums_ref[7:8, :] = row_sum(g_qkv[:, 2 * width :])
    g_x = g_one + mm_nt(g_qkv, wqkv[...])
    whole_ref[1] = g_x
    gcls_ref[...] = whole_ref[1, mine, :]
    gpos_ref[...] = lax.dot_general(onehot, g_x, (((0,), (0,)), ((), ())), preferred_element_type=F32, precision=lax.Precision.HIGHEST)


def cross_block(cls, cot, place, keys, table, w_qkv, w_out, w_up, w_down, bias, gain, bup, devices, ff_chunk=768):
    own, width = cls.shape
    rows = own * devices
    inners = w_up.shape[-1]
    vmem = pl.BlockSpec(memory_space=pltpu.VMEM)
    any_spec = pl.BlockSpec(memory_space=pl.ANY)
    outs = [
        ((own, width), F32), ((own, width), F32), ((8, width), F32), ((1, inners), F32), (table.shape, F32),
        ((width, rows), BF16), ((width, rows), BF16), ((width, rows), BF16), ((inners, rows), BF16),
        ((rows, 3 * width), BF16), ((rows, width), BF16), ((rows, inners), BF16), ((rows, width), BF16),
    ]
    return pl.pallas_call(
        functools.partial(cross_kernel, ff_chunk=ff_chunk, devices=devices),
        in_specs=[vmem] * 6 + [any_spec] * 4 + [vmem] * 3,
        out_specs=[vmem] * len(outs),
        out_shape=[jax.ShapeDtypeStruct(*o) for o in outs],
        scratch_shapes=[
            pltpu.VMEM(w_qkv.shape[1:], BF16),
            pltpu.VMEM(w_out.shape[1:], BF16),
            pltpu.VMEM(w_up.shape[1:], BF16),
            pltpu.VMEM(w_down.shape[1:], BF16),
            pltpu.VMEM((2 * own, width), BF16),
            pltpu.VMEM((devices, 2 * own, width), BF16),
            pltpu.VMEM((rows, 3 * width), BF16),
            pltpu.VMEM((width // LANES, rows, 2 * rows), F32),
            pltpu.VMEM((rows, width), BF16),
            pltpu.VMEM((rows, inners), F32),
            pltpu.VMEM((2, rows, width), F32),
            pltpu.SemaphoreType.DMA((4,)),
            pltpu.SemaphoreType.DMA((devices,)),
            pltpu.SemaphoreType.DMA((devices,)),
        ],
        compiler_params=pltpu.CompilerParams(vmem_limit_bytes=50 * 2**20, collective_id=0, has_side_effects=True),
        name="cross_block",
    )(cls, cot, place, keys, jnp.tile(keys.reshape(1, rows), (1, 2)), table, w_qkv, w_out, w_up, w_down, bias, gain, bup)

RING = 4
CROSS_UNITS = 3
SEG_UNITS = 12
UNITS = CROSS_UNITS + SEG_UNITS
PAIRS = (UNITS + 1) // 2
AHEAD = 4
PART = 48


def add_low(a, b):
    return (a.astype(F32) + b.astype(F32)).astype(BF16)


def total_kernel(
    firstt, ginner, hiddent, gsecond, mixedt, gbranch, xt, gqkv,
    cfirstt, cginner, chiddent, cgsecond, cmixedt, cgbranch, cxt, cgqkv,
    sums, bsums, csums, cbsums, gpos,
    dqkv_ref, dout_ref, dup_ref, ddown_ref, small_ref,
    aslot, bslot, csend, crecv, keep, r1, r2, r3, rf, acc, racc,
    load_sems, csend_sems, crecv_sems, s1_sems, q1_sems, s2_sems, q2_sems, s3_sems, q3_sems, sf_sems, qf_sems, sa_sems, qa_sems,
    *, share,
):
    width = bslot.shape[-1]
    line, z = lax.axis_index("row"), lax.axis_index("seg")
    y, x, c = line // 4, (line // 2) % 2, line % 2
    zh, zl = z // 2, z % 2
    flip_c = (y * 4 + x * 2 + 1 - c, z)
    flip_x = (y * 4 + (1 - x) * 2 + c, z)
    flip_y = ((1 - y) * 4 + x * 2 + c, z)
    flip_zl = (line, zh * 2 + 1 - zl)
    flip_zh = (line, (1 - zh) * 2 + zl)
    flip_yzh = ((1 - y) * 4 + x * 2 + c, (1 - zh) * 2 + zl)
    barrier = pltpu.get_barrier_semaphore()
    for peer in (flip_c, flip_x, flip_y, flip_zl, flip_zh, flip_yzh):
        pl.semaphore_signal(barrier, inc=1, device_id=peer, device_id_type=MESH)

    def load(u, do):
        slot = u % 2
        a_sem, b_sem = load_sems.at[slot, 0], load_sems.at[slot, 1]

        def pair(a, b):
            for copy in (pltpu.make_async_copy(a, aslot.at[slot], a_sem), pltpu.make_async_copy(b, bslot.at[slot], b_sem)):
                getattr(copy, do)()

        def columns(ref, j):
            return ref.at[:, pl.ds(pl.multiple_of(j * width, width), width)]

        @pl.when(u < 4)
        def _():
            pair(firstt, columns(ginner, u))

        @pl.when((u >= 4) & (u < 8))
        def _():
            pair(hiddent.at[:, :, :, u - 4], gsecond)

        @pl.when(u == 8)
        def _():
            pair(mixedt, gbranch)

        @pl.when(u >= 9)
        def _():
            pair(xt, columns(gqkv, u - 9))

    load(0, "start")

    def remote(src, dst, send_sem, recv_sem, peer):
        return pltpu.make_async_remote_copy(
            src_ref=src, dst_ref=dst, send_sem=send_sem, recv_sem=recv_sem, device_id=peer, device_id_type=MESH
        )

    def choose(t, a, b):
        return t * a + (1 - t) * b

    def pick(t, a, b):
        return tuple(choose(t, p, q) for p, q in zip(a, b))

    def way(t):
        bits = (choose(t, x, y), choose(t, zl, x), choose(t, zh, zl))
        peers = (pick(t, flip_x, flip_y), pick(t, flip_zl, flip_x), pick(t, flip_zh, flip_zl))
        return bits, peers

    def core_copy(n):
        slot = n % RING
        return remote(csend.at[slot], crecv.at[slot], csend_sems.at[slot], crecv_sems.at[slot], flip_c)

    def copy_one(n, t):
        (b1, _, _), (peer, _, _) = way(t)
        return remote(keep.at[n, pl.ds(4 * (1 - b1), 4)], r1.at[n], s1_sems.at[n], q1_sems.at[n], peer)

    def copy_two(n, t):
        (b1, b2, _), (_, peer, _) = way(t)
        return remote(keep.at[n, pl.ds(4 * b1 + 2 * (1 - b2), 2)], r2.at[n], s2_sems.at[n], q2_sems.at[n], peer)

    def copy_three(n, t):
        (b1, b2, b3), (_, _, peer) = way(t)
        return remote(keep.at[n, 4 * b1 + 2 * b2 + 1 - b3], r3.at[n], s3_sems.at[n], q3_sems.at[n], peer)

    def own_block(n, t):
        (b1, b2, b3), _ = way(t)
        return keep.at[n, 4 * b1 + 2 * b2 + b3]

    def step_one(n, t):
        core_copy(n).wait_recv()
        keep[n] = add_low(keep[n], crecv[n % RING])

        @pl.when(jnp.asarray(n) < AHEAD)
        def _():
            copy_one(n, t).start()

    def step_two(n, t):
        (b1, _, _), _ = way(t)
        copy_one(n, t).wait()
        at = pl.ds(4 * b1, 4)
        keep[n, at] = add_low(keep[n, at], r1[n])
        copy_two(n, t).start()

    def step_three(n, t):
        (b1, b2, _), _ = way(t)
        copy_two(n, t).wait()
        at = pl.ds(4 * b1 + 2 * b2, 2)
        keep[n, at] = add_low(keep[n, at], r2[n])
        copy_three(n, t).start()

    def final_to(n, t, slot, peer):
        return remote(own_block(n, t), rf.at[n, slot], sf_sems.at[n], qf_sems.at[n, slot], peer)

    def sends_final(n, t, act):
        straight = (y == 1) & ((t == 1) | (zh == 1))

        @pl.when(straight)
        def _():
            act(final_to(n, t, 0, flip_y))

        @pl.when((t == 0) & (y == 0) & (zh == 1))
        def _():
            act(final_to(n, t, 0, flip_zh))

        @pl.when((t == 0) & (y == 1) & (zh == 0))
        def _():
            act(final_to(n, t, 1, flip_yzh))

    def step_final(n, t):
        copy_three(n, t).wait()
        (b1, b2, b3), _ = way(t)
        at = 4 * b1 + 2 * b2 + b3
        keep[n, at] = add_low(keep[n, at], r3[n])
        sends_final(n, t, lambda copy: copy.start())

    def put(u, value):
        def columns(j):
            return pl.ds(pl.multiple_of(j * width, width), width)

        @pl.when(u < 4)
        def _():
            dup_ref[:, columns(u)] = value

        @pl.when((u >= 4) & (u < 8))
        def _():
            ddown_ref[pl.ds(pl.multiple_of((u - 4) * PART, PART), PART), :] = value

        @pl.when(u == 8)
        def _():
            dout_ref[...] = value

        @pl.when(u >= 9)
        def _():
            dqkv_ref[:, columns(u - 9)] = value

    def step_out(n, t, u):
        sends_final(n, t, lambda copy: copy.wait_send())

        @pl.when(y == 0)
        def _():
            final_to(n, t, 0, flip_y).wait_recv()

            @pl.when((t == 1) | (zh == 0))
            def _():
                put(u, own_block(n, t)[...].astype(F32) + rf[n, 0].astype(F32))

            @pl.when((t == 0) & (zh == 1))
            def _():
                final_to(n, t, 1, flip_y).wait_recv()
                put(u, rf[n, 0].astype(F32) + rf[n, 1].astype(F32))

    def cross_final(n):
        return remote(keep.at[n, pl.ds(2 * x, 2)], rf.at[n], sf_sems.at[n], qf_sems.at[n, 0], flip_y)

    def cross_step_final(n):
        copy_two(n, 0).wait()
        at = pl.ds(4 * y + 2 * x, 2)
        keep[n, at] = add_low(keep[n, at], r2[n])

        @pl.when(y == 0)
        def _():
            cross_final(n).start()

    def cross_step_out(n, index):
        @pl.when(y == 0)
        def _():
            cross_final(n).wait_send()

        @pl.when(y == 1)
        def _():
            cross_final(n).wait_recv()
            for sub in range(4):
                block = rf[n, sub] if sub < 2 else keep[n, 4 + 2 * x + sub - 2]
                put(4 * index + sub, block.astype(F32))

    small_peers = (flip_c, flip_x, flip_y, flip_zl, flip_zh)

    def small_copy(d):
        return remote(acc.at[d], racc.at[d], sa_sems.at[d], qa_sems.at[d], small_peers[d])

    def small_step(d):
        small_copy(d).wait()
        acc[d + 1] = acc[d] + racc[d]
        if d + 1 < len(small_peers):
            small_copy(d + 1).start()
        else:
            small_ref[...] = acc[d + 1]

    seg_rows = [jnp.sum(sums[i], axis=0, keepdims=True) for i in range(8)]
    seg_up = jnp.sum(bsums[...], axis=0, keepdims=True)
    order = (6, 7, 5, 4, 2, 1)
    for i, row in enumerate(order):
        acc[0, i : i + 1, :] = seg_rows[row]
        acc[0, 6 + i : 7 + i, :] = csums[row : row + 1, :] * share
    for i, row in enumerate((3, 0)):
        acc[0, 12 + i : 13 + i, :] = seg_rows[row]
        acc[0, 14 + i : 15 + i, :] = csums[row : row + 1, :] * share
    for i in range(4):
        acc[0, 16 + i : 17 + i, :] = seg_up[:, i * width : (i + 1) * width]
        acc[0, 20 + i : 21 + i, :] = cbsums[:, i * width : (i + 1) * width] * share
    acc[0, 24:32, :] = gpos[...] * share

    def cross_unit(n, parts):
        if n >= RING:
            core_copy(n).wait_send()
        for rel in (1, 0):
            core = c if rel == 0 else 1 - c
            for sub, (left, right) in enumerate(parts):
                for far in range(2):
                    value = mm(left(far, core), right).astype(BF16)
                    at = (sub // 2) * 4 + far * 2 + sub % 2
                    if rel == 1:
                        csend[n % RING, at] = value
                    else:
                        keep[n, at] = value
            if rel == 1:
                if n == 0:
                    pl.semaphore_wait(barrier, 6)
                    small_copy(0).start()
                core_copy(n).start()

    def plain(ref):
        return lambda far, core: ref[far, core, z]

    def nested(ref, j):
        return lambda far, core: ref[far, core, z, j]

    def cut(ref, j):
        return ref[:, j * width : (j + 1) * width]

    cross_parts = (
        lambda: [(plain(cfirstt), cut(cginner, j)) for j in range(4)],
        lambda: [(nested(chiddent, j), cgsecond[...]) for j in range(4)],
        lambda: [(plain(cmixedt), cgbranch[...])] + [(plain(cxt), cut(cgqkv, j)) for j in range(3)],
    )

    def compute(u):
        n = u + CROSS_UNITS - jnp.maximum(CROSS_UNITS - 1 - u, 0)
        t = n % 2
        for i in range(CROSS_UNITS):
            @pl.when(u == i)
            def _(i=i):
                cross_unit(2 * i, cross_parts[i]())
                if i > 0:
                    step_one(2 * i - 1, 1)

        load(u, "wait")

        @pl.when(u + 1 < SEG_UNITS)
        def _():
            load(u + 1, "start")

        @pl.when(n >= RING)
        def _():
            core_copy(n).wait_send()

        right = bslot[u % 2]
        for rel in (1, 0):
            core = c if rel == 0 else 1 - c
            left = aslot[u % 2, :, core].reshape(8 * PART, -1)
            value = mm(left, right).astype(BF16)
            for far in range(2):
                for part in range(4):
                    block = value[(far * 4 + part) * PART : (far * 4 + part + 1) * PART]
                    at = choose(t, far * 4 + (part % 2) * 2 + part // 2, (part // 2) * 4 + far * 2 + part % 2)
                    if rel == 1:
                        csend[n % RING, at] = block
                    else:
                        keep[n, at] = block
            if rel == 1:
                core_copy(n).start()
        step_one(n - 1, (n - 1) % 2)

    def step(u, carry):
        @pl.when(u < SEG_UNITS)
        def _():
            compute(u)

        @pl.when(u == SEG_UNITS)
        def _():
            step_one(UNITS - 1, (UNITS - 1) % 2)

        for d in range(len(small_peers)):
            @pl.when(u == 2 * d + 1)
            def _(d=d):
                small_step(d)

        def on_pair(p, even, odd, cross):
            @pl.when((p >= 0) & (p < CROSS_UNITS))
            def _():
                cross(2 * p)

            @pl.when((p >= CROSS_UNITS) & (p < PAIRS))
            def _():
                even(2 * p)

            @pl.when((p >= 0) & (p < PAIRS - 1))
            def _():
                odd(2 * p + 1)

        @pl.when(u % 2 == 1)
        def _():
            p = u // 2 - 1
            on_pair(
                p - 3,
                lambda n: step_out(n, 0, 2 * (p - 3) - CROSS_UNITS),
                lambda n: step_out(n, 1, p - 3 + jnp.maximum(p - 3 - CROSS_UNITS + 1, 0)),
                lambda n: None,
            )
            on_pair(p - 2, lambda n: step_final(n, 0), lambda n: step_final(n, 1), lambda n: cross_step_out(n, p - 2))
            on_pair(p - 1, lambda n: step_three(n, 0), lambda n: step_three(n, 1), lambda n: cross_step_final(n))
            on_pair(p, lambda n: step_two(n, 0), lambda n: step_two(n, 1), lambda n: step_two(n, 0))
            q = p + AHEAD // 2

            @pl.when((q >= AHEAD // 2) & (q < PAIRS))
            def _():
                copy_one(2 * q, 0).start()

            @pl.when((q >= AHEAD // 2) & (q < PAIRS - 1))
            def _():
                copy_one(2 * q + 1, 1).start()

        return carry

    lax.fori_loop(0, 2 * PAIRS + 8, step, 0)
    for n in range(UNITS - RING, UNITS):
        core_copy(n).wait_send()


def total_grads(big, cross, small, share):
    firstt, ginner, hiddent, gsecond, mixedt, gbranch, xt, gqkv = big
    cfirstt, cginner, chiddent, cgsecond, cmixedt, cgbranch, cxt, cgqkv = cross
    width, depth = firstt.shape
    inners = ginner.shape[1]
    rows = cfirstt.shape[1]
    assert width == 16 * PART and inners == 4 * width

    def blocks(a, n):
        return a.reshape((2, 2, 4) + ((n,) if n > 1 else ()) + (PART, a.shape[1]))

    operands = [
        blocks(firstt, 1), ginner, blocks(hiddent, 4), gsecond, blocks(mixedt, 1), gbranch, blocks(xt, 1), gqkv,
        blocks(cfirstt, 1), cginner, blocks(chiddent, 4), cgsecond, blocks(cmixedt, 1), cgbranch, blocks(cxt, 1), cgqkv, *small,
    ]
    vmem = pl.BlockSpec(memory_space=pltpu.VMEM)
    any_spec = pl.BlockSpec(memory_space=pl.ANY)
    outs = [(PART, 3 * width), (PART, width), (PART, inners), (4 * PART, width), (32, width)]
    dma = pltpu.SemaphoreType.DMA
    return pl.pallas_call(
        functools.partial(total_kernel, share=share),
        in_specs=[any_spec] * 8 + [vmem] * (len(operands) - 8),
        out_specs=[vmem] * len(outs),
        out_shape=[jax.ShapeDtypeStruct(o, F32) for o in outs],
        scratch_shapes=[
            pltpu.VMEM((2, 2, 2, 4, PART, depth), BF16),
            pltpu.VMEM((2, depth, width), BF16),
            pltpu.VMEM((RING, 8, PART, width), BF16),
            pltpu.VMEM((RING, 8, PART, width), BF16),
            pltpu.VMEM((UNITS, 8, PART, width), BF16),
            pltpu.VMEM((UNITS, 4, PART, width), BF16),
            pltpu.VMEM((UNITS, 2, PART, width), BF16),
            pltpu.VMEM((UNITS, PART, width), BF16),
            pltpu.VMEM((UNITS, 2, PART, width), BF16),
            pltpu.VMEM((6, 32, width), F32),
            pltpu.VMEM((5, 32, width), F32),
            dma((2, 2)), dma((RING,)), dma((RING,)), dma((UNITS,)), dma((UNITS,)), dma((UNITS,)), dma((UNITS,)),
            dma((UNITS,)), dma((UNITS,)), dma((UNITS,)), dma((UNITS, 2)), dma((5,)), dma((5,)),
        ],
        compiler_params=pltpu.CompilerParams(vmem_limit_bytes=60 * 2**20, collective_id=1, has_side_effects=True),
        name="total_grads",
    )(*operands)

def small_grads(sums, bsums, csums, cbsums, gpos, cross_share):
    seg_rows = jnp.sum(sums, axis=1)
    cross_rows = csums * cross_share
    seg_up = jnp.sum(bsums, axis=0)
    order = jnp.array([6, 7, 5, 4, 2, 1])
    biases = jnp.stack([seg_rows[order], cross_rows[order]])
    gains = jnp.stack([seg_rows[jnp.array([3, 0])], cross_rows[jnp.array([3, 0])]])
    ups = jnp.stack([seg_up, cbsums[0] * cross_share])
    return biases.reshape(-1), gains.reshape(-1), ups.reshape(-1), (gpos * cross_share).reshape(-1)


def per_device(
    tokens, doc_ids, w_qkv, w_out, w_up, w_down, biases, gains, b_up, pos_table, cotangent, *, sizes
):
    lines, planes = sizes
    row_count, local_length, width = tokens.shape
    seg_here = local_length // SEGLEN
    segments = doc_ids.shape[1]
    total = row_count * local_length
    own = row_count * seg_here
    me = lax.axis_index("seg")

    seg_place = jnp.arange(segments)
    same_doc = doc_ids[:, :, None] == doc_ids[:, None, :]
    doc_start = jnp.min(jnp.where(same_doc, seg_place[None, None, :], segments), axis=2)

    def by_device(values):
        return values.reshape(row_count, planes, seg_here).transpose(1, 0, 2).reshape(-1, 1)

    place = by_device(seg_place[None, :] - doc_start)
    keys = by_device(doc_ids + segments * jnp.arange(row_count)[:, None])

    cot = cotangent.reshape(total, width)
    cot_cls = cotangent.reshape(own, SEGLEN, width)[:, 0]
    qkv, probs, n1, r1, slope, n2, r2, y, cls, xt, mixedt, firstt, hiddent = forward_block(
        tokens.reshape(total, width), w_qkv, w_out, w_up, w_down, biases[0], gains[0], b_up[0:1]
    )
    (ccls, gcls, csums, cbsums, gpos, cxt, cmixedt, cfirstt, chiddent, cgqkv, cgbranch, cginner, cgsecond) = cross_block(
        cls, cot_cls, place, keys, pos_table, w_qkv, w_out, w_up, w_down, biases[1], gains[1], b_up[1:2], planes
    )
    output, gsecond, ginner, gbranch, gqkv, gx, sums, bsums = backward_block(
        gcls, ccls, cot, y, n2, r2, slope, n1, r1, qkv, probs, w_qkv, w_out, w_up, w_down, gains[0]
    )
    seg_pairs = (firstt, ginner, hiddent, gsecond, mixedt, gbranch, xt, gqkv)
    cross_pairs = (cfirstt, cginner, chiddent, cgsecond, cmixedt, cgbranch, cxt, cgqkv)
    if (lines, planes) == (8, 4) and width == 16 * PART:
        *big, small = total_grads(seg_pairs, cross_pairs, (sums, bsums, csums, cbsums, gpos), 1.0 / planes)
        small = small.reshape(-1)
        index = lax.axis_index("row") * planes + me
        shards, start = [], 0
        for size in (12 * width, 4 * width, 8 * width, segments * width):
            count = size // (lines * planes)
            shards.append(lax.dynamic_slice_in_dim(small, start + index * count, count, 0))
            start += size
    else:
        big, shards = generic_total(seg_pairs, cross_pairs, (sums, bsums, csums, cbsums, gpos), planes, own)
    return (output.reshape(tokens.shape), gx.reshape(tokens.shape), *big, *shards)


def generic_total(seg_pairs, cross_pairs, small, planes, own):
    axes = ("row", "seg")
    me = lax.axis_index("seg")
    shards = [
        lax.psum_scatter(part, axes, scatter_dimension=0, tiled=True) for part in small_grads(*small, 1.0 / planes)
    ]

    def mine(values, dim):
        return lax.dynamic_slice_in_dim(values, me * own, own, dim)

    big = []
    for at in (6, 4, 0, 2):
        cross = mm(mine(cross_pairs[at], 1), mine(cross_pairs[at + 1], 0))
        both = jnp.concatenate([mm(seg_pairs[at], seg_pairs[at + 1]), cross], axis=0)
        big.append(lax.psum_scatter(both, axes, scatter_dimension=0, tiled=True))
    return big, shards


def solution(mesh):
    sizes = (mesh.shape["row"], mesh.shape["seg"])
    tokens_at = P("row", "seg", None)
    return jax.shard_map(
        functools.partial(per_device, sizes=sizes),
        mesh=mesh,
        in_specs=(tokens_at, P("row", None)) + (P(),) * 8 + (tokens_at,),
        out_specs=(tokens_at, tokens_at) + (P(("row", "seg"), None),) * 4 + (P(("row", "seg")),) * 4,
        check_vma=False,
    )
```

```python
import functools

import jax
import jax.numpy as jnp
from jax import lax
from jax.experimental import pallas as pl
from jax.experimental.pallas import tpu as pltpu
from jax.sharding import PartitionSpec as P


HDIM = 64
SEGLEN = 128
LANES = 128
GROUP = 2 * LANES
EPSILON = 1e-05
GELU_A = 0.7978845608028654
GELU_B = 0.044715 * GELU_A
F32, BF16 = jnp.float32, jnp.bfloat16


def mm(a, b):
    return lax.dot_general(a, b, (((1,), (0,)), ((), ())), preferred_element_type=F32)


def mm_nt(a, b):
    return lax.dot_general(a, b, (((1,), (1,)), ((), ())), preferred_element_type=F32)


def mm_tn(a, b):
    return lax.dot_general(a, b, (((0,), (0,)), ((), ())), preferred_element_type=F32)


def low_lanes(shape):
    return lax.broadcasted_iota(jnp.int32, shape, 1) < HDIM


def stack_heads(pair):
    keep = low_lanes(pair.shape)
    zero = jnp.zeros_like(pair)
    return jnp.concatenate([jnp.where(keep, pair, zero), jnp.where(keep, zero, pair)], axis=0)


def pair_lanes(half):
    return [slice(part * GROUP + half * LANES, part * GROUP + (half + 1) * LANES) for part in range(3)]


def norm_stats(values):
    centered = values - jnp.mean(values, axis=-1, keepdims=True)
    variance = jnp.mean(centered * centered, axis=-1, keepdims=True)
    rstd = lax.rsqrt(variance + EPSILON)
    return centered * rstd, rstd


def gelu_both(u):
    square = u * u
    t = jnp.tanh(u * (GELU_A + GELU_B * square))
    half = 0.5 * u
    hidden = half + half * t
    slope = 0.5 + 0.5 * t + half * (1.0 - t * t) * (GELU_A + (3.0 * GELU_B) * square)
    return hidden, slope


def forward_kernel(
    x_ref, wqkv_hbm, wout_hbm, wup_hbm, wdown_hbm, bias_ref, gain_ref, bup_ref,
    qkv_ref, probs_ref, n1_ref, r1_ref, slope_ref, n2_ref, r2_ref, y_ref, cls_ref, xt_ref, mixedt_ref, firstt_ref, hiddent_ref,
    wqkv, wout, wup, wdown, mixed_ref, sems, *, ff_chunk,
):
    step = pl.program_id(0)
    copies = [
        pltpu.make_async_copy(src.at[0], dst, sems.at[i])
        for i, (src, dst) in enumerate(
            ((wqkv_hbm, wqkv), (wout_hbm, wout), (wup_hbm, wup), (wdown_hbm, wdown))
        )
    ]

    @pl.when(step == 0)
    def _():
        for copy in copies:
            copy.start()
        copies[0].wait()

    rows, width = x_ref.shape
    bias = bias_ref[0].astype(F32)
    gain = gain_ref[0].astype(F32)
    up_bias = bup_ref[0:1, :].astype(F32)
    x = x_ref[...]
    xt_ref[...] = x.T
    for part in range(3):
        cols = slice(part * width, (part + 1) * width)
        out = mm(x, wqkv[:, cols])
        if part == 0:
            out = out + bias[0:1]
        if part == 2:
            out = out + bias[1:2]
        out = out.astype(BF16)
        for group in range(width // GROUP):
            qkv_ref[group, :, part * GROUP : (part + 1) * GROUP] = out[:, group * GROUP : (group + 1) * GROUP]
    for seg in range(rows // SEGLEN):
        at = slice(seg * SEGLEN, (seg + 1) * SEGLEN)
        for pair in range(width // LANES):
            q, k, v = (qkv_ref[pair // 2, at, lanes] for lanes in pair_lanes(pair % 2))
            scores = mm_nt(k, stack_heads(q * HDIM**-0.5))
            e = jnp.exp(scores - jnp.max(scores, axis=0, keepdims=True))
            p = (e * (1.0 / jnp.sum(e, axis=0, keepdims=True))).astype(BF16)
            probs_ref[seg, pair] = p
            pt = jnp.concatenate([p[:, :SEGLEN].T, p[:, SEGLEN:].T], axis=1)
            mixed_ref[at, pair * LANES : (pair + 1) * LANES] = mm(pt, stack_heads(v)).astype(BF16)

    @pl.when(step == 0)
    def _():
        for copy in copies[1:]:
            copy.wait()

    mixed = mixed_ref[...]
    mixedt_ref[...] = mixed.T
    resid = x.astype(F32) + mm(mixed, wout[...]) + bias[2:3]
    n1, r1 = norm_stats(resid)
    n1_ref[...] = n1.astype(BF16)
    r1_ref[...] = jnp.broadcast_to(r1, r1_ref.shape)
    first = (n1 * gain[0:1] + bias[3:4]).astype(BF16)
    firstt_ref[...] = first.T
    total = first.astype(F32) + bias[4:5]
    inners = wup.shape[1]
    for c in range(inners // ff_chunk):
        cols = slice(c * ff_chunk, (c + 1) * ff_chunk)
        inner = mm(first, wup[:, cols]) + up_bias[:, cols]
        hidden, slope = gelu_both(inner)
        hidden = hidden.astype(BF16)
        hiddent_ref[cols, :] = hidden.T
        slope_ref[:, cols] = slope.astype(BF16)
        total = total + mm(hidden, wdown[cols, :])
    n2, r2 = norm_stats(total)
    n2_ref[...] = n2.astype(BF16)
    r2_ref[...] = jnp.broadcast_to(r2, r2_ref.shape)
    y = (n2 * gain[1:2] + bias[5:6]).astype(BF16)
    y_ref[...] = y
    for seg in range(rows // SEGLEN):
        cls_ref[pl.ds(step * (rows // SEGLEN) + seg, 1), :] = y[seg * SEGLEN : seg * SEGLEN + 8].astype(F32)[0:1]


def forward_block(x, w_qkv, w_out, w_up, w_down, bias, gain, bup, tile=256, ff_chunk=768):
    total, width = x.shape
    inners = w_up.shape[-1]
    segs = tile // SEGLEN
    pairs = width // LANES
    any_spec = pl.BlockSpec(memory_space=pl.ANY)

    def rows_of(cols):
        return pl.BlockSpec((tile, cols), lambda i: (i, 0))

    def whole(a):
        return pl.BlockSpec(a.shape, lambda i: (0,) * a.ndim)

    def cols_of(rows):
        return pl.BlockSpec((rows, tile), lambda i: (0, i))

    outs = [
        ((width // GROUP, total, 3 * GROUP), BF16, pl.BlockSpec((width // GROUP, tile, 3 * GROUP), lambda i: (0, i, 0))),
        ((total // SEGLEN, pairs, SEGLEN, 2 * SEGLEN), BF16, pl.BlockSpec((segs, pairs, SEGLEN, 2 * SEGLEN), lambda i: (i, 0, 0, 0))),
        ((total, width), BF16, rows_of(width)),
        ((total, LANES), F32, rows_of(LANES)),
        ((total, inners), BF16, rows_of(inners)),
        ((total, width), BF16, rows_of(width)),
        ((total, LANES), F32, rows_of(LANES)),
        ((total, width), BF16, rows_of(width)),
        ((total // SEGLEN, width), F32, pl.BlockSpec((total // SEGLEN, width), lambda i: (0, 0))),
        ((width, total), BF16, cols_of(width)),
        ((width, total), BF16, cols_of(width)),
        ((width, total), BF16, cols_of(width)),
        ((inners, total), BF16, cols_of(inners)),
    ]
    return pl.pallas_call(
        functools.partial(forward_kernel, ff_chunk=ff_chunk),
        grid=(total // tile,),
        in_specs=[rows_of(width), any_spec, any_spec, any_spec, any_spec, whole(bias), whole(gain), whole(bup)],
        out_specs=[o[2] for o in outs],
        out_shape=[jax.ShapeDtypeStruct(o[0], o[1]) for o in outs],
        scratch_shapes=[
            pltpu.VMEM(w_qkv.shape[1:], BF16),
            pltpu.VMEM(w_out.shape[1:], BF16),
            pltpu.VMEM(w_up.shape[1:], BF16),
            pltpu.VMEM(w_down.shape[1:], BF16),
            pltpu.VMEM((tile, width), BF16),
            pltpu.SemaphoreType.DMA((4,)),
        ],
        compiler_params=pltpu.CompilerParams(vmem_limit_bytes=60 * 2**20),
        name="segment_forward",
    )(x, w_qkv, w_out, w_up, w_down, bias, gain, bup)

def fold_rows(values):
    rows, cols = values.shape
    return jnp.sum(values.reshape(rows // 8, 8, cols), axis=0)


def norm_back(grad, gain, normal, rstd):
    scaled = grad * gain
    a = jnp.mean(scaled, axis=-1, keepdims=True)
    b = jnp.mean(scaled * normal, axis=-1, keepdims=True)
    return (scaled - a - normal * b) * rstd


def early_kernel(
    gcls_ref, ccls_ref, cot_ref, y_ref, n2_ref, r2_ref, slope_ref, n1_ref, r1_ref, wup_hbm, wdown_hbm, gain_ref,
    out_ref, gsecond_ref, ginner_ref, gbranch_ref, sums_ref, bsums_ref, wup, wdown, sems, *, ff_chunk,
):
    step = pl.program_id(0)
    copies = [
        pltpu.make_async_copy(src.at[0], dst, sems.at[i]) for i, (src, dst) in enumerate(((wdown_hbm, wdown), (wup_hbm, wup)))
    ]

    @pl.when(step == 0)
    def _():
        for copy in copies:
            copy.start()
        sums_ref[...] = jnp.zeros_like(sums_ref)
        bsums_ref[...] = jnp.zeros_like(bsums_ref)
        for copy in copies:
            copy.wait()

    rows, width = cot_ref.shape
    segs = rows // SEGLEN
    inners = wup.shape[1]
    gain = gain_ref[0].astype(F32)
    place = lax.broadcasted_iota(jnp.int32, (rows, width), 0)
    gy = cot_ref[...].astype(F32)
    y = y_ref[...].astype(F32)
    for seg in range(segs):
        at = pl.ds(step * segs + seg, 1)
        gy = jnp.where(place == seg * SEGLEN, gcls_ref[at, :], gy)
        y = jnp.where(place == seg * SEGLEN, ccls_ref[at, :], y)
    out_ref[...] = y.astype(BF16)
    n2 = n2_ref[...].astype(F32)
    sums_ref[0] += fold_rows(gy * n2)
    sums_ref[1] += fold_rows(gy)
    g_two = norm_back(gy, gain[1:2], n2, r2_ref[:, 0:1])
    g_second = g_two.astype(BF16)
    gsecond_ref[...] = g_second
    sums_ref[2] += fold_rows(g_second.astype(F32))
    g_first = g_two
    for c in range(inners // ff_chunk):
        cols = slice(c * ff_chunk, (c + 1) * ff_chunk)
        g_inner = mm_nt(g_second, wdown[cols, :]) * slope_ref[:, cols].astype(F32)
        g_low = g_inner.astype(BF16)
        ginner_ref[:, cols] = g_low
        bsums_ref[:, cols] += fold_rows(g_low.astype(F32))
        g_first = g_first + mm_nt(g_low, wup[:, cols])
    n1 = n1_ref[...].astype(F32)
    sums_ref[3] += fold_rows(g_first * n1)
    sums_ref[4] += fold_rows(g_first)
    g_branch = norm_back(g_first, gain[0:1], n1, r1_ref[:, 0:1]).astype(BF16)
    gbranch_ref[...] = g_branch
    sums_ref[5] += fold_rows(g_branch.astype(F32))


def early_backward(gcls, ccls, cot, y, n2, r2, slope, n1, r1, w_up, w_down, gains, tile=256, ff_chunk=768):
    total, width = cot.shape
    inners = w_up.shape[-1]
    any_spec = pl.BlockSpec(memory_space=pl.ANY)

    def rows_of(cols):
        return pl.BlockSpec((tile, cols), lambda i: (i, 0))

    def whole(a):
        return pl.BlockSpec(a.shape, lambda i: (0,) * len(a.shape))

    outs = [
        ((total, width), BF16, rows_of(width)),
        ((total, width), BF16, rows_of(width)),
        ((total, inners), BF16, rows_of(inners)),
        ((total, width), BF16, rows_of(width)),
        ((6, 8, width), F32, pl.BlockSpec((6, 8, width), lambda i: (0, 0, 0))),
        ((8, inners), F32, pl.BlockSpec((8, inners), lambda i: (0, 0))),
    ]
    return pl.pallas_call(
        functools.partial(early_kernel, ff_chunk=ff_chunk),
        grid=(total // tile,),
        in_specs=[whole(gcls), whole(ccls), rows_of(width), rows_of(width), rows_of(width), rows_of(LANES), rows_of(inners),
                  rows_of(width), rows_of(LANES), any_spec, any_spec, whole(gains)],
        out_specs=[o[2] for o in outs],
        out_shape=[jax.ShapeDtypeStruct(o[0], o[1]) for o in outs],
        scratch_shapes=[pltpu.VMEM(w_up.shape[1:], BF16), pltpu.VMEM(w_down.shape[1:], BF16), pltpu.SemaphoreType.DMA((2,))],
        compiler_params=pltpu.CompilerParams(vmem_limit_bytes=60 * 2**20),
        name="early_backward",
    )(gcls, ccls, cot, y, n2, r2, slope, n1, r1, w_up, w_down, gains)

OUTS = 13
NEGATIVE = -1000000000.0
MESH = pl.DeviceIdType.MESH


def turned(values):
    return values.astype(F32).T.astype(BF16)


def cross_kernel(
    cls_ref, cot_hbm, place_ref, keycol_ref, keyrow_ref, table_ref, wqkv_hbm, wout_hbm, wup_hbm, wdown_hbm, bias_ref, gain_ref, bup_ref,
    *refs, ff_chunk, devices,
):
    (
        ccls_ref, gcls_ref, sums_ref, bsums_ref, gpos_ref, xt_ref, mixedt_ref, firstt_ref, hiddent_ref,
        gqkv_ref, gbranch_ref, ginner_ref, gsecond_ref,
    ) = outs = refs[OUTS : 2 * OUTS]
    homes = refs[:OUTS]
    (
        wqkv, wout, wup, wdown, cot_rows, cot_low, packed, gathered, qkv_ref, probs_ref, mixed_ref, slope_ref, whole_ref, sems, out_sems, cot_sems, send_sems, recv_sems,
    ) = refs[2 * OUTS :]
    writes = [pltpu.make_async_copy(src, dst, out_sems.at[i]) for i, (src, dst) in enumerate(zip(outs, homes))]
    copies = [
        pltpu.make_async_copy(src.at[1], dst, sems.at[i])
        for i, (src, dst) in enumerate(
            ((wqkv_hbm, wqkv), (wout_hbm, wout), (wup_hbm, wup), (wdown_hbm, wdown))
        )
    ]
    own, width = cls_ref.shape
    cot_copies = [
        pltpu.make_async_copy(cot_hbm.at[pl.ds(i * SEGLEN, 16)], cot_rows.at[i], cot_sems.at[i]) for i in range(own)
    ]
    for copy in cot_copies + copies:
        copy.start()
    rows = own * devices
    inners = wup.shape[1]
    me = lax.axis_index("seg")
    line = lax.axis_index("row")
    barrier = pltpu.get_barrier_semaphore()
    for hop in range(1, devices):
        pl.semaphore_signal(barrier, inc=1, device_id=(line, lax.rem(me + hop, devices)), device_id_type=MESH)
    packed[0:own, :] = cls_ref[...].astype(BF16)
    for i, copy in enumerate(cot_copies):
        copy.wait()
        cot_low[i : i + 1, :] = cot_rows[i, 0:8, :].astype(F32)[0:1]
    packed[own:, :] = cot_low[...].astype(BF16)
    pl.semaphore_wait(barrier, devices - 1)
    sends = []
    for hop in range(1, devices):
        send = pltpu.make_async_remote_copy(
            src_ref=packed, dst_ref=gathered.at[hop], send_sem=send_sems.at[hop], recv_sem=recv_sems.at[hop],
            device_id=(line, lax.rem(me + hop, devices)), device_id_type=MESH,
        )
        send.start()
        sends.append(send)
    bias = bias_ref[1].astype(F32)
    gain = gain_ref[1].astype(F32)
    up_bias = bup_ref[1:2, :].astype(F32)
    onehot = (place_ref[...] == lax.broadcasted_iota(jnp.int32, (rows, table_ref.shape[0]), 1)).astype(F32)
    embed = mm(onehot.astype(BF16), table_ref[...])
    allowed = keycol_ref[...] == keyrow_ref[...]
    gathered[0] = packed[...]
    for send in sends:
        send.wait()
    for hop in range(devices):
        at = pl.ds(pl.multiple_of(lax.rem(me - hop + devices, devices) * own, own), own)
        block = gathered[hop].astype(F32)
        whole_ref[0, at, :] = block[:own]
        whole_ref[1, at, :] = block[own:]
    x = (whole_ref[0] + embed).astype(BF16)
    gy = whole_ref[1]
    xt_ref[...] = turned(x)
    copies[0].wait()
    for part in range(3):
        cols = slice(part * width, (part + 1) * width)
        out = mm(x, wqkv[:, cols])
        if part == 0:
            out = out + bias[0:1]
        if part == 2:
            out = out + bias[1:2]
        qkv_ref[:, cols] = out.astype(BF16)
    for pair in range(width // LANES):
        q, k, v = (qkv_ref[:, part * width + pair * LANES : part * width + (pair + 1) * LANES] for part in range(3))
        scores = jnp.where(allowed, mm_nt(k, stack_heads(q * HDIM**-0.5)), NEGATIVE)
        e = jnp.exp(scores - jnp.max(scores, axis=0, keepdims=True))
        p = e * (1.0 / jnp.sum(e, axis=0, keepdims=True))
        probs_ref[pair] = p
        pt = p.T.astype(BF16)
        low = low_lanes((rows, LANES))
        mixed = jnp.where(low, mm(pt[:rows], v), mm(pt[rows:], v))
        mixed_ref[:, pair * LANES : (pair + 1) * LANES] = mixed.astype(BF16)
    copies[1].wait()
    mixed = mixed_ref[...]
    mixedt_ref[...] = turned(mixed)
    n1, r1 = norm_stats(x.astype(F32) + mm(mixed, wout[...]) + bias[2:3])
    first = (n1 * gain[0:1] + bias[3:4]).astype(BF16)
    firstt_ref[...] = turned(first)
    copies[2].wait()
    copies[3].wait()
    total = first.astype(F32) + bias[4:5]
    for c in range(inners // ff_chunk):
        cols = slice(c * ff_chunk, (c + 1) * ff_chunk)
        hidden, slope = gelu_both(mm(first, wup[:, cols]) + up_bias[:, cols])
        hidden = hidden.astype(BF16)
        hiddent_ref[cols, :] = turned(hidden)
        slope_ref[:, cols] = slope
        total = total + mm(hidden, wdown[cols, :])
    n2, r2 = norm_stats(total)
    mine = pl.ds(pl.multiple_of(me * own, own), own)
    whole_ref[0] = (n2 * gain[1:2] + bias[5:6]).astype(BF16).astype(F32)
    ccls_ref[...] = whole_ref[0, mine, :]
    for i in (0, 5, 6, 7, 8):
        writes[i].start()

    def row_sum(values):
        return jnp.sum(values.astype(F32), axis=0, keepdims=True)

    sums_ref[0:1, :] = row_sum(gy * n2)
    sums_ref[1:2, :] = row_sum(gy)
    g_two = norm_back(gy, gain[1:2], n2, r2)
    g_second = g_two.astype(BF16)
    gsecond_ref[...] = g_second
    sums_ref[2:3, :] = row_sum(g_second)
    g_first = g_two
    for c in range(inners // ff_chunk):
        cols = slice(c * ff_chunk, (c + 1) * ff_chunk)
        g_inner = (mm_nt(g_second, wdown[cols, :]) * slope_ref[:, cols]).astype(BF16)
        ginner_ref[:, cols] = g_inner
        bsums_ref[:, cols] = row_sum(g_inner)
        g_first = g_first + mm_nt(g_inner, wup[:, cols])
    sums_ref[3:4, :] = row_sum(g_first * n1)
    sums_ref[4:5, :] = row_sum(g_first)
    g_one = norm_back(g_first, gain[0:1], n1, r1)
    g_branch = g_one.astype(BF16)
    gbranch_ref[...] = g_branch
    sums_ref[5:6, :] = row_sum(g_branch)
    for i in (10, 11, 12):
        writes[i].start()
    g_mixed = mm_nt(g_branch, wout[...]).astype(BF16)
    for pair in range(width // LANES):
        lanes = [slice(part * width + pair * LANES, part * width + (pair + 1) * LANES) for part in range(3)]
        q, k, v = (qkv_ref[:, at] for at in lanes)
        p = probs_ref[pair]
        g_out = stack_heads(g_mixed[:, lanes[0]])
        g_p = mm_nt(v, g_out)
        g_s = p * (g_p - jnp.sum(g_p * p, axis=0, keepdims=True))
        g_st = g_s.T.astype(BF16)
        g_s = g_s.astype(BF16)
        low = low_lanes((rows, LANES))
        g_q = jnp.where(low, mm(g_st[:rows], k), mm(g_st[rows:], k)) * HDIM**-0.5
        gqkv_ref[:, lanes[0]] = g_q.astype(BF16)
        gqkv_ref[:, lanes[1]] = mm(g_s, stack_heads(q * HDIM**-0.5)).astype(BF16)
        gqkv_ref[:, lanes[2]] = mm(p.astype(BF16), g_out).astype(BF16)
    g_qkv = gqkv_ref[...]
    sums_ref[6:7, :] = row_sum(g_qkv[:, :width])
    sums_ref[7:8, :] = row_sum(g_qkv[:, 2 * width :])
    g_x = g_one + mm_nt(g_qkv, wqkv[...])
    whole_ref[1] = g_x
    gcls_ref[...] = whole_ref[1, mine, :]
    gpos_ref[...] = lax.dot_general(onehot, g_x, (((0,), (0,)), ((), ())), preferred_element_type=F32, precision=lax.Precision.HIGHEST)
    for i in (1, 2, 3, 4, 9):
        writes[i].start()
    for write in writes:
        write.wait()


def cross_block(cls, cot, place, keys, table, w_qkv, w_out, w_up, w_down, biases, gains, b_up, devices, ff_chunk=768):
    own, width = cls.shape
    rows = own * devices
    inners = w_up.shape[-1]
    vmem = pl.BlockSpec(memory_space=pltpu.VMEM)
    any_spec = pl.BlockSpec(memory_space=pl.ANY)
    outs = [
        ((own, width), F32), ((own, width), F32), ((8, width), F32), ((1, inners), F32), (table.shape, F32),
        ((width, rows), BF16), ((width, rows), BF16), ((width, rows), BF16), ((inners, rows), BF16),
        ((rows, 3 * width), BF16), ((rows, width), BF16), ((rows, inners), BF16), ((rows, width), BF16),
    ]
    return pl.pallas_call(
        functools.partial(cross_kernel, ff_chunk=ff_chunk, devices=devices),
        in_specs=[vmem, any_spec] + [vmem] * 4 + [any_spec] * 4 + [vmem] * 3,
        out_specs=[any_spec] * len(outs),
        out_shape=[jax.ShapeDtypeStruct(*o) for o in outs],
        scratch_shapes=[pltpu.VMEM(*o) for o in outs]
        + [
            pltpu.VMEM(w_qkv.shape[1:], BF16),
            pltpu.VMEM(w_out.shape[1:], BF16),
            pltpu.VMEM(w_up.shape[1:], BF16),
            pltpu.VMEM(w_down.shape[1:], BF16),
            pltpu.VMEM((own, 16, width), BF16),
            pltpu.VMEM((own, width), F32),
            pltpu.VMEM((2 * own, width), BF16),
            pltpu.VMEM((devices, 2 * own, width), BF16),
            pltpu.VMEM((rows, 3 * width), BF16),
            pltpu.VMEM((width // LANES, rows, 2 * rows), F32),
            pltpu.VMEM((rows, width), BF16),
            pltpu.VMEM((rows, inners), F32),
            pltpu.VMEM((2, rows, width), F32),
            pltpu.SemaphoreType.DMA((4,)),
            pltpu.SemaphoreType.DMA((OUTS,)),
            pltpu.SemaphoreType.DMA((own,)),
            pltpu.SemaphoreType.DMA((devices,)),
            pltpu.SemaphoreType.DMA((devices,)),
        ],
        compiler_params=pltpu.CompilerParams(vmem_limit_bytes=50 * 2**20, collective_id=0, has_side_effects=True),
        name="cross_block",
    )(cls, cot, place, keys, jnp.tile(keys.reshape(1, rows), (1, 2)), table, w_qkv, w_out, w_up, w_down, biases, gains, b_up)

RING = 4
CROSS_UNITS = 3
SEG_UNITS = 12
UNITS = CROSS_UNITS + SEG_UNITS
CHAINS = UNITS + 1
PART = 48
GROUPS = 3
EARLY = 9
TILES = 4
GROUP_STEPS = TILES + 1
LAST_AT = EARLY + GROUPS * GROUP_STEPS
STEPS = LAST_AT + TILES


PAIR_MOMENTS = [(4, 6, 8, 13), (6, 8, 11, 16), (8, 11, 14, 19), (11, 14, 17, 21), (14, 17, 20, 24), (17, 20, 23, 26)]
LATE_MOMENTS = [(14, 18, 21, 23, 26), (19, 23, 25, 27, STEPS), (24, STEPS, STEPS, STEPS, STEPS), (STEPS,) * 5]
SMALL_MOMENTS = (1, 4, 6, 8, 10, 12)
SMALL_LATE = (24, 25, 26, STEPS, STEPS, STEPS)


def comm_schedule():
    table = {s: [] for s in range(STEPS + 1)}
    for pair, moments in enumerate(PAIR_MOMENTS):
        for n in (2 * pair, 2 * pair + 1):
            for action, at in zip(("two", "three", "final", "out"), moments):
                table[at].append((action, n))
            if n + 4 < CROSS_UNITS + EARLY:
                table[moments[0]].append(("send", n + 4))
    first = CROSS_UNITS + EARLY
    table[EARLY + 1].append(("one", first - 1))
    for n, moments in enumerate(LATE_MOMENTS, first):
        for action, at in zip(("one", "two", "three", "final", "out"), moments):
            if action != "one" or n < UNITS:
                table[at].append((action, n))
    for d in range(6):
        table[SMALL_MOMENTS[d]].append(("small", d))
        table[SMALL_LATE[d]].append(("late", d))
    order = ("small", "late", "one", "out", "final", "three", "two", "send")
    for at in range(STEPS):
        table[at].sort(key=lambda item: (order.index(item[0]), item[1]))
    rank = {"late": 0, "two": 1, "three": 2, "final": 3, "out": 4}
    table[STEPS].sort(key=lambda item: (rank[item[0]] if item[0] != "late" else item[1] - 2.5, item[1]))
    return table


def add_low(a, b):
    return (a.astype(F32) + b.astype(F32)).astype(BF16)


def late_kernel(
    firstt, ginner, hiddent, gsecond, mixedt, gbranch, xt, qkv, probs, wqkv_hbm, wout_hbm,
    cfirstt, cginner, chiddent, cgsecond, cmixedt, cgbranch, cxt, cgqkv,
    sums, bsums, csums, cbsums, gpos,
    dqkv_ref, dout_ref, dup_ref, ddown_ref, small_ref, gx_ref,
    aslot, bslot, qkv_slot, probs_slot, gbranch_slot, gx_slot, wqkv, wout, fold, csend, crecv, keep, r1, r2, r3, rf, acc, racc, late_acc, late_racc,
    load_sems, tile_sems, store_sems, weight_sems, csend_sems, crecv_sems, s1_sems, q1_sems, s2_sems, q2_sems, s3_sems, q3_sems, sf_sems, qf_sems, sa_sems, qa_sems,
    *, share,
):
    width = bslot.shape[-1]
    line, z = lax.axis_index("row"), lax.axis_index("seg")
    y, x, c = line // 4, (line // 2) % 2, line % 2
    zh, zl = z // 2, z % 2
    flip_c = (y * 4 + x * 2 + 1 - c, z)
    flip_x = (y * 4 + (1 - x) * 2 + c, z)
    flip_y = ((1 - y) * 4 + x * 2 + c, z)
    flip_zl = (line, zh * 2 + 1 - zl)
    flip_zh = (line, (1 - zh) * 2 + zl)
    flip_yzh = ((1 - y) * 4 + x * 2 + c, (1 - zh) * 2 + zl)
    barrier = pltpu.get_barrier_semaphore()
    for peer in (flip_c, flip_x, flip_y, flip_zl, flip_zh, flip_yzh):
        pl.semaphore_signal(barrier, inc=1, device_id=peer, device_id_type=MESH)

    tile = gbranch_slot.shape[1]
    segs = tile // SEGLEN

    def a_slot(u):
        return jnp.where((u < 4) | (u >= EARLY), 0, (u + 1) % 2)

    def b_slot(u):
        return jnp.where(u < 4, u % 2, jnp.where(u < EARLY, u // 8, u - EARLY))

    def load_unit(u, do):
        def act(src, dst, side):
            getattr(pltpu.make_async_copy(src, dst, load_sems.at[side]), do)()

        def columns(ref, j):
            return ref.at[:, pl.ds(pl.multiple_of(j * width, width), width)]

        @pl.when(u == 0)
        def _():
            act(firstt, aslot.at[0], 0)

        @pl.when(u < 4)
        def _():
            act(columns(ginner, u), bslot.at[u % 2], 1)

        @pl.when((u >= 4) & (u < 8))
        def _():
            act(hiddent.at[:, :, :, u - 4], aslot.at[(u + 1) % 2], 0)

        @pl.when(u == 4)
        def _():
            act(gsecond, bslot.at[0], 1)

        @pl.when(u == 8)
        def _():
            act(mixedt, aslot.at[1], 0)
            act(gbranch, bslot.at[1], 1)

        @pl.when(u == EARLY)
        def _():
            act(xt, aslot.at[0], 0)

    def tile_rows(i):
        return pl.ds(pl.multiple_of(i * tile, tile), tile)

    def load_tile(j, i, slot, late, do):
        copies = [pltpu.make_async_copy(gbranch.at[tile_rows(i)], gbranch_slot.at[slot], tile_sems.at[slot, 0])]
        if not late:
            copies.append(pltpu.make_async_copy(qkv.at[j, tile_rows(i)], qkv_slot.at[slot], tile_sems.at[slot, 1]))
            copies.append(
                pltpu.make_async_copy(probs.at[pl.ds(i * segs, segs), pl.ds(2 * j, 2)], probs_slot.at[slot], tile_sems.at[slot, 2])
            )
        for copy in copies:
            getattr(copy, do)()

    def place(s):
        group = (s - EARLY) // GROUP_STEPS
        return group, (s - EARLY) % GROUP_STEPS

    def load(s, do):
        group, part = place(s)
        inside = (s >= EARLY) & (s < LAST_AT)

        @pl.when(s < EARLY)
        def _():
            load_unit(s, do)

        @pl.when(inside & (part < TILES))
        def _():
            load_tile(group, part, part % 2, False, do)

        @pl.when(inside & (part == TILES))
        def _():
            load_unit(EARLY + group, do)

        @pl.when(s >= LAST_AT)
        def _():
            load_tile(0, s - LAST_AT, (s - LAST_AT) % 2, True, do)

    def store_gx(i):
        return pltpu.make_async_copy(gx_slot.at[i % 2], gx_ref.at[tile_rows(i)], store_sems.at[i % 2])

    weight_copies = [pltpu.make_async_copy(wout_hbm.at[0], wout, weight_sems.at[0])]
    for j in range(GROUPS):
        for part in range(3):
            weight_copies.append(
                pltpu.make_async_copy(
                    wqkv_hbm.at[0, :, pl.ds(part * width + j * GROUP, GROUP)],
                    wqkv.at[j, :, pl.ds(part * GROUP, GROUP)],
                    weight_sems.at[1 + 3 * j + part],
                )
            )
    load(0, "start")

    def remote(src, dst, send_sem, recv_sem, peer):
        return pltpu.make_async_remote_copy(
            src_ref=src, dst_ref=dst, send_sem=send_sem, recv_sem=recv_sem, device_id=peer, device_id_type=MESH
        )

    def choose(t, a, b):
        return t * a + (1 - t) * b

    def pick(t, a, b):
        return tuple(choose(t, p, q) for p, q in zip(a, b))

    def way(t):
        bits = (choose(t, x, y), choose(t, zl, x), choose(t, zh, zl))
        peers = (pick(t, flip_x, flip_y), pick(t, flip_zl, flip_x), pick(t, flip_zh, flip_zl))
        return bits, peers

    def core_copy(n):
        slot = n % RING
        return remote(csend.at[slot], crecv.at[slot], csend_sems.at[slot], crecv_sems.at[slot], flip_c)

    def part_of(n):
        if isinstance(n, int) and n >= UNITS - 1:
            half = width // 2
            return UNITS - 1, slice((n - UNITS + 1) * half, (n - UNITS + 2) * half)
        return n, slice(0, width)

    def copy_one(n, t):
        (b1, _, _), (peer, _, _) = way(t)
        m, cols = part_of(n)
        return remote(keep.at[m, pl.ds(4 * (1 - b1), 4), :, cols], r1.at[m, :, :, cols], s1_sems.at[n], q1_sems.at[n], peer)

    def copy_two(n, t):
        (b1, b2, _), (_, peer, _) = way(t)
        m, cols = part_of(n)
        return remote(keep.at[m, pl.ds(4 * b1 + 2 * (1 - b2), 2), :, cols], r2.at[m, :, :, cols], s2_sems.at[n], q2_sems.at[n], peer)

    def copy_three(n, t):
        (b1, b2, b3), (_, _, peer) = way(t)
        m, cols = part_of(n)
        return remote(keep.at[m, 4 * b1 + 2 * b2 + 1 - b3, :, cols], r3.at[m, :, cols], s3_sems.at[n], q3_sems.at[n], peer)

    def own_block(n, t):
        (b1, b2, b3), _ = way(t)
        m, cols = part_of(n)
        return keep.at[m, 4 * b1 + 2 * b2 + b3, :, cols]

    def step_one(n, t):
        core_copy(n).wait_recv()
        keep[n] = add_low(keep[n], crecv[n % RING])

        @pl.when((n < 4) | (n >= CROSS_UNITS + EARLY))
        def _():
            copy_one(n, t).start()

        if isinstance(n, int) and n == UNITS - 1:
            copy_one(n + 1, 1).start()

    def step_two(n, t):
        (b1, _, _), _ = way(t)
        copy_one(n, t).wait()
        m, cols = part_of(n)
        at = pl.ds(4 * b1, 4)
        keep[m, at, :, cols] = add_low(keep[m, at, :, cols], r1[m, :, :, cols])
        copy_two(n, t).start()

    def step_three(n, t):
        (b1, b2, _), _ = way(t)
        copy_two(n, t).wait()
        m, cols = part_of(n)
        at = pl.ds(4 * b1 + 2 * b2, 2)
        keep[m, at, :, cols] = add_low(keep[m, at, :, cols], r2[m, :, :, cols])
        copy_three(n, t).start()

    def final_to(n, t, slot, peer):
        m, cols = part_of(n)
        return remote(own_block(n, t), rf.at[m, slot, :, cols], sf_sems.at[n], qf_sems.at[n, slot], peer)

    def sends_final(n, t, act):
        straight = (y == 1) & ((t == 1) | (zh == 1))

        @pl.when(straight)
        def _():
            act(final_to(n, t, 0, flip_y))

        @pl.when((t == 0) & (y == 0) & (zh == 1))
        def _():
            act(final_to(n, t, 0, flip_zh))

        @pl.when((t == 0) & (y == 1) & (zh == 0))
        def _():
            act(final_to(n, t, 1, flip_yzh))

    def step_final(n, t):
        copy_three(n, t).wait()
        (b1, b2, b3), _ = way(t)
        m, cols = part_of(n)
        at = 4 * b1 + 2 * b2 + b3
        keep[m, at, :, cols] = add_low(keep[m, at, :, cols], r3[m, :, cols])
        sends_final(n, t, lambda copy: copy.start())

    def put(u, value, cols=slice(0, 16 * PART)):
        def columns(j):
            return pl.ds(pl.multiple_of(j * width, width), width)

        @pl.when(u < 4)
        def _():
            dup_ref[:, columns(u)] = value

        @pl.when((u >= 4) & (u < 8))
        def _():
            ddown_ref[pl.ds(pl.multiple_of((u - 4) * PART, PART), PART), :] = value

        @pl.when(u == 8)
        def _():
            dout_ref[...] = value

        for j in range(GROUPS):
            @pl.when(u == EARLY + j)
            def _(j=j):
                for part in range(3):
                    first, last = max(part * GROUP, cols.start), min((part + 1) * GROUP, cols.stop)
                    if first < last:
                        to = part * (width - GROUP) + j * GROUP
                        dqkv_ref[:, to + first : to + last] = value[:, first - cols.start : last - cols.start]

    def step_out(n, t, u):
        m, cols = part_of(n)
        sends_final(n, t, lambda copy: copy.wait_send())

        @pl.when(y == 0)
        def _():
            final_to(n, t, 0, flip_y).wait_recv()

            @pl.when((t == 1) | (zh == 0))
            def _():
                put(u, own_block(n, t)[...].astype(F32) + rf[m, 0, :, cols].astype(F32), cols)

            @pl.when((t == 0) & (zh == 1))
            def _():
                final_to(n, t, 1, flip_y).wait_recv()
                put(u, rf[m, 0, :, cols].astype(F32) + rf[m, 1, :, cols].astype(F32), cols)

    def cross_final(n):
        return remote(keep.at[n, pl.ds(2 * x, 2)], rf.at[n], sf_sems.at[n], qf_sems.at[n, 0], flip_y)

    def cross_step_final(n):
        copy_two(n, 0).wait()
        at = pl.ds(4 * y + 2 * x, 2)
        keep[n, at] = add_low(keep[n, at], r2[n])

        @pl.when(y == 0)
        def _():
            cross_final(n).start()

    def cross_step_out(n, index):
        @pl.when(y == 0)
        def _():
            cross_final(n).wait_send()

        @pl.when(y == 1)
        def _():
            cross_final(n).wait_recv()
            for sub in range(4):
                block = rf[n, sub] if sub < 2 else keep[n, 4 + 2 * x + sub - 2]
                put(4 * index + sub, block.astype(F32))

    small_peers = (flip_c, flip_x, flip_y, flip_zl, flip_zh)

    rounds = ((acc, racc), (late_acc, late_racc))

    def small_copy(late, d):
        own, other = rounds[late]
        return remote(own.at[d], other.at[d], sa_sems.at[late, d], qa_sems.at[late, d], small_peers[d])

    def small_step(late, d):
        own, other = rounds[late]
        small_copy(late, d).wait()
        own[d + 1] = own[d] + other[d]
        if d + 1 < len(small_peers):
            small_copy(late, d + 1).start()
        elif late:
            small_ref[0:8, :] = acc[d + 1, 0:8, :] + own[d + 1]
            small_ref[8:32, :] = acc[d + 1, 8:32, :]

    seg_rows = [jnp.sum(sums[i], axis=0, keepdims=True) for i in range(6)]
    seg_up = jnp.sum(bsums[...], axis=0, keepdims=True)
    order = (6, 7, 5, 4, 2, 1)
    for i, row in enumerate(order):
        if row < 6:
            acc[0, i : i + 1, :] = seg_rows[row]
        acc[0, 6 + i : 7 + i, :] = csums[row : row + 1, :] * share
    for i, row in enumerate((3, 0)):
        acc[0, 12 + i : 13 + i, :] = seg_rows[row]
        acc[0, 14 + i : 15 + i, :] = csums[row : row + 1, :] * share
    for i in range(4):
        acc[0, 16 + i : 17 + i, :] = seg_up[:, i * width : (i + 1) * width]
        acc[0, 20 + i : 21 + i, :] = cbsums[:, i * width : (i + 1) * width] * share
    acc[0, 0:2, :] = jnp.zeros_like(acc[0, 0:2, :])
    acc[0, 24:32, :] = gpos[...] * share
    late_acc[0] = jnp.zeros_like(late_acc[0])

    def cross_unit(n, parts):
        if n >= RING:
            core_copy(n).wait_send()
        for rel in (1, 0):
            core = c if rel == 0 else 1 - c
            for sub, (left, right) in enumerate(parts):
                for far in range(2):
                    value = mm(left(far, core), right).astype(BF16)
                    at = (sub // 2) * 4 + far * 2 + sub % 2
                    if rel == 1:
                        csend[n % RING, at] = value
                    else:
                        keep[n, at] = value
            if rel == 1:
                if n == 0:
                    pl.semaphore_wait(barrier, 6)
                core_copy(n).start()

    def plain(ref):
        return lambda far, core: ref[far, core, z]

    def nested(ref, j):
        return lambda far, core: ref[far, core, z, j]

    def cut(ref, j):
        return ref[:, j * width : (j + 1) * width]

    def cut_group(ref, j):
        return jnp.concatenate([ref[:, part * width + j * GROUP : part * width + (j + 1) * GROUP] for part in range(3)], axis=1)

    cross_parts = (
        lambda: [(plain(cfirstt), cut(cginner, j)) for j in range(4)],
        lambda: [(nested(chiddent, j), cgsecond[...]) for j in range(4)],
        lambda: [(plain(cmixedt), cgbranch[...])] + [(plain(cxt), cut_group(cgqkv, j)) for j in range(GROUPS)],
    )

    def compute(u):
        n = u + CROSS_UNITS - jnp.maximum(CROSS_UNITS - 1 - u, 0)
        t = n % 2
        @pl.when(n >= RING)
        def _():
            core_copy(n).wait_send()

        right = bslot[b_slot(u)]
        for rel in (1, 0):
            core = c if rel == 0 else 1 - c
            left = aslot[a_slot(u), :, core].reshape(8 * PART, -1)
            value = mm(left, right).astype(BF16)
            for far in range(2):
                for part in range(4):
                    block = value[(far * 4 + part) * PART : (far * 4 + part + 1) * PART]
                    ways = far * 4 + (part % 2) * 2 + part // 2, (part // 2) * 4 + far * 2 + part % 2
                    for side, way_of in ((0, t), (1, t + (1 - t) * (n // (UNITS - 1)))):
                        at = choose(way_of, *ways)
                        cols = slice(side * width // 2, (side + 1) * width // 2)
                        if rel == 1:
                            csend[n % RING, at, :, cols] = block[:, cols]
                        else:
                            keep[n, at, :, cols] = block[:, cols]
            if rel == 1:
                core_copy(n).start()

        @pl.when(n < CROSS_UNITS + EARLY)
        def _():
            step_one(n - 1, (n - 1) % 2)

    def attention_tile(j, i):
        slot = i % 2
        out_rows = pl.ds(pl.multiple_of(j * GROUP, GROUP), GROUP)
        g_mixed = mm_nt(gbranch_slot[slot], wout[out_rows, :]).astype(BF16)
        for seg in range(segs):
            at = slice(seg * SEGLEN, (seg + 1) * SEGLEN)
            to = pl.ds(pl.multiple_of(i * tile + seg * SEGLEN, SEGLEN), SEGLEN)
            for half in range(2):
                lanes = pair_lanes(half)
                q = qkv_slot[slot, at, lanes[0]] * HDIM**-0.5
                k = qkv_slot[slot, at, lanes[1]]
                v = qkv_slot[slot, at, lanes[2]]
                p_low = probs_slot[slot, seg, half]
                p = p_low.astype(F32)
                g_out = stack_heads(g_mixed[at, lanes[0]])
                g_p = mm_nt(v, g_out)
                g_s = (p * (g_p - jnp.sum(g_p * p, axis=0, keepdims=True))).astype(BF16)
                g_v = mm(p_low, g_out).astype(BF16)
                g_k = mm(g_s, stack_heads(q)).astype(BF16)
                g_st = jnp.concatenate([g_s[:, :SEGLEN].T, g_s[:, SEGLEN:].T], axis=1)
                g_q = (mm(g_st, stack_heads(k)) * HDIM**-0.5).astype(BF16)
                bslot[j, to, lanes[0]] = g_q
                bslot[j, to, lanes[1]] = g_k
                bslot[j, to, lanes[2]] = g_v
                fold[0, j, :, lanes[0]] += fold_rows(g_q.astype(F32))
                fold[1, j, :, lanes[0]] += fold_rows(g_v.astype(F32))

    def last_tile(i):
        slot = i % 2

        @pl.when(i >= 2)
        def _():
            store_gx(i - 2).wait()

        total = gbranch_slot[slot].astype(F32)
        for j in range(GROUPS):
            total = total + mm_nt(bslot[j, tile_rows(i), :], wqkv[j])
        gx_slot[slot] = total.astype(BF16)
        store_gx(i).start()

    def run(action, n):
        if action in ("small", "late"):
            late = int(action == "late")
            if late and n == 0:
                for row in range(2):
                    for j in range(GROUPS):
                        late_acc[0, row : row + 1, j * GROUP : (j + 1) * GROUP] = jnp.sum(fold[row, j], axis=0, keepdims=True)
            if n == 0:
                small_copy(late, 0).start()
            else:
                small_step(late, n - 1)
            return
        t = n % 2
        cross = t == 0 and n < 2 * CROSS_UNITS
        if action == "one":
            step_one(n, t)
        elif action == "send":
            copy_one(n, t).start()
        elif action == "two":
            step_two(n, t)
        elif action == "three":
            cross_step_final(n) if cross else step_three(n, t)
        elif action == "final":
            cross_step_out(n, n // 2) if cross else step_final(n, t)
        elif not cross:
            step_out(n, t, n // 2 if n < 2 * CROSS_UNITS else min(n, UNITS - 1) - CROSS_UNITS)

    schedule = comm_schedule()

    def step(s, carry):
        for at in range(STEPS):
            if schedule[at]:
                @pl.when(s == at)
                def _(at=at):
                    for action, n in schedule[at]:
                        run(action, n)

        @pl.when(s == EARLY)
        def _():
            for copy in weight_copies:
                copy.wait()

        for i in range(1, CROSS_UNITS):
            @pl.when(s == i)
            def _(i=i):
                cross_unit(2 * i, cross_parts[i]())
                step_one(2 * i - 1, 1)

        load(s, "wait")

        @pl.when(s == 1)
        def _():
            for copy in weight_copies:
                copy.start()

        @pl.when(s + 1 < STEPS)
        def _():
            load(s + 1, "start")

        group, part = place(s)
        inside = (s >= EARLY) & (s < LAST_AT)
        multiply = (s < EARLY) | (inside & (part == TILES))

        @pl.when(multiply)
        def _():
            compute(jnp.where(s < EARLY, s, EARLY + group))

        @pl.when(inside & (part < TILES))
        def _():
            attention_tile(group, part)

        @pl.when(s >= LAST_AT)
        def _():
            last_tile(s - LAST_AT)

        return carry

    fold[...] = jnp.zeros_like(fold)
    cross_unit(0, cross_parts[0]())
    lax.fori_loop(0, STEPS, step, 0)
    for action, n in schedule[STEPS]:
        run(action, n)
    for i in range(TILES - 2, TILES):
        store_gx(i).wait()
    for n in range(UNITS - RING, UNITS):
        core_copy(n).wait_send()


def late_backward(big, cross, small, attn, share):
    firstt, ginner, hiddent, gsecond, mixedt, gbranch, xt = big
    qkv, probs, w_qkv, w_out = attn
    cfirstt, cginner, chiddent, cgsecond, cmixedt, cgbranch, cxt, cgqkv = cross
    width, depth = firstt.shape
    inners = ginner.shape[1]
    rows = cfirstt.shape[1]
    tile = depth // TILES
    assert width == 16 * PART and inners == 4 * width

    def blocks(a, n):
        return a.reshape((2, 2, 4) + ((n,) if n > 1 else ()) + (PART, a.shape[1]))

    operands = [
        blocks(firstt, 1), ginner, blocks(hiddent, 4), gsecond, blocks(mixedt, 1), gbranch, blocks(xt, 1), qkv, probs, w_qkv, w_out,
        blocks(cfirstt, 1), cginner, blocks(chiddent, 4), cgsecond, blocks(cmixedt, 1), cgbranch, blocks(cxt, 1), cgqkv, *small,
    ]
    vmem = pl.BlockSpec(memory_space=pltpu.VMEM)
    any_spec = pl.BlockSpec(memory_space=pl.ANY)
    outs = [((PART, 3 * width), F32), ((PART, width), F32), ((PART, inners), F32), ((4 * PART, width), F32), ((32, width), F32), ((depth, width), BF16)]
    segs = tile // SEGLEN
    dma = pltpu.SemaphoreType.DMA
    return pl.pallas_call(
        functools.partial(late_kernel, share=share),
        in_specs=[any_spec] * 11 + [vmem] * (len(operands) - 11),
        out_specs=[vmem] * 5 + [any_spec],
        out_shape=[jax.ShapeDtypeStruct(*o) for o in outs],
        scratch_shapes=[
            pltpu.VMEM((2, 2, 2, 4, PART, depth), BF16),
            pltpu.VMEM((GROUPS, depth, width), BF16),
            pltpu.VMEM((2, tile, width), BF16),
            pltpu.VMEM((2, segs, 2, SEGLEN, 2 * SEGLEN), BF16),
            pltpu.VMEM((2, tile, width), BF16),
            pltpu.VMEM((2, tile, width), BF16),
            pltpu.VMEM((GROUPS, width, 3 * GROUP), BF16),
            pltpu.VMEM(w_out.shape[1:], BF16),
            pltpu.VMEM((2, GROUPS, 8, GROUP), F32),
            pltpu.VMEM((RING, 8, PART, width), BF16),
            pltpu.VMEM((RING, 8, PART, width), BF16),
            pltpu.VMEM((UNITS, 8, PART, width), BF16),
            pltpu.VMEM((UNITS, 4, PART, width), BF16),
            pltpu.VMEM((UNITS, 2, PART, width), BF16),
            pltpu.VMEM((UNITS, PART, width), BF16),
            pltpu.VMEM((UNITS, 2, PART, width), BF16),
            pltpu.VMEM((6, 32, width), F32),
            pltpu.VMEM((5, 32, width), F32),
            pltpu.VMEM((6, 8, width), F32),
            pltpu.VMEM((5, 8, width), F32),
            dma((2,)), dma((2, 3)), dma((2,)), dma((1 + 3 * GROUPS,)), dma((RING,)), dma((RING,)), dma((CHAINS,)), dma((CHAINS,)), dma((CHAINS,)), dma((CHAINS,)),
            dma((CHAINS,)), dma((CHAINS,)), dma((CHAINS,)), dma((CHAINS, 2)), dma((2, 5)), dma((2, 5)),
        ],
        compiler_params=pltpu.CompilerParams(vmem_limit_bytes=63 * 2**20, collective_id=1, has_side_effects=True),
        name="late_backward",
    )(*operands)

def finish_kernel(gx_ref, a_ref, b_ref, c_ref, d_ref, gx_out, a_out, b_out, c_out, d_out):
    gx_out[...] = gx_ref[...].astype(F32)

    @pl.when(pl.program_id(0) == 0)
    def _():
        for src, dst in ((a_ref, a_out), (b_ref, b_out), (c_ref, c_out), (d_ref, d_out)):
            dst[...] = src[...]


def finish(gx, grads, tile=512):
    total, width = gx.shape
    rows = pl.BlockSpec((tile, width), lambda i: (i, 0))
    held = [pl.BlockSpec(g.shape, lambda i: (0, 0)) for g in grads]
    return pl.pallas_call(
        finish_kernel,
        grid=(total // tile,),
        in_specs=[rows] + held,
        out_specs=[rows] + held,
        out_shape=[jax.ShapeDtypeStruct(gx.shape, F32)] + [jax.ShapeDtypeStruct(g.shape, F32) for g in grads],
        name="finish",
    )(gx, *grads)


def small_grads(sums, bsums, csums, cbsums, gpos, bias_sums, cross_share):
    seg_rows = jnp.concatenate([jnp.sum(sums, axis=1), bias_sums])
    cross_rows = csums * cross_share
    order = jnp.array([6, 7, 5, 4, 2, 1])
    biases = jnp.stack([seg_rows[order], cross_rows[order]])
    gains = jnp.stack([seg_rows[jnp.array([3, 0])], cross_rows[jnp.array([3, 0])]])
    ups = jnp.stack([jnp.sum(bsums, axis=0), cbsums[0] * cross_share])
    return biases.reshape(-1), gains.reshape(-1), ups.reshape(-1), (gpos * cross_share).reshape(-1)


def attention_back(qkv, probs, gbranch, w_qkv, w_out):
    total, width = gbranch.shape
    heads = width // HDIM
    segs = total // SEGLEN
    scale = HDIM**-0.5

    def split(a):
        return a.reshape(segs, SEGLEN, heads, HDIM)

    def merge(a):
        return a.reshape(total, width)

    q, k, v = (
        split(qkv[:, :, part * GROUP : (part + 1) * GROUP].transpose(1, 0, 2).reshape(total, width)) for part in range(3)
    )
    p_low = probs.reshape(segs, heads // 2, SEGLEN, 2, SEGLEN).transpose(0, 1, 3, 2, 4).reshape(segs, heads, SEGLEN, SEGLEN)
    g_out = split(mm_nt(gbranch, w_out).astype(BF16))
    p = p_low.astype(F32)
    g_p = jnp.einsum("sqhd,skhd->shkq", g_out, v, preferred_element_type=F32)
    g_s = (p * (g_p - jnp.sum(g_p * p, axis=2, keepdims=True))).astype(BF16)
    g_v = jnp.einsum("shkq,sqhd->skhd", p_low, g_out, preferred_element_type=F32)
    g_k = jnp.einsum("shkq,sqhd->skhd", g_s, q, preferred_element_type=F32) * scale
    g_q = jnp.einsum("shkq,skhd->sqhd", g_s, k, preferred_element_type=F32) * scale
    g_qkv = jnp.concatenate([merge(g_q), merge(g_k), merge(g_v)], axis=1).astype(BF16)
    return g_qkv, gbranch.astype(F32) + mm_nt(g_qkv, w_qkv)


def generic_total(seg_pairs, cross_pairs, small, planes, own):
    axes = ("row", "seg")
    me = lax.axis_index("seg")
    shards = [
        lax.psum_scatter(part, axes, scatter_dimension=0, tiled=True) for part in small_grads(*small, 1.0 / planes)
    ]

    def mine(values, dim):
        return lax.dynamic_slice_in_dim(values, me * own, own, dim)

    big = []
    for at in (6, 4, 0, 2):
        cross = mm(mine(cross_pairs[at], 1), mine(cross_pairs[at + 1], 0))
        both = jnp.concatenate([mm(seg_pairs[at], seg_pairs[at + 1]), cross], axis=0)
        big.append(lax.psum_scatter(both, axes, scatter_dimension=0, tiled=True))
    return big, shards


def per_device(
    tokens, doc_ids, w_qkv, w_out, w_up, w_down, biases, gains, b_up, pos_table, cotangent, *, sizes
):
    lines, planes = sizes
    row_count, local_length, width = tokens.shape
    seg_here = local_length // SEGLEN
    segments = doc_ids.shape[1]
    total = row_count * local_length
    own = row_count * seg_here

    seg_place = jnp.arange(segments)
    same_doc = doc_ids[:, :, None] == doc_ids[:, None, :]
    doc_start = jnp.min(jnp.where(same_doc, seg_place[None, None, :], segments), axis=2)

    def by_device(values):
        return values.reshape(row_count, planes, seg_here).transpose(1, 0, 2).reshape(-1, 1)

    place = by_device(seg_place[None, :] - doc_start)
    keys = by_device(doc_ids + segments * jnp.arange(row_count)[:, None])

    cot = cotangent.reshape(total, width)
    qkv, probs, n1, r1, slope, n2, r2, y, cls, xt, mixedt, firstt, hiddent = forward_block(
        tokens.reshape(total, width), w_qkv, w_out, w_up, w_down, biases, gains, b_up
    )
    (ccls, gcls, csums, cbsums, gpos, cxt, cmixedt, cfirstt, chiddent, cgqkv, cgbranch, cginner, cgsecond) = cross_block(
        cls, cot, place, keys, pos_table, w_qkv, w_out, w_up, w_down, biases, gains, b_up, planes
    )
    output, gsecond, ginner, gbranch, sums, bsums = early_backward(
        gcls, ccls, cot, y, n2, r2, slope, n1, r1, w_up, w_down, gains
    )
    cross_pairs = (cfirstt, cginner, chiddent, cgsecond, cmixedt, cgbranch, cxt, cgqkv)
    share = 1.0 / planes
    if (lines, planes) == (8, 4) and total == 2048 and width == 16 * PART:
        *grads, small, gx = late_backward(
            (firstt, ginner, hiddent, gsecond, mixedt, gbranch, xt), cross_pairs, (sums, bsums, csums, cbsums, gpos), (qkv, probs, w_qkv, w_out), share
        )
        gx, *grads = finish(gx, grads)
        small = small.reshape(-1)
        index = lax.axis_index("row") * planes + lax.axis_index("seg")
        shards, start = [], 0
        for size in (12 * width, 4 * width, 8 * width, segments * width):
            count = size // (lines * planes)
            shards.append(lax.dynamic_slice_in_dim(small, start + index * count, count, 0))
            start += size
    else:
        gqkv, gx = attention_back(qkv, probs, gbranch, w_qkv[0], w_out[0])
        bias_sums = jnp.stack([jnp.sum(gqkv[:, at : at + width].astype(F32), axis=0) for at in (0, 2 * width)])
        grads, shards = generic_total(
            (firstt, ginner, hiddent, gsecond, mixedt, gbranch, xt, gqkv), cross_pairs, (sums, bsums, csums, cbsums, gpos, bias_sums), planes, own
        )
    return (output.reshape(tokens.shape), gx.reshape(tokens.shape), *grads, *shards)


def solution(mesh):
    sizes = (mesh.shape["row"], mesh.shape["seg"])
    tokens_at = P("row", "seg", None)
    return jax.shard_map(
        functools.partial(per_device, sizes=sizes),
        mesh=mesh,
        in_specs=(tokens_at, P("row", None)) + (P(),) * 8 + (tokens_at,),
        out_specs=(tokens_at, tokens_at) + (P(("row", "seg"), None),) * 4 + (P(("row", "seg")),) * 4,
        check_vma=False,
    )
```

```python
import functools

import jax
import jax.numpy as jnp
from jax import lax
from jax.experimental import pallas as pl
from jax.experimental.pallas import tpu as pltpu
from jax.sharding import PartitionSpec as P


HDIM = 64
SEGLEN = 128
LANES = 128
GROUP = 2 * LANES
EPSILON = 1e-05
GELU_A = 0.7978845608028654
GELU_B = 0.044715 * GELU_A
F32, BF16 = jnp.float32, jnp.bfloat16


def mm(a, b):
    return lax.dot_general(a, b, (((1,), (0,)), ((), ())), preferred_element_type=F32)


def mm_nt(a, b):
    return lax.dot_general(a, b, (((1,), (1,)), ((), ())), preferred_element_type=F32)


def mm_tn(a, b):
    return lax.dot_general(a, b, (((0,), (0,)), ((), ())), preferred_element_type=F32)


def low_lanes(shape):
    return lax.broadcasted_iota(jnp.int32, shape, 1) < HDIM


def stack_heads(pair):
    keep = low_lanes(pair.shape)
    zero = jnp.zeros_like(pair)
    return jnp.concatenate([jnp.where(keep, pair, zero), jnp.where(keep, zero, pair)], axis=0)


def pair_lanes(half):
    return [slice(part * GROUP + half * LANES, part * GROUP + (half + 1) * LANES) for part in range(3)]


def norm_stats(values):
    centered = values - jnp.mean(values, axis=-1, keepdims=True)
    variance = jnp.mean(centered * centered, axis=-1, keepdims=True)
    rstd = lax.rsqrt(variance + EPSILON)
    return centered * rstd, rstd


def gelu_both(u):
    u = u.astype(BF16)
    square = u * u
    bend = GELU_B * square
    half = 0.5 * jnp.tanh(u * (GELU_A + bend))
    gate = half + 0.5
    hidden = u * gate
    slope = gate + hidden * (0.5 - half) * (2.0 * GELU_A + 6.0 * bend)
    return hidden, slope


def norm_back(grad, gain, normal, rstd):
    scaled = grad * gain
    a = jnp.mean(scaled, axis=-1, keepdims=True)
    b = jnp.mean(scaled * normal, axis=-1, keepdims=True)
    return (scaled - a - normal * b) * rstd


OUTS = 13
NEGATIVE = -1000000000.0
MESH = pl.DeviceIdType.MESH


def turned(values):
    return values.astype(F32).T.astype(BF16)


def cross_part(me, place_ref, keycol_ref, keyrow_ref, table_ref, bias_ref, gain_ref, bup_ref, outs, writes, weights, copies, scratch, ff_chunk):
    (
        ccls_ref, gcls_ref, sums_ref, bsums_ref, gpos_ref, xt_ref, mixedt_ref, firstt_ref, hiddent_ref,
        gqkv_ref, gbranch_ref, ginner_ref, gsecond_ref,
    ) = outs
    wqkv, wout, wup, wdown = weights
    qkv_ref, probs_ref, mixed_ref, slope_ref, whole_ref = scratch
    own, width = ccls_ref.shape
    rows = whole_ref.shape[1]
    inners = wup.shape[1]
    bias = bias_ref[1].astype(F32)
    gain = gain_ref[1].astype(F32)
    up_bias = bup_ref[1:2, :].astype(F32)
    onehot = (place_ref[...] == lax.broadcasted_iota(jnp.int32, (rows, table_ref.shape[0]), 1)).astype(F32)
    embed = mm(onehot.astype(BF16), table_ref[...])
    allowed = keycol_ref[...] == keyrow_ref[...]
    x = (whole_ref[0] + embed).astype(BF16)
    gy = whole_ref[1]
    xt_ref[...] = turned(x)
    copies[0].wait()
    for part in range(3):
        cols = slice(part * width, (part + 1) * width)
        out = mm(x, wqkv[:, cols])
        if part == 0:
            out = out + bias[0:1]
        if part == 2:
            out = out + bias[1:2]
        qkv_ref[:, cols] = out.astype(BF16)
    low = low_lanes((rows, LANES))
    pairs = range(width // LANES)
    lanes = [[slice(part * width + pair * LANES, part * width + (pair + 1) * LANES) for part in range(3)] for pair in pairs]
    scores = [
        jnp.where(allowed, mm_nt(qkv_ref[:, at[1]], stack_heads(qkv_ref[:, at[0]] * HDIM**-0.5)), NEGATIVE) for at in lanes
    ]
    pt = []
    for pair in pairs:
        e = jnp.exp(scores[pair] - jnp.max(scores[pair], axis=0, keepdims=True))
        p = e * (1.0 / jnp.sum(e, axis=0, keepdims=True))
        probs_ref[pair] = p
        pt.append(p.T.astype(BF16))
    for pair, at in enumerate(lanes):
        v = qkv_ref[:, at[2]]
        mixed_ref[:, at[0]] = jnp.where(low, mm(pt[pair][:rows], v), mm(pt[pair][rows:], v)).astype(BF16)
    copies[1].wait()
    mixed = mixed_ref[...]
    mixedt_ref[...] = turned(mixed)
    n1, r1 = norm_stats(x.astype(F32) + mm(mixed, wout[...]) + bias[2:3])
    first = (n1 * gain[0:1] + bias[3:4]).astype(BF16)
    firstt_ref[...] = turned(first)
    copies[2].wait()
    copies[3].wait()
    total = first.astype(F32) + bias[4:5]
    chunks = [slice(c * ff_chunk, (c + 1) * ff_chunk) for c in range(inners // ff_chunk)]
    inner = [mm(first, wup[:, cols]) for cols in chunks]
    for c, cols in enumerate(chunks):
        hidden, slope = gelu_both(inner[c] + up_bias[:, cols])
        hidden = hidden.astype(BF16)
        hiddent_ref[cols, :] = turned(hidden)
        slope_ref[:, cols] = slope.astype(F32)
        total = total + mm(hidden, wdown[cols, :])
    n2, r2 = norm_stats(total)
    mine = pl.ds(pl.multiple_of(me * own, own), own)
    whole_ref[0] = (n2 * gain[1:2] + bias[5:6]).astype(BF16).astype(F32)
    ccls_ref[...] = whole_ref[0, mine, :]
    for i in (0, 5, 6, 7, 8):
        writes[i].start()

    def row_sum(values):
        return jnp.sum(values.astype(F32), axis=0, keepdims=True)

    sums_ref[0:1, :] = row_sum(gy * n2)
    sums_ref[1:2, :] = row_sum(gy)
    g_two = norm_back(gy, gain[1:2], n2, r2)
    g_second = g_two.astype(BF16)
    gsecond_ref[...] = g_second
    sums_ref[2:3, :] = row_sum(g_second)
    g_first = g_two
    g_hidden = [mm_nt(g_second, wdown[cols, :]) for cols in chunks]
    for c, cols in enumerate(chunks):
        g_inner = (g_hidden[c] * slope_ref[:, cols]).astype(BF16)
        ginner_ref[:, cols] = g_inner
        bsums_ref[:, cols] = row_sum(g_inner)
        g_first = g_first + mm_nt(g_inner, wup[:, cols])
    sums_ref[3:4, :] = row_sum(g_first * n1)
    sums_ref[4:5, :] = row_sum(g_first)
    g_one = norm_back(g_first, gain[0:1], n1, r1)
    g_branch = g_one.astype(BF16)
    gbranch_ref[...] = g_branch
    sums_ref[5:6, :] = row_sum(g_branch)
    for i in (10, 11, 12):
        writes[i].start()
    g_mixed = mm_nt(g_branch, wout[...]).astype(BF16)
    g_out = [stack_heads(g_mixed[:, at[0]]) for at in lanes]
    g_p = [mm_nt(qkv_ref[:, at[2]], g_out[pair]) for pair, at in enumerate(lanes)]
    g_s, g_st = [], []
    for pair in pairs:
        p = probs_ref[pair]
        g = p * (g_p[pair] - jnp.sum(g_p[pair] * p, axis=0, keepdims=True))
        g_s.append(g.astype(BF16))
        g_st.append(g.T.astype(BF16))
    for pair, at in enumerate(lanes):
        q, k, _ = (qkv_ref[:, part] for part in at)
        g_q = jnp.where(low, mm(g_st[pair][:rows], k), mm(g_st[pair][rows:], k)) * HDIM**-0.5
        gqkv_ref[:, at[0]] = g_q.astype(BF16)
        gqkv_ref[:, at[1]] = mm(g_s[pair], stack_heads(q * HDIM**-0.5)).astype(BF16)
        gqkv_ref[:, at[2]] = mm(probs_ref[pair].astype(BF16), g_out[pair]).astype(BF16)
    g_qkv = gqkv_ref[...]
    sums_ref[6:7, :] = row_sum(g_qkv[:, :width])
    sums_ref[7:8, :] = row_sum(g_qkv[:, 2 * width :])
    g_x = g_one + mm_nt(g_qkv, wqkv[...])
    whole_ref[1] = g_x
    gcls_ref[...] = whole_ref[1, mine, :]
    gpos_ref[...] = lax.dot_general(onehot, g_x, (((0,), (0,)), ((), ())), preferred_element_type=F32, precision=lax.Precision.HIGHEST)
    for i in (1, 2, 3, 4, 9):
        writes[i].start()
    for write in writes:
        write.wait()


def forward_kernel(
    x_ref, wqkv_hbm, wout_hbm, wup_hbm, wdown_hbm, cot_hbm, bias_ref, gain_ref, bup_ref, place_ref, keycol_ref, keyrow_ref, table_ref,
    qkv_ref, probs_ref, n1_ref, r1_ref, slope_ref, n2_ref, r2_ref, y_ref, xt_ref, mixedt_ref, firstt_ref, hiddent_ref,
    *refs, ff_chunk, devices,
):
    homes, outs, refs = refs[:OUTS], refs[OUTS : 2 * OUTS], refs[2 * OUTS :]
    wqkv, wout, wup, wdown, mixed_ref, first_ref, sems, cls_ref, cot_rows, cot_low, packed, gathered = refs[:12]
    cross_weights, cross_scratch = refs[12:16], refs[16:21]
    cross_sems, out_sems, cot_sems, send_sems, recv_sems = refs[21:]
    step = pl.program_id(0)
    last = pl.num_programs(0) - 1
    copies = [
        pltpu.make_async_copy(src.at[0], dst, sems.at[i])
        for i, (src, dst) in enumerate(
            ((wqkv_hbm, wqkv), (wout_hbm, wout), (wup_hbm, wup), (wdown_hbm, wdown))
        )
    ]

    own = cls_ref.shape[0]
    line, me = lax.axis_index("row"), lax.axis_index("seg")
    peers = [(line, lax.rem(me + hop, devices)) for hop in range(1, devices)]
    cot_copies = [
        pltpu.make_async_copy(cot_hbm.at[pl.ds(i * SEGLEN, 16)], cot_rows.at[i], cot_sems.at[i]) for i in range(own)
    ]
    cross_copies = [
        pltpu.make_async_copy(src.at[1], dst, cross_sems.at[i])
        for i, (src, dst) in enumerate(zip((wqkv_hbm, wout_hbm, wup_hbm, wdown_hbm), cross_weights))
    ]
    writes = [pltpu.make_async_copy(src, dst, out_sems.at[i]) for i, (src, dst) in enumerate(zip(outs, homes))]
    barrier = pltpu.get_barrier_semaphore()

    def sends(kind):
        return [
            pltpu.make_async_remote_copy(
                src_ref=packed.at[kind], dst_ref=gathered.at[kind, hop + 1], send_sem=send_sems.at[kind, hop],
                recv_sem=recv_sems.at[kind, hop], device_id=peer, device_id_type=MESH,
            )
            for hop, peer in enumerate(peers)
        ]

    def arrived(kind, whole_ref):
        for send in sends(kind):
            send.wait()
        gathered[kind, 0] = packed[kind]
        for hop in range(devices):
            rows_at = pl.ds(pl.multiple_of(lax.rem(me - hop + devices, devices) * own, own), own)
            whole_ref[1 - kind, rows_at, :] = gathered[kind, hop].astype(F32)

    @pl.when(step == 0)
    def _():
        for peer in peers:
            pl.semaphore_signal(barrier, inc=1, device_id=peer, device_id_type=MESH)
        for copy in copies:
            copy.start()
        copies[0].wait()
        copies[1].wait()

    @pl.when(step == 1)
    def _():
        copies[2].wait()
        copies[3].wait()
        for copy in cot_copies + cross_copies:
            copy.start()

    @pl.when(step == 2)
    def _():
        for i, copy in enumerate(cot_copies):
            copy.wait()
            cot_low[i : i + 1, :] = cot_rows[i, 0:8, :].astype(F32)[0:1]
        packed[0] = cot_low[...].astype(BF16)
        pl.semaphore_wait(barrier, devices - 1)
        for send in sends(0):
            send.start()

    rows, width = x_ref.shape
    bias = bias_ref[0].astype(F32)
    gain = gain_ref[0].astype(F32)
    up_bias = bup_ref[0:1, :].astype(F32)
    inners = wup.shape[1]
    chunks = [slice(c * ff_chunk, (c + 1) * ff_chunk) for c in range(inners // ff_chunk)]
    items = [(seg, pair) for seg in range(rows // SEGLEN) for pair in range(width // LANES)]
    every = range(len(items))
    at = [slice(seg * SEGLEN, (seg + 1) * SEGLEN) for seg, _ in items]

    def front(state):
        def project_part(part):
            x = x_ref[...]
            out = mm(x, wqkv[:, part * width : (part + 1) * width])
            if part == 0:
                out = out + bias[0:1]
            if part == 2:
                out = out + bias[1:2]
            out = out.astype(BF16)
            for group in range(width // GROUP):
                qkv_ref[group, :, part * GROUP : (part + 1) * GROUP] = out[:, group * GROUP : (group + 1) * GROUP]

        def piece(e, part):
            pair = items[e][1]
            return qkv_ref[pair // 2, at[e], pair_lanes(pair % 2)[part]]

        def scores():
            xt_ref[...] = x_ref[...].T
            state["scores"] = [mm_nt(piece(e, 1), stack_heads(piece(e, 0) * HDIM**-0.5)) for e in every]

        def softmax(part):
            for e in every[part :: 2]:
                score = state["scores"][e]
                ex = jnp.exp(score - jnp.max(score, axis=0, keepdims=True))
                p = (ex * (1.0 / jnp.sum(ex, axis=0, keepdims=True))).astype(BF16)
                probs_ref[items[e][0], items[e][1]] = p
                state[e] = jnp.concatenate([p[:, :SEGLEN].T, p[:, SEGLEN:].T], axis=1)

        def mix():
            for e, (_, pair) in enumerate(items):
                mixed_ref[at[e], pair * LANES : (pair + 1) * LANES] = mm(state[e], stack_heads(piece(e, 2))).astype(BF16)

        def project_out():
            mixed = mixed_ref[...]
            mixedt_ref[...] = mixed.T
            state["resid"] = x_ref[...].astype(F32) + mm(mixed, wout[...]) + bias[2:3]

        def norm():
            n1, r1 = norm_stats(state["resid"])
            n1_ref[...] = n1.astype(BF16)
            r1_ref[...] = jnp.broadcast_to(r1, r1_ref.shape)
            first = (n1 * gain[0:1] + bias[3:4]).astype(BF16)
            firstt_ref[...] = first.T
            state["first"] = first

        return [lambda part=part: project_part(part) for part in range(3)] + [scores, lambda: softmax(0), lambda: softmax(1), mix, project_out, norm]

    def back(state):
        first = first_ref[...]
        state["total"] = first.astype(F32) + bias[4:5]

        def up(c):
            state["inner", c] = mm(first, wup[:, chunks[c]])

        def gelu(c):
            cols = chunks[c]
            hidden, slope = gelu_both(state["inner", c] + up_bias[:, cols])
            hidden = hidden.astype(BF16)
            hiddent_ref[cols, :] = hidden.T
            slope_ref[:, cols] = slope.astype(BF16)
            state["hidden", c] = hidden

        def down(c):
            state["total"] = state["total"] + mm(state["hidden", c], wdown[chunks[c], :])

        def norm():
            n2, r2 = norm_stats(state["total"])
            n2_ref[...] = n2.astype(BF16)
            r2_ref[...] = jnp.broadcast_to(r2, r2_ref.shape)
            y = (n2 * gain[1:2] + bias[5:6]).astype(BF16)
            y_ref[...] = y
            segs = rows // SEGLEN
            for seg in range(segs):
                cls_ref[pl.ds((step - 1) * segs + seg, 1), :] = y[seg * SEGLEN : seg * SEGLEN + 8].astype(F32)[0:1]

        pieces = [lambda: up(0)]
        for c in range(len(chunks)):
            if c + 1 < len(chunks):
                pieces.append(lambda c=c: up(c + 1))
            pieces += [lambda c=c: gelu(c), lambda c=c: down(c)]
        return pieces + [norm]

    def run(with_front, with_back):
        state = {}
        lists = ([back(state)] if with_back else []) + ([front(state)] if with_front else [])
        turns = sorted((((i + 0.5) / len(pieces), k, i) for k, pieces in enumerate(lists) for i in range(len(pieces))))
        for _, k, i in turns:
            lists[k][i]()
        if with_front:
            first_ref[...] = state["first"]

    @pl.when(step == 0)
    def _():
        run(True, False)

    @pl.when((step > 0) & (step < last))
    def _():
        run(True, True)

    @pl.when(step == last)
    def _():
        run(False, True)
        packed[1] = cls_ref[...].astype(BF16)
        for send in sends(1):
            send.start()
        arrived(0, cross_scratch[-1])
        arrived(1, cross_scratch[-1])
        cross_part(
            me, place_ref, keycol_ref, keyrow_ref, table_ref, bias_ref, gain_ref, bup_ref, outs, writes,
            cross_weights, cross_copies, cross_scratch, ff_chunk,
        )


def forward_blocks(x, cot, w_qkv, w_out, w_up, w_down, bias, gain, bup, place, keys, table, devices, tile=256, ff_chunk=768):
    total, width = x.shape
    inners = w_up.shape[-1]
    segs = tile // SEGLEN
    pairs = width // LANES
    any_spec = pl.BlockSpec(memory_space=pl.ANY)

    steps = total // tile

    def rows_of(cols, late):
        return pl.BlockSpec((tile, cols), lambda i: (jnp.maximum(i - 1, 0) if late else jnp.minimum(i, steps - 1), 0))

    def whole(a):
        return pl.BlockSpec(a.shape, lambda i: (0,) * a.ndim)

    def cols_of(rows, late):
        return pl.BlockSpec((rows, tile), lambda i: (0, jnp.maximum(i - 1, 0) if late else jnp.minimum(i, steps - 1)))

    outs = [
        ((width // GROUP, total, 3 * GROUP), BF16, pl.BlockSpec((width // GROUP, tile, 3 * GROUP), lambda i: (0, jnp.minimum(i, steps - 1), 0))),
        ((total // SEGLEN, pairs, SEGLEN, 2 * SEGLEN), BF16, pl.BlockSpec((segs, pairs, SEGLEN, 2 * SEGLEN), lambda i: (jnp.minimum(i, steps - 1), 0, 0, 0))),
        ((total, width), BF16, rows_of(width, False)),
        ((total, LANES), F32, rows_of(LANES, False)),
        ((total, inners), BF16, rows_of(inners, True)),
        ((total, width), BF16, rows_of(width, True)),
        ((total, LANES), F32, rows_of(LANES, True)),
        ((total, width), BF16, rows_of(width, True)),
        ((width, total), BF16, cols_of(width, False)),
        ((width, total), BF16, cols_of(width, False)),
        ((width, total), BF16, cols_of(width, False)),
        ((inners, total), BF16, cols_of(inners, True)),
    ]
    own = total // SEGLEN
    rows = own * devices
    cross_outs = [
        ((own, width), F32), ((own, width), F32), ((8, width), F32), ((1, inners), F32), (table.shape, F32),
        ((width, rows), BF16), ((width, rows), BF16), ((width, rows), BF16), ((inners, rows), BF16),
        ((rows, 3 * width), BF16), ((rows, width), BF16), ((rows, inners), BF16), ((rows, width), BF16),
    ]
    keyrow = jnp.tile(keys.reshape(1, rows), (1, 2))
    dma = pltpu.SemaphoreType.DMA
    return pl.pallas_call(
        functools.partial(forward_kernel, ff_chunk=ff_chunk, devices=devices),
        grid=(steps + 1,),
        in_specs=[rows_of(width, False), any_spec, any_spec, any_spec, any_spec, any_spec]
        + [whole(a) for a in (bias, gain, bup, place, keys, keyrow, table)],
        out_specs=[o[2] for o in outs] + [pl.BlockSpec(memory_space=pltpu.HBM)] * OUTS,
        out_shape=[jax.ShapeDtypeStruct(o[0], o[1]) for o in outs + cross_outs],
        scratch_shapes=[pltpu.VMEM(*o) for o in cross_outs]
        + [
            pltpu.VMEM(w_qkv.shape[1:], BF16),
            pltpu.VMEM(w_out.shape[1:], BF16),
            pltpu.VMEM(w_up.shape[1:], BF16),
            pltpu.VMEM(w_down.shape[1:], BF16),
            pltpu.VMEM((tile, width), BF16),
            pltpu.VMEM((tile, width), BF16),
            dma((4,)),
            pltpu.VMEM((own, width), F32),
            pltpu.VMEM((own, 16, width), BF16),
            pltpu.VMEM((own, width), F32),
            pltpu.VMEM((2, own, width), BF16),
            pltpu.VMEM((2, devices, own, width), BF16),
            pltpu.VMEM(w_qkv.shape[1:], BF16),
            pltpu.VMEM(w_out.shape[1:], BF16),
            pltpu.VMEM(w_up.shape[1:], BF16),
            pltpu.VMEM(w_down.shape[1:], BF16),
            pltpu.VMEM((rows, 3 * width), BF16),
            pltpu.VMEM((pairs, rows, 2 * rows), F32),
            pltpu.VMEM((rows, width), BF16),
            pltpu.VMEM((rows, inners), F32),
            pltpu.VMEM((2, rows, width), F32),
            dma((4,)), dma((OUTS,)), dma((own,)), dma((2, devices - 1)), dma((2, devices - 1)),
        ],
        compiler_params=pltpu.CompilerParams(vmem_limit_bytes=63 * 2**20, collective_id=0, has_side_effects=True),
        name="forward_blocks",
    )(x, w_qkv, w_out, w_up, w_down, cot, bias, gain, bup, place, keys, keyrow, table)

def fold_rows(values):
    rows, cols = values.shape
    return jnp.sum(values.reshape(rows // 8, 8, cols), axis=0)


def early_kernel(
    gcls_ref, ccls_ref, cot_ref, y_ref, n2_ref, r2_ref, slope_ref, n1_ref, r1_ref, wup_hbm, wdown_hbm, gain_ref,
    out_ref, gsecond_ref, ginner_ref, gbranch_ref, sums_ref, bsums_ref, wup, wdown, two_ref, sems, *, ff_chunk,
):
    step = pl.program_id(0)
    last = pl.num_programs(0) - 1
    copies = [
        pltpu.make_async_copy(src.at[0], dst, sems.at[i]) for i, (src, dst) in enumerate(((wdown_hbm, wdown), (wup_hbm, wup)))
    ]

    @pl.when(step == 0)
    def _():
        for copy in copies:
            copy.start()
        sums_ref[...] = jnp.zeros_like(sums_ref)
        bsums_ref[...] = jnp.zeros_like(bsums_ref)

    @pl.when(step == 1)
    def _():
        for copy in copies:
            copy.wait()

    rows, width = cot_ref.shape
    segs = rows // SEGLEN
    inners = wup.shape[1]
    gain = gain_ref[0].astype(F32)
    chunks = [slice(c * ff_chunk, (c + 1) * ff_chunk) for c in range(inners // ff_chunk)]

    def front(state):
        def gradient():
            place = lax.broadcasted_iota(jnp.int32, (rows, width), 0)
            gy = cot_ref[...].astype(F32)
            y = y_ref[...].astype(F32)
            for seg in range(segs):
                at = pl.ds(step * segs + seg, 1)
                gy = jnp.where(place == seg * SEGLEN, gcls_ref[at, :], gy)
                y = jnp.where(place == seg * SEGLEN, ccls_ref[at, :], y)
            out_ref[...] = y.astype(BF16)
            state["gy"] = gy

        def norm():
            gy = state["gy"]
            n2 = n2_ref[...].astype(F32)
            sums_ref[0] += fold_rows(gy * n2)
            sums_ref[1] += fold_rows(gy)
            state["two"] = norm_back(gy, gain[1:2], n2, r2_ref[:, 0:1])

        def store():
            low = state["two"].astype(BF16)
            gsecond_ref[...] = low
            sums_ref[2] += fold_rows(low.astype(F32))

        return [gradient, norm, store]

    def back(state):
        g_two = two_ref[...]
        g_second = g_two.astype(BF16)
        state["first"] = g_two

        def down(c):
            state["hidden", c] = mm_nt(g_second, wdown[chunks[c], :])

        def slope(c):
            cols = chunks[c]
            g_low = state["hidden", c].astype(BF16) * slope_ref[:, cols]
            ginner_ref[:, cols] = g_low
            bsums_ref[:, cols] += fold_rows(g_low.astype(F32))
            state["inner", c] = g_low

        def up(c):
            state["first"] = state["first"] + mm_nt(state["inner", c], wup[:, chunks[c]])

        def norm():
            g_first = state["first"]
            n1 = n1_ref[...].astype(F32)
            sums_ref[3] += fold_rows(g_first * n1)
            sums_ref[4] += fold_rows(g_first)
            g_branch = norm_back(g_first, gain[0:1], n1, r1_ref[:, 0:1]).astype(BF16)
            gbranch_ref[...] = g_branch
            sums_ref[5] += fold_rows(g_branch.astype(F32))

        pieces = [lambda: down(0)]
        for c in range(len(chunks)):
            if c + 1 < len(chunks):
                pieces.append(lambda c=c: down(c + 1))
            pieces += [lambda c=c: slope(c), lambda c=c: up(c)]
        return pieces + [norm]

    def run(with_front, with_back):
        state = {}
        lists = ([back(state)] if with_back else []) + ([front(state)] if with_front else [])
        turns = sorted((((i + 0.5) / len(pieces), k, i) for k, pieces in enumerate(lists) for i in range(len(pieces))))
        for _, k, i in turns:
            lists[k][i]()
        if with_front:
            two_ref[...] = state["two"]

    @pl.when(step == 0)
    def _():
        run(True, False)

    @pl.when((step > 0) & (step < last))
    def _():
        run(True, True)

    @pl.when(step == last)
    def _():
        run(False, True)


def early_backward(gcls, ccls, cot, y, n2, r2, slope, n1, r1, w_up, w_down, gains, tile=256, ff_chunk=768):
    total, width = cot.shape
    inners = w_up.shape[-1]
    any_spec = pl.BlockSpec(memory_space=pl.ANY)

    steps = total // tile

    def rows_of(cols, late=False):
        return pl.BlockSpec((tile, cols), lambda i: (jnp.maximum(i - 1, 0) if late else jnp.minimum(i, steps - 1), 0))

    def whole(a):
        return pl.BlockSpec(a.shape, lambda i: (0,) * len(a.shape))

    outs = [
        ((total, width), BF16, rows_of(width)),
        ((total, width), BF16, rows_of(width)),
        ((total, inners), BF16, rows_of(inners, True)),
        ((total, width), BF16, rows_of(width, True)),
        ((6, 8, width), F32, pl.BlockSpec((6, 8, width), lambda i: (0, 0, 0))),
        ((8, inners), F32, pl.BlockSpec((8, inners), lambda i: (0, 0))),
    ]
    return pl.pallas_call(
        functools.partial(early_kernel, ff_chunk=ff_chunk),
        grid=(steps + 1,),
        in_specs=[whole(gcls), whole(ccls), rows_of(width), rows_of(width), rows_of(width), rows_of(LANES), rows_of(inners, True),
                  rows_of(width, True), rows_of(LANES, True), any_spec, any_spec, whole(gains)],
        out_specs=[o[2] for o in outs],
        out_shape=[jax.ShapeDtypeStruct(o[0], o[1]) for o in outs],
        scratch_shapes=[pltpu.VMEM(w_up.shape[1:], BF16), pltpu.VMEM(w_down.shape[1:], BF16), pltpu.VMEM((tile, width), F32), pltpu.SemaphoreType.DMA((2,))],
        compiler_params=pltpu.CompilerParams(vmem_limit_bytes=60 * 2**20),
        name="early_backward",
    )(gcls, ccls, cot, y, n2, r2, slope, n1, r1, w_up, w_down, gains)

RING = 4
CROSS_UNITS = 3
SEG_UNITS = 12
UNITS = CROSS_UNITS + SEG_UNITS
CHAINS = UNITS + 1
PART = 48
GROUPS = 3
EARLY = 9
TILES = 4
GROUP_STEPS = TILES + 1
LAST_AT = EARLY + GROUPS * GROUP_STEPS
STEPS = LAST_AT + TILES


PAIR_MOMENTS = [(4, 6, 8, 13), (6, 8, 11, 16), (8, 11, 14, 19), (11, 14, 17, 21), (14, 17, 20, 24), (17, 20, 23, 26)]
LATE_MOMENTS = [(14, 18, 21, 23, 26), (19, 23, 25, 27, STEPS), (24, STEPS, STEPS, STEPS, STEPS), (STEPS,) * 5]
SMALL_MOMENTS = (1, 4, 6, 8, 10, 12)
SMALL_LATE = (24, 25, 26, STEPS, STEPS, STEPS)


def comm_schedule():
    table = {s: [] for s in range(STEPS + 1)}
    for pair, moments in enumerate(PAIR_MOMENTS):
        for n in (2 * pair, 2 * pair + 1):
            for action, at in zip(("two", "three", "final", "out"), moments):
                table[at].append((action, n))
            if n + 4 < CROSS_UNITS + EARLY:
                table[moments[0]].append(("send", n + 4))
    first = CROSS_UNITS + EARLY
    table[EARLY + 1].append(("one", first - 1))
    for n, moments in enumerate(LATE_MOMENTS, first):
        for action, at in zip(("one", "two", "three", "final", "out"), moments):
            if action != "one" or n < UNITS:
                table[at].append((action, n))
    for d in range(6):
        table[SMALL_MOMENTS[d]].append(("small", d))
        table[SMALL_LATE[d]].append(("late", d))
    order = ("small", "late", "one", "out", "final", "three", "two", "send")
    for at in range(STEPS):
        table[at].sort(key=lambda item: (order.index(item[0]), item[1]))
    rank = {"late": 0, "two": 1, "three": 2, "final": 3, "out": 4}
    table[STEPS].sort(key=lambda item: (rank[item[0]] if item[0] != "late" else item[1] - 2.5, item[1]))
    return table


def add_low(a, b):
    return (a.astype(F32) + b.astype(F32)).astype(BF16)


def late_kernel(
    firstt, ginner, hiddent, gsecond, mixedt, gbranch, xt, qkv, probs, wqkv_hbm, wout_hbm,
    cfirstt, cginner, chiddent, cgsecond, cmixedt, cgbranch, cxt, cgqkv,
    sums, bsums, csums, cbsums, gpos,
    dqkv_ref, dout_ref, dup_ref, ddown_ref, small_ref, gx_ref,
    aslot, bslot, qkv_slot, probs_slot, gbranch_slot, gx_slot, wqkv, wout, fold, csend, crecv, keep, r1, r2, r3, rf, acc, racc, late_acc, late_racc,
    load_sems, tile_sems, store_sems, weight_sems, csend_sems, crecv_sems, s1_sems, q1_sems, s2_sems, q2_sems, s3_sems, q3_sems, sf_sems, qf_sems, sa_sems, qa_sems,
    *, share,
):
    width = bslot.shape[-1]
    line, z = lax.axis_index("row"), lax.axis_index("seg")
    y, x, c = line // 4, (line // 2) % 2, line % 2
    zh, zl = z // 2, z % 2
    flip_c = (y * 4 + x * 2 + 1 - c, z)
    flip_x = (y * 4 + (1 - x) * 2 + c, z)
    flip_y = ((1 - y) * 4 + x * 2 + c, z)
    flip_zl = (line, zh * 2 + 1 - zl)
    flip_zh = (line, (1 - zh) * 2 + zl)
    flip_yzh = ((1 - y) * 4 + x * 2 + c, (1 - zh) * 2 + zl)
    barrier = pltpu.get_barrier_semaphore()
    for peer in (flip_c, flip_x, flip_y, flip_zl, flip_zh, flip_yzh):
        pl.semaphore_signal(barrier, inc=1, device_id=peer, device_id_type=MESH)

    tile = gbranch_slot.shape[1]
    segs = tile // SEGLEN

    def a_slot(u):
        return jnp.where((u < 4) | (u >= EARLY), 0, (u + 1) % 2)

    def b_slot(u):
        return jnp.where(u < 4, u % 2, jnp.where(u < EARLY, u // 8, u - EARLY))

    def load_unit(u, do):
        def act(src, dst, side):
            getattr(pltpu.make_async_copy(src, dst, load_sems.at[side]), do)()

        def columns(ref, j):
            return ref.at[:, pl.ds(pl.multiple_of(j * width, width), width)]

        @pl.when(u == 0)
        def _():
            act(firstt, aslot.at[0], 0)

        @pl.when(u < 4)
        def _():
            act(columns(ginner, u), bslot.at[u % 2], 1)

        @pl.when((u >= 4) & (u < 8))
        def _():
            act(hiddent.at[:, :, :, u - 4], aslot.at[(u + 1) % 2], 0)

        @pl.when(u == 4)
        def _():
            act(gsecond, bslot.at[0], 1)

        @pl.when(u == 8)
        def _():
            act(mixedt, aslot.at[1], 0)
            act(gbranch, bslot.at[1], 1)

        @pl.when(u == EARLY)
        def _():
            act(xt, aslot.at[0], 0)

    def tile_rows(i):
        return pl.ds(pl.multiple_of(i * tile, tile), tile)

    def load_tile(j, i, slot, late, do):
        copies = [pltpu.make_async_copy(gbranch.at[tile_rows(i)], gbranch_slot.at[slot], tile_sems.at[slot, 0])]
        if not late:
            copies.append(pltpu.make_async_copy(qkv.at[j, tile_rows(i)], qkv_slot.at[slot], tile_sems.at[slot, 1]))
            copies.append(
                pltpu.make_async_copy(probs.at[pl.ds(i * segs, segs), pl.ds(2 * j, 2)], probs_slot.at[slot], tile_sems.at[slot, 2])
            )
        for copy in copies:
            getattr(copy, do)()

    def place(s):
        group = (s - EARLY) // GROUP_STEPS
        return group, (s - EARLY) % GROUP_STEPS

    def load(s, do):
        group, part = place(s)
        inside = (s >= EARLY) & (s < LAST_AT)

        @pl.when(s < EARLY)
        def _():
            load_unit(s, do)

        @pl.when(inside & (part < TILES))
        def _():
            load_tile(group, part, part % 2, False, do)

        @pl.when(inside & (part == TILES))
        def _():
            load_unit(EARLY + group, do)

        @pl.when(s >= LAST_AT)
        def _():
            load_tile(0, s - LAST_AT, (s - LAST_AT) % 2, True, do)

    def store_gx(i):
        return pltpu.make_async_copy(gx_slot.at[i % 2], gx_ref.at[tile_rows(i)], store_sems.at[i % 2])

    weight_copies = [pltpu.make_async_copy(wout_hbm.at[0], wout, weight_sems.at[0])]
    for j in range(GROUPS):
        for part in range(3):
            weight_copies.append(
                pltpu.make_async_copy(
                    wqkv_hbm.at[0, :, pl.ds(part * width + j * GROUP, GROUP)],
                    wqkv.at[j, :, pl.ds(part * GROUP, GROUP)],
                    weight_sems.at[1 + 3 * j + part],
                )
            )
    load(0, "start")

    def remote(src, dst, send_sem, recv_sem, peer):
        return pltpu.make_async_remote_copy(
            src_ref=src, dst_ref=dst, send_sem=send_sem, recv_sem=recv_sem, device_id=peer, device_id_type=MESH
        )

    def choose(t, a, b):
        return t * a + (1 - t) * b

    def pick(t, a, b):
        return tuple(choose(t, p, q) for p, q in zip(a, b))

    def way(t):
        bits = (choose(t, x, y), choose(t, zl, x), choose(t, zh, zl))
        peers = (pick(t, flip_x, flip_y), pick(t, flip_zl, flip_x), pick(t, flip_zh, flip_zl))
        return bits, peers

    def core_copy(n):
        slot = n % RING
        return remote(csend.at[slot], crecv.at[slot], csend_sems.at[slot], crecv_sems.at[slot], flip_c)

    def part_of(n):
        if isinstance(n, int) and n >= UNITS - 1:
            half = width // 2
            return UNITS - 1, slice((n - UNITS + 1) * half, (n - UNITS + 2) * half)
        return n, slice(0, width)

    def copy_one(n, t):
        (b1, _, _), (peer, _, _) = way(t)
        m, cols = part_of(n)
        return remote(keep.at[m, pl.ds(4 * (1 - b1), 4), :, cols], r1.at[m, :, :, cols], s1_sems.at[n], q1_sems.at[n], peer)

    def copy_two(n, t):
        (b1, b2, _), (_, peer, _) = way(t)
        m, cols = part_of(n)
        return remote(keep.at[m, pl.ds(4 * b1 + 2 * (1 - b2), 2), :, cols], r2.at[m, :, :, cols], s2_sems.at[n], q2_sems.at[n], peer)

    def copy_three(n, t):
        (b1, b2, b3), (_, _, peer) = way(t)
        m, cols = part_of(n)
        return remote(keep.at[m, 4 * b1 + 2 * b2 + 1 - b3, :, cols], r3.at[m, :, cols], s3_sems.at[n], q3_sems.at[n], peer)

    def own_block(n, t):
        (b1, b2, b3), _ = way(t)
        m, cols = part_of(n)
        return keep.at[m, 4 * b1 + 2 * b2 + b3, :, cols]

    def step_one(n, t):
        core_copy(n).wait_recv()
        keep[n] = add_low(keep[n], crecv[n % RING])

        @pl.when((n < 4) | (n >= CROSS_UNITS + EARLY))
        def _():
            copy_one(n, t).start()

        if isinstance(n, int) and n == UNITS - 1:
            copy_one(n + 1, 1).start()

    def step_two(n, t):
        (b1, _, _), _ = way(t)
        copy_one(n, t).wait()
        m, cols = part_of(n)
        at = pl.ds(4 * b1, 4)
        keep[m, at, :, cols] = add_low(keep[m, at, :, cols], r1[m, :, :, cols])
        copy_two(n, t).start()

    def step_three(n, t):
        (b1, b2, _), _ = way(t)
        copy_two(n, t).wait()
        m, cols = part_of(n)
        at = pl.ds(4 * b1 + 2 * b2, 2)
        keep[m, at, :, cols] = add_low(keep[m, at, :, cols], r2[m, :, :, cols])
        copy_three(n, t).start()

    def final_to(n, t, slot, peer):
        m, cols = part_of(n)
        return remote(own_block(n, t), rf.at[m, slot, :, cols], sf_sems.at[n], qf_sems.at[n, slot], peer)

    def sends_final(n, t, act):
        straight = (y == 1) & ((t == 1) | (zh == 1))

        @pl.when(straight)
        def _():
            act(final_to(n, t, 0, flip_y))

        @pl.when((t == 0) & (y == 0) & (zh == 1))
        def _():
            act(final_to(n, t, 0, flip_zh))

        @pl.when((t == 0) & (y == 1) & (zh == 0))
        def _():
            act(final_to(n, t, 1, flip_yzh))

    def step_final(n, t):
        copy_three(n, t).wait()
        (b1, b2, b3), _ = way(t)
        m, cols = part_of(n)
        at = 4 * b1 + 2 * b2 + b3
        keep[m, at, :, cols] = add_low(keep[m, at, :, cols], r3[m, :, cols])
        sends_final(n, t, lambda copy: copy.start())

    def put(u, value, cols=slice(0, 16 * PART)):
        def columns(j):
            return pl.ds(pl.multiple_of(j * width, width), width)

        @pl.when(u < 4)
        def _():
            dup_ref[:, columns(u)] = value

        @pl.when((u >= 4) & (u < 8))
        def _():
            ddown_ref[pl.ds(pl.multiple_of((u - 4) * PART, PART), PART), :] = value

        @pl.when(u == 8)
        def _():
            dout_ref[...] = value

        for j in range(GROUPS):
            @pl.when(u == EARLY + j)
            def _(j=j):
                for part in range(3):
                    first, last = max(part * GROUP, cols.start), min((part + 1) * GROUP, cols.stop)
                    if first < last:
                        to = part * (width - GROUP) + j * GROUP
                        dqkv_ref[:, to + first : to + last] = value[:, first - cols.start : last - cols.start]

    def step_out(n, t, u):
        m, cols = part_of(n)
        sends_final(n, t, lambda copy: copy.wait_send())

        @pl.when(y == 0)
        def _():
            final_to(n, t, 0, flip_y).wait_recv()

            @pl.when((t == 1) | (zh == 0))
            def _():
                put(u, own_block(n, t)[...].astype(F32) + rf[m, 0, :, cols].astype(F32), cols)

            @pl.when((t == 0) & (zh == 1))
            def _():
                final_to(n, t, 1, flip_y).wait_recv()
                put(u, rf[m, 0, :, cols].astype(F32) + rf[m, 1, :, cols].astype(F32), cols)

    def cross_final(n):
        return remote(keep.at[n, pl.ds(2 * x, 2)], rf.at[n], sf_sems.at[n], qf_sems.at[n, 0], flip_y)

    def cross_step_final(n):
        copy_two(n, 0).wait()
        at = pl.ds(4 * y + 2 * x, 2)
        keep[n, at] = add_low(keep[n, at], r2[n])

        @pl.when(y == 0)
        def _():
            cross_final(n).start()

    def cross_step_out(n, index):
        @pl.when(y == 0)
        def _():
            cross_final(n).wait_send()

        @pl.when(y == 1)
        def _():
            cross_final(n).wait_recv()
            for sub in range(4):
                block = rf[n, sub] if sub < 2 else keep[n, 4 + 2 * x + sub - 2]
                put(4 * index + sub, block.astype(F32))

    small_peers = (flip_c, flip_x, flip_y, flip_zl, flip_zh)

    rounds = ((acc, racc), (late_acc, late_racc))

    def small_copy(late, d):
        own, other = rounds[late]
        return remote(own.at[d], other.at[d], sa_sems.at[late, d], qa_sems.at[late, d], small_peers[d])

    def small_step(late, d):
        own, other = rounds[late]
        small_copy(late, d).wait()
        own[d + 1] = own[d] + other[d]
        if d + 1 < len(small_peers):
            small_copy(late, d + 1).start()
        elif late:
            small_ref[0:8, :] = acc[d + 1, 0:8, :] + own[d + 1]
            small_ref[8:32, :] = acc[d + 1, 8:32, :]

    seg_rows = [jnp.sum(sums[i], axis=0, keepdims=True) for i in range(6)]
    seg_up = jnp.sum(bsums[...], axis=0, keepdims=True)
    order = (6, 7, 5, 4, 2, 1)
    for i, row in enumerate(order):
        if row < 6:
            acc[0, i : i + 1, :] = seg_rows[row]
        acc[0, 6 + i : 7 + i, :] = csums[row : row + 1, :] * share
    for i, row in enumerate((3, 0)):
        acc[0, 12 + i : 13 + i, :] = seg_rows[row]
        acc[0, 14 + i : 15 + i, :] = csums[row : row + 1, :] * share
    for i in range(4):
        acc[0, 16 + i : 17 + i, :] = seg_up[:, i * width : (i + 1) * width]
        acc[0, 20 + i : 21 + i, :] = cbsums[:, i * width : (i + 1) * width] * share
    acc[0, 0:2, :] = jnp.zeros_like(acc[0, 0:2, :])
    acc[0, 24:32, :] = gpos[...] * share
    late_acc[0] = jnp.zeros_like(late_acc[0])

    def cross_unit(n, parts):
        if n >= RING:
            core_copy(n).wait_send()
        for rel in (1, 0):
            core = c if rel == 0 else 1 - c
            for sub, (left, right) in enumerate(parts):
                for far in range(2):
                    value = mm(left(far, core), right).astype(BF16)
                    at = (sub // 2) * 4 + far * 2 + sub % 2
                    if rel == 1:
                        csend[n % RING, at] = value
                    else:
                        keep[n, at] = value
            if rel == 1:
                if n == 0:
                    pl.semaphore_wait(barrier, 6)
                core_copy(n).start()

    def plain(ref):
        return lambda far, core: ref[far, core, z]

    def nested(ref, j):
        return lambda far, core: ref[far, core, z, j]

    def cut(ref, j):
        return ref[:, j * width : (j + 1) * width]

    def cut_group(ref, j):
        return jnp.concatenate([ref[:, part * width + j * GROUP : part * width + (j + 1) * GROUP] for part in range(3)], axis=1)

    cross_parts = (
        lambda: [(plain(cfirstt), cut(cginner, j)) for j in range(4)],
        lambda: [(nested(chiddent, j), cgsecond[...]) for j in range(4)],
        lambda: [(plain(cmixedt), cgbranch[...])] + [(plain(cxt), cut_group(cgqkv, j)) for j in range(GROUPS)],
    )

    def compute(u):
        n = u + CROSS_UNITS - jnp.maximum(CROSS_UNITS - 1 - u, 0)
        t = n % 2
        @pl.when(n >= RING)
        def _():
            core_copy(n).wait_send()

        right = bslot[b_slot(u)]
        for rel in (1, 0):
            core = c if rel == 0 else 1 - c
            left = aslot[a_slot(u), :, core].reshape(8 * PART, -1)
            value = mm(left, right).astype(BF16)
            for far in range(2):
                for part in range(4):
                    block = value[(far * 4 + part) * PART : (far * 4 + part + 1) * PART]
                    ways = far * 4 + (part % 2) * 2 + part // 2, (part // 2) * 4 + far * 2 + part % 2
                    for side, way_of in ((0, t), (1, t + (1 - t) * (n // (UNITS - 1)))):
                        at = choose(way_of, *ways)
                        cols = slice(side * width // 2, (side + 1) * width // 2)
                        if rel == 1:
                            csend[n % RING, at, :, cols] = block[:, cols]
                        else:
                            keep[n, at, :, cols] = block[:, cols]
            if rel == 1:
                core_copy(n).start()

        @pl.when(n < CROSS_UNITS + EARLY)
        def _():
            step_one(n - 1, (n - 1) % 2)

    def attention_tile(j, i):
        slot = i % 2
        out_rows = pl.ds(pl.multiple_of(j * GROUP, GROUP), GROUP)
        g_mixed = mm_nt(gbranch_slot[slot], wout[out_rows, :]).astype(BF16)
        items = [(seg, half) for seg in range(segs) for half in range(2)]
        at = [slice(seg * SEGLEN, (seg + 1) * SEGLEN) for seg, _ in items]
        lanes = [pair_lanes(half) for _, half in items]
        to = [pl.ds(pl.multiple_of(i * tile + seg * SEGLEN, SEGLEN), SEGLEN) for seg, _ in items]
        every = range(len(items))
        g_out = [stack_heads(g_mixed[at[e], lanes[e][0]]) for e in every]
        g_p = [mm_nt(qkv_slot[slot, at[e], lanes[e][2]], g_out[e]) for e in every]
        g_v = [mm(probs_slot[slot, seg, half], g_out[e]) for e, (seg, half) in enumerate(items)]
        g_s = []
        for e, (seg, half) in enumerate(items):
            p = probs_slot[slot, seg, half].astype(F32)
            g_s.append((p * (g_p[e] - jnp.sum(g_p[e] * p, axis=0, keepdims=True))).astype(BF16))
        g_k = [mm(g_s[e], stack_heads(qkv_slot[slot, at[e], lanes[e][0]] * HDIM**-0.5)) for e in every]
        g_st = [jnp.concatenate([g_s[e][:, :SEGLEN].T, g_s[e][:, SEGLEN:].T], axis=1) for e in every]
        g_q = [mm(g_st[e], stack_heads(qkv_slot[slot, at[e], lanes[e][1]])) * HDIM**-0.5 for e in every]
        for e in every:
            for part, value in enumerate((g_q[e], g_k[e], g_v[e])):
                value = value.astype(BF16)
                bslot[j, to[e], lanes[e][part]] = value
                if part != 1:
                    fold[part // 2, j, :, lanes[e][0]] += fold_rows(value.astype(F32))

    def last_tile(i):
        slot = i % 2

        @pl.when(i >= 2)
        def _():
            store_gx(i - 2).wait()

        total = gbranch_slot[slot].astype(F32)
        for j in range(GROUPS):
            total = total + mm_nt(bslot[j, tile_rows(i), :], wqkv[j])
        gx_slot[slot] = total.astype(BF16)
        store_gx(i).start()

    def run(action, n):
        if action in ("small", "late"):
            late = int(action == "late")
            if late and n == 0:
                for row in range(2):
                    for j in range(GROUPS):
                        late_acc[0, row : row + 1, j * GROUP : (j + 1) * GROUP] = jnp.sum(fold[row, j], axis=0, keepdims=True)
            if n == 0:
                small_copy(late, 0).start()
            else:
                small_step(late, n - 1)
            return
        t = n % 2
        cross = t == 0 and n < 2 * CROSS_UNITS
        if action == "one":
            step_one(n, t)
        elif action == "send":
            copy_one(n, t).start()
        elif action == "two":
            step_two(n, t)
        elif action == "three":
            cross_step_final(n) if cross else step_three(n, t)
        elif action == "final":
            cross_step_out(n, n // 2) if cross else step_final(n, t)
        elif not cross:
            step_out(n, t, n // 2 if n < 2 * CROSS_UNITS else min(n, UNITS - 1) - CROSS_UNITS)

    schedule = comm_schedule()

    def step(s, carry):
        for at in range(STEPS):
            if schedule[at]:
                @pl.when(s == at)
                def _(at=at):
                    for action, n in schedule[at]:
                        run(action, n)

        @pl.when(s == EARLY)
        def _():
            for copy in weight_copies:
                copy.wait()

        for i in range(1, CROSS_UNITS):
            @pl.when(s == i)
            def _(i=i):
                cross_unit(2 * i, cross_parts[i]())
                step_one(2 * i - 1, 1)

        load(s, "wait")

        @pl.when(s == 1)
        def _():
            for copy in weight_copies:
                copy.start()

        @pl.when(s + 1 < STEPS)
        def _():
            load(s + 1, "start")

        group, part = place(s)
        inside = (s >= EARLY) & (s < LAST_AT)
        multiply = (s < EARLY) | (inside & (part == TILES))

        @pl.when(multiply)
        def _():
            compute(jnp.where(s < EARLY, s, EARLY + group))

        @pl.when(inside & (part < TILES))
        def _():
            attention_tile(group, part)

        @pl.when(s >= LAST_AT)
        def _():
            last_tile(s - LAST_AT)

        return carry

    fold[...] = jnp.zeros_like(fold)
    cross_unit(0, cross_parts[0]())
    lax.fori_loop(0, STEPS, step, 0)
    for action, n in schedule[STEPS]:
        run(action, n)
    for i in range(TILES - 2, TILES):
        store_gx(i).wait()
    for n in range(UNITS - RING, UNITS):
        core_copy(n).wait_send()


def late_backward(big, cross, small, attn, share):
    firstt, ginner, hiddent, gsecond, mixedt, gbranch, xt = big
    qkv, probs, w_qkv, w_out = attn
    cfirstt, cginner, chiddent, cgsecond, cmixedt, cgbranch, cxt, cgqkv = cross
    width, depth = firstt.shape
    inners = ginner.shape[1]
    rows = cfirstt.shape[1]
    tile = depth // TILES
    assert width == 16 * PART and inners == 4 * width

    def blocks(a, n):
        return a.reshape((2, 2, 4) + ((n,) if n > 1 else ()) + (PART, a.shape[1]))

    operands = [
        blocks(firstt, 1), ginner, blocks(hiddent, 4), gsecond, blocks(mixedt, 1), gbranch, blocks(xt, 1), qkv, probs, w_qkv, w_out,
        blocks(cfirstt, 1), cginner, blocks(chiddent, 4), cgsecond, blocks(cmixedt, 1), cgbranch, blocks(cxt, 1), cgqkv, *small,
    ]
    vmem = pl.BlockSpec(memory_space=pltpu.VMEM)
    any_spec = pl.BlockSpec(memory_space=pl.ANY)
    outs = [((PART, 3 * width), F32), ((PART, width), F32), ((PART, inners), F32), ((4 * PART, width), F32), ((32, width), F32), ((depth, width), BF16)]
    segs = tile // SEGLEN
    dma = pltpu.SemaphoreType.DMA
    return pl.pallas_call(
        functools.partial(late_kernel, share=share),
        in_specs=[any_spec] * 11 + [vmem] * (len(operands) - 11),
        out_specs=[vmem] * 5 + [any_spec],
        out_shape=[jax.ShapeDtypeStruct(*o) for o in outs],
        scratch_shapes=[
            pltpu.VMEM((2, 2, 2, 4, PART, depth), BF16),
            pltpu.VMEM((GROUPS, depth, width), BF16),
            pltpu.VMEM((2, tile, width), BF16),
            pltpu.VMEM((2, segs, 2, SEGLEN, 2 * SEGLEN), BF16),
            pltpu.VMEM((2, tile, width), BF16),
            pltpu.VMEM((2, tile, width), BF16),
            pltpu.VMEM((GROUPS, width, 3 * GROUP), BF16),
            pltpu.VMEM(w_out.shape[1:], BF16),
            pltpu.VMEM((2, GROUPS, 8, GROUP), F32),
            pltpu.VMEM((RING, 8, PART, width), BF16),
            pltpu.VMEM((RING, 8, PART, width), BF16),
            pltpu.VMEM((UNITS, 8, PART, width), BF16),
            pltpu.VMEM((UNITS, 4, PART, width), BF16),
            pltpu.VMEM((UNITS, 2, PART, width), BF16),
            pltpu.VMEM((UNITS, PART, width), BF16),
            pltpu.VMEM((UNITS, 2, PART, width), BF16),
            pltpu.VMEM((6, 32, width), F32),
            pltpu.VMEM((5, 32, width), F32),
            pltpu.VMEM((6, 8, width), F32),
            pltpu.VMEM((5, 8, width), F32),
            dma((2,)), dma((2, 3)), dma((2,)), dma((1 + 3 * GROUPS,)), dma((RING,)), dma((RING,)), dma((CHAINS,)), dma((CHAINS,)), dma((CHAINS,)), dma((CHAINS,)),
            dma((CHAINS,)), dma((CHAINS,)), dma((CHAINS,)), dma((CHAINS, 2)), dma((2, 5)), dma((2, 5)),
        ],
        compiler_params=pltpu.CompilerParams(vmem_limit_bytes=63 * 2**20, collective_id=1, has_side_effects=True),
        name="late_backward",
    )(*operands)

def finish_kernel(gx_ref, a_ref, b_ref, c_ref, d_ref, gx_out, a_out, b_out, c_out, d_out):
    gx_out[...] = gx_ref[...].astype(F32)

    @pl.when(pl.program_id(0) == 0)
    def _():
        for src, dst in ((a_ref, a_out), (b_ref, b_out), (c_ref, c_out), (d_ref, d_out)):
            dst[...] = src[...]


def finish(gx, grads, tile=512):
    total, width = gx.shape
    rows = pl.BlockSpec((tile, width), lambda i: (i, 0))
    held = [pl.BlockSpec(g.shape, lambda i: (0, 0)) for g in grads]
    return pl.pallas_call(
        finish_kernel,
        grid=(total // tile,),
        in_specs=[rows] + held,
        out_specs=[rows] + held,
        out_shape=[jax.ShapeDtypeStruct(gx.shape, F32)] + [jax.ShapeDtypeStruct(g.shape, F32) for g in grads],
        name="finish",
    )(gx, *grads)


def small_grads(sums, bsums, csums, cbsums, gpos, bias_sums, cross_share):
    seg_rows = jnp.concatenate([jnp.sum(sums, axis=1), bias_sums])
    cross_rows = csums * cross_share
    order = jnp.array([6, 7, 5, 4, 2, 1])
    biases = jnp.stack([seg_rows[order], cross_rows[order]])
    gains = jnp.stack([seg_rows[jnp.array([3, 0])], cross_rows[jnp.array([3, 0])]])
    ups = jnp.stack([jnp.sum(bsums, axis=0), cbsums[0] * cross_share])
    return biases.reshape(-1), gains.reshape(-1), ups.reshape(-1), (gpos * cross_share).reshape(-1)


def attention_back(qkv, probs, gbranch, w_qkv, w_out):
    total, width = gbranch.shape
    heads = width // HDIM
    segs = total // SEGLEN
    scale = HDIM**-0.5

    def split(a):
        return a.reshape(segs, SEGLEN, heads, HDIM)

    def merge(a):
        return a.reshape(total, width)

    q, k, v = (
        split(qkv[:, :, part * GROUP : (part + 1) * GROUP].transpose(1, 0, 2).reshape(total, width)) for part in range(3)
    )
    p_low = probs.reshape(segs, heads // 2, SEGLEN, 2, SEGLEN).transpose(0, 1, 3, 2, 4).reshape(segs, heads, SEGLEN, SEGLEN)
    g_out = split(mm_nt(gbranch, w_out).astype(BF16))
    p = p_low.astype(F32)
    g_p = jnp.einsum("sqhd,skhd->shkq", g_out, v, preferred_element_type=F32)
    g_s = (p * (g_p - jnp.sum(g_p * p, axis=2, keepdims=True))).astype(BF16)
    g_v = jnp.einsum("shkq,sqhd->skhd", p_low, g_out, preferred_element_type=F32)
    g_k = jnp.einsum("shkq,sqhd->skhd", g_s, q, preferred_element_type=F32) * scale
    g_q = jnp.einsum("shkq,skhd->sqhd", g_s, k, preferred_element_type=F32) * scale
    g_qkv = jnp.concatenate([merge(g_q), merge(g_k), merge(g_v)], axis=1).astype(BF16)
    return g_qkv, gbranch.astype(F32) + mm_nt(g_qkv, w_qkv)


def generic_total(seg_pairs, cross_pairs, small, planes, own):
    axes = ("row", "seg")
    me = lax.axis_index("seg")
    shards = [
        lax.psum_scatter(part, axes, scatter_dimension=0, tiled=True) for part in small_grads(*small, 1.0 / planes)
    ]

    def mine(values, dim):
        return lax.dynamic_slice_in_dim(values, me * own, own, dim)

    big = []
    for at in (6, 4, 0, 2):
        cross = mm(mine(cross_pairs[at], 1), mine(cross_pairs[at + 1], 0))
        both = jnp.concatenate([mm(seg_pairs[at], seg_pairs[at + 1]), cross], axis=0)
        big.append(lax.psum_scatter(both, axes, scatter_dimension=0, tiled=True))
    return big, shards


def per_device(
    tokens, doc_ids, w_qkv, w_out, w_up, w_down, biases, gains, b_up, pos_table, cotangent, *, sizes
):
    lines, planes = sizes
    row_count, local_length, width = tokens.shape
    seg_here = local_length // SEGLEN
    segments = doc_ids.shape[1]
    total = row_count * local_length
    own = row_count * seg_here

    seg_place = jnp.arange(segments)
    same_doc = doc_ids[:, :, None] == doc_ids[:, None, :]
    doc_start = jnp.min(jnp.where(same_doc, seg_place[None, None, :], segments), axis=2)

    def by_device(values):
        return values.reshape(row_count, planes, seg_here).transpose(1, 0, 2).reshape(-1, 1)

    place = by_device(seg_place[None, :] - doc_start)
    keys = by_device(doc_ids + segments * jnp.arange(row_count)[:, None])

    cot = cotangent.reshape(total, width)
    (
        qkv, probs, n1, r1, slope, n2, r2, y, xt, mixedt, firstt, hiddent,
        ccls, gcls, csums, cbsums, gpos, cxt, cmixedt, cfirstt, chiddent, cgqkv, cgbranch, cginner, cgsecond,
    ) = forward_blocks(
        tokens.reshape(total, width), cot, w_qkv, w_out, w_up, w_down, biases, gains, b_up, place, keys, pos_table, planes,
        tile=256 if planes <= 4 else 128,
    )
    output, gsecond, ginner, gbranch, sums, bsums = early_backward(
        gcls, ccls, cot, y, n2, r2, slope, n1, r1, w_up, w_down, gains
    )
    cross_pairs = (cfirstt, cginner, chiddent, cgsecond, cmixedt, cgbranch, cxt, cgqkv)
    share = 1.0 / planes
    if (lines, planes) == (8, 4) and total == 2048 and width == 16 * PART:
        *grads, small, gx = late_backward(
            (firstt, ginner, hiddent, gsecond, mixedt, gbranch, xt), cross_pairs, (sums, bsums, csums, cbsums, gpos), (qkv, probs, w_qkv, w_out), share
        )
        gx, *grads = finish(gx, grads)
        small = small.reshape(-1)
        index = lax.axis_index("row") * planes + lax.axis_index("seg")
        shards, start = [], 0
        for size in (12 * width, 4 * width, 8 * width, segments * width):
            count = size // (lines * planes)
            shards.append(lax.dynamic_slice_in_dim(small, start + index * count, count, 0))
            start += size
    else:
        gqkv, gx = attention_back(qkv, probs, gbranch, w_qkv[0], w_out[0])
        bias_sums = jnp.stack([jnp.sum(gqkv[:, at : at + width].astype(F32), axis=0) for at in (0, 2 * width)])
        grads, shards = generic_total(
            (firstt, ginner, hiddent, gsecond, mixedt, gbranch, xt, gqkv), cross_pairs, (sums, bsums, csums, cbsums, gpos, bias_sums), planes, own
        )
    return (output.reshape(tokens.shape), gx.reshape(tokens.shape), *grads, *shards)


def solution(mesh):
    sizes = (mesh.shape["row"], mesh.shape["seg"])
    tokens_at = P("row", "seg", None)
    return jax.shard_map(
        functools.partial(per_device, sizes=sizes),
        mesh=mesh,
        in_specs=(tokens_at, P("row", None)) + (P(),) * 8 + (tokens_at,),
        out_specs=(tokens_at, tokens_at) + (P(("row", "seg"), None),) * 4 + (P(("row", "seg")),) * 4,
        check_vma=False,
    )
```

```python
import functools

import jax
import jax.numpy as jnp
from jax import lax
from jax.experimental import pallas as pl
from jax.experimental.pallas import tpu as pltpu
from jax.sharding import PartitionSpec as P


HDIM = 64
SEGLEN = 128
LANES = 128
GROUP = 2 * LANES
EPSILON = 1e-05
GELU_A = 0.7978845608028654
GELU_B = 0.044715 * GELU_A
F32, BF16 = jnp.float32, jnp.bfloat16


def mm(a, b):
    return lax.dot_general(a, b, (((1,), (0,)), ((), ())), preferred_element_type=F32)


def mm_nt(a, b):
    return lax.dot_general(a, b, (((1,), (1,)), ((), ())), preferred_element_type=F32)


def mm_tn(a, b):
    return lax.dot_general(a, b, (((0,), (0,)), ((), ())), preferred_element_type=F32)


def low_lanes(shape):
    return lax.broadcasted_iota(jnp.int32, shape, 1) < HDIM


def stack_heads(pair):
    keep = low_lanes(pair.shape)
    zero = jnp.zeros_like(pair)
    return jnp.concatenate([jnp.where(keep, pair, zero), jnp.where(keep, zero, pair)], axis=0)


def pair_lanes(half):
    return [slice(part * GROUP + half * LANES, part * GROUP + (half + 1) * LANES) for part in range(3)]


def norm_stats(values):
    centered = values - jnp.mean(values, axis=-1, keepdims=True)
    variance = jnp.mean(centered * centered, axis=-1, keepdims=True)
    rstd = lax.rsqrt(variance + EPSILON)
    return centered * rstd, rstd


def gelu_both(u):
    u = u.astype(BF16)
    square = u * u
    bend = GELU_B * square
    half = 0.5 * jnp.tanh(u * (GELU_A + bend))
    gate = half + 0.5
    hidden = u * gate
    slope = gate + hidden * (0.5 - half) * (2.0 * GELU_A + 6.0 * bend)
    return hidden, slope


def norm_back(grad, gain, normal, rstd):
    scaled = grad * gain
    a = jnp.mean(scaled, axis=-1, keepdims=True)
    b = jnp.mean(scaled * normal, axis=-1, keepdims=True)
    return (scaled - a - normal * b) * rstd


OUTS = 13
NEGATIVE = -1000000000.0
MESH = pl.DeviceIdType.MESH


def turned(values):
    return values.astype(F32).T.astype(BF16)


def places(docs, rows, own, kinds):
    lines, segments = docs.shape
    here = own // lines
    count = 2 * rows

    def spread(width, axis):
        return lax.broadcasted_iota(jnp.int32, (count, width), axis)

    def line_of(at):
        return lax.shift_right_logical(at & (own - 1), here.bit_length() - 1)

    in_line = line_of(spread(lines, 0)) == spread(lines, 1)
    row_docs = mm(in_line.astype(BF16), docs.astype(F32).astype(BF16))
    at = spread(segments, 0) & (rows - 1)
    segment = lax.shift_right_logical(at, own.bit_length() - 1) * here + (at & (here - 1))
    across = spread(segments, 1)
    doc = jnp.sum(jnp.where(across == segment, row_docs, 0.0), axis=1, keepdims=True)
    start = jnp.min(jnp.where(row_docs == doc, across.astype(F32), float(segments)), axis=1, keepdims=True)
    place = segment[:, 0:1].astype(F32) - start
    onehot = (place == spread(kinds, 1).astype(F32))[:rows].astype(F32)
    key = doc + segments * line_of(spread(1, 0)).astype(F32)
    keys_across = jnp.broadcast_to(key, (count, max(rows, LANES))).T[:rows]
    return onehot, key[:rows] == keys_across


def cross_part(me, doc_ref, table_ref, bias_ref, gain_ref, bup_ref, outs, writes, weights, copies, scratch, ff_chunk):
    (
        ccls_ref, gcls_ref, sums_ref, bsums_ref, gpos_ref, xt_ref, mixedt_ref, firstt_ref, hiddent_ref,
        gqkv_ref, gbranch_ref, ginner_ref, gsecond_ref,
    ) = outs
    wqkv, wout, wup, wdown = weights
    qkv_ref, probs_ref, mixed_ref, slope_ref, whole_ref = scratch
    own, width = ccls_ref.shape
    rows = whole_ref.shape[1]
    inners = wup.shape[1]
    bias = bias_ref[...].astype(F32)[:, 1]
    gain = gain_ref[1].astype(F32)
    up_bias = bup_ref[1:2, :].astype(F32)
    onehot, allowed = places(doc_ref[...], rows, own, table_ref.shape[0])
    embed = mm(onehot.astype(BF16), table_ref[...])
    x = (whole_ref[0] + embed).astype(BF16)
    gy = whole_ref[1]
    xt_ref[...] = turned(x)
    copies[0].wait()
    for part in range(3):
        cols = slice(part * width, (part + 1) * width)
        out = mm(x, wqkv[:, cols])
        if part == 0:
            out = out + bias[0:1]
        if part == 2:
            out = out + bias[1:2]
        qkv_ref[:, cols] = out.astype(BF16)
    low = low_lanes((rows, LANES))
    pairs = range(width // LANES)
    lanes = [[slice(part * width + pair * LANES, part * width + (pair + 1) * LANES) for part in range(3)] for pair in pairs]
    scores = [
        jnp.where(allowed, mm_nt(qkv_ref[:, at[1]], stack_heads(qkv_ref[:, at[0]] * HDIM**-0.5)), NEGATIVE) for at in lanes
    ]
    pt = []
    for pair in pairs:
        e = jnp.exp(scores[pair] - jnp.max(scores[pair], axis=0, keepdims=True))
        p = e * (1.0 / jnp.sum(e, axis=0, keepdims=True))
        probs_ref[pair] = p
        pt.append(p.T.astype(BF16))
    for pair, at in enumerate(lanes):
        v = qkv_ref[:, at[2]]
        mixed_ref[:, at[0]] = jnp.where(low, mm(pt[pair][:rows], v), mm(pt[pair][rows:], v)).astype(BF16)
    copies[1].wait()
    mixed = mixed_ref[...]
    mixedt_ref[...] = turned(mixed)
    n1, r1 = norm_stats(x.astype(F32) + mm(mixed, wout[...]) + bias[2:3])
    first = (n1 * gain[0:1] + bias[3:4]).astype(BF16)
    firstt_ref[...] = turned(first)
    copies[2].wait()
    copies[3].wait()
    total = first.astype(F32) + bias[4:5]
    chunks = [slice(c * ff_chunk, (c + 1) * ff_chunk) for c in range(inners // ff_chunk)]
    inner = [mm(first, wup[:, cols]) for cols in chunks]
    for c, cols in enumerate(chunks):
        hidden, slope = gelu_both(inner[c] + up_bias[:, cols])
        hidden = hidden.astype(BF16)
        hiddent_ref[cols, :] = turned(hidden)
        slope_ref[:, cols] = slope.astype(F32)
        total = total + mm(hidden, wdown[cols, :])
    n2, r2 = norm_stats(total)
    mine = pl.ds(pl.multiple_of(me * own, own), own)
    whole_ref[0] = (n2 * gain[1:2] + bias[5:6]).astype(BF16).astype(F32)
    ccls_ref[...] = whole_ref[0, mine, :]
    for i in (0, 5, 6, 7, 8):
        writes[i].start()

    def row_sum(values):
        return jnp.sum(values.astype(F32), axis=0, keepdims=True)

    sums_ref[0:1, :] = row_sum(gy * n2)
    sums_ref[1:2, :] = row_sum(gy)
    g_two = norm_back(gy, gain[1:2], n2, r2)
    g_second = g_two.astype(BF16)
    gsecond_ref[...] = g_second
    sums_ref[2:3, :] = row_sum(g_second)
    g_first = g_two
    g_hidden = [mm_nt(g_second, wdown[cols, :]) for cols in chunks]
    for c, cols in enumerate(chunks):
        g_inner = (g_hidden[c] * slope_ref[:, cols]).astype(BF16)
        ginner_ref[:, cols] = g_inner
        bsums_ref[:, cols] = row_sum(g_inner)
        g_first = g_first + mm_nt(g_inner, wup[:, cols])
    sums_ref[3:4, :] = row_sum(g_first * n1)
    sums_ref[4:5, :] = row_sum(g_first)
    g_one = norm_back(g_first, gain[0:1], n1, r1)
    g_branch = g_one.astype(BF16)
    gbranch_ref[...] = g_branch
    sums_ref[5:6, :] = row_sum(g_branch)
    for i in (10, 11, 12):
        writes[i].start()
    g_mixed = mm_nt(g_branch, wout[...]).astype(BF16)
    g_out = [stack_heads(g_mixed[:, at[0]]) for at in lanes]
    g_p = [mm_nt(qkv_ref[:, at[2]], g_out[pair]) for pair, at in enumerate(lanes)]
    g_s, g_st = [], []
    for pair in pairs:
        p = probs_ref[pair]
        g = p * (g_p[pair] - jnp.sum(g_p[pair] * p, axis=0, keepdims=True))
        g_s.append(g.astype(BF16))
        g_st.append(g.T.astype(BF16))
    for pair, at in enumerate(lanes):
        q, k, _ = (qkv_ref[:, part] for part in at)
        g_q = jnp.where(low, mm(g_st[pair][:rows], k), mm(g_st[pair][rows:], k)) * HDIM**-0.5
        gqkv_ref[:, at[0]] = g_q.astype(BF16)
        gqkv_ref[:, at[1]] = mm(g_s[pair], stack_heads(q * HDIM**-0.5)).astype(BF16)
        gqkv_ref[:, at[2]] = mm(probs_ref[pair].astype(BF16), g_out[pair]).astype(BF16)
    g_qkv = gqkv_ref[...]
    sums_ref[6:7, :] = row_sum(g_qkv[:, :width])
    sums_ref[7:8, :] = row_sum(g_qkv[:, 2 * width :])
    g_x = g_one + mm_nt(g_qkv, wqkv[...])
    whole_ref[1] = g_x
    gcls_ref[...] = whole_ref[1, mine, :]
    gpos_ref[...] = lax.dot_general(onehot, g_x, (((0,), (0,)), ((), ())), preferred_element_type=F32, precision=lax.Precision.HIGHEST)
    for i in (1, 2, 3, 4, 9):
        writes[i].start()
    for write in writes:
        write.wait()


def forward_kernel(
    x_ref, wqkv_hbm, wout_hbm, wup_hbm, wdown_hbm, cot_hbm, bias_ref, gain_ref, bup_ref, doc_ref, table_ref,
    qkv_ref, probs_ref, n1_ref, r1_ref, slope_ref, n2_ref, r2_ref, y_ref, xt_ref, mixedt_ref, firstt_ref, hiddent_ref,
    *refs, ff_chunk, devices,
):
    homes, outs, refs = refs[:OUTS], refs[OUTS : 2 * OUTS], refs[2 * OUTS :]
    wqkv, wout, wup, wdown, mixed_ref, first_ref, sems, cls_ref, cot_rows, cot_low, packed, gathered = refs[:12]
    cross_weights, cross_scratch = refs[12:16], refs[16:21]
    cross_sems, out_sems, cot_sems, send_sems, recv_sems = refs[21:]
    step = pl.program_id(0)
    last = pl.num_programs(0) - 1
    rows, width = x_ref.shape
    parts = [slice(part * width, (part + 1) * width) for part in range(3)]
    part_copies = [pltpu.make_async_copy(wqkv_hbm.at[0, :, cols], wqkv.at[:, cols], sems.at[3 + i]) for i, cols in enumerate(parts)]
    copies = part_copies + [
        pltpu.make_async_copy(src.at[0], dst, sems.at[i])
        for i, (src, dst) in enumerate(((wout_hbm, wout), (wup_hbm, wup), (wdown_hbm, wdown)))
    ]

    own = cls_ref.shape[0]
    line, me = lax.axis_index("row"), lax.axis_index("seg")
    peers = [(line, lax.rem(me + hop, devices)) for hop in range(1, devices)]
    cot_copies = [
        pltpu.make_async_copy(cot_hbm.at[pl.ds(i * SEGLEN, 16)], cot_rows.at[i], cot_sems.at[i]) for i in range(own)
    ]
    cross_copies = [
        pltpu.make_async_copy(src.at[1], dst, cross_sems.at[i])
        for i, (src, dst) in enumerate(zip((wqkv_hbm, wout_hbm, wup_hbm, wdown_hbm), cross_weights))
    ]
    writes = [pltpu.make_async_copy(src, dst, out_sems.at[i]) for i, (src, dst) in enumerate(zip(outs, homes))]
    barrier = pltpu.get_barrier_semaphore()

    def sends(kind):
        return [
            pltpu.make_async_remote_copy(
                src_ref=packed.at[kind], dst_ref=gathered.at[kind, hop + 1], send_sem=send_sems.at[kind, hop],
                recv_sem=recv_sems.at[kind, hop], device_id=peer, device_id_type=MESH,
            )
            for hop, peer in enumerate(peers)
        ]

    def arrived(kind, whole_ref):
        for send in sends(kind):
            send.wait()
        gathered[kind, 0] = packed[kind]
        for hop in range(devices):
            rows_at = pl.ds(pl.multiple_of(lax.rem(me - hop + devices, devices) * own, own), own)
            whole_ref[1 - kind, rows_at, :] = gathered[kind, hop].astype(F32)

    @pl.when(step == 0)
    def _():
        for peer in peers:
            pl.semaphore_signal(barrier, inc=1, device_id=peer, device_id_type=MESH)
        for copy in copies[:4]:
            copy.start()

    @pl.when(step == 1)
    def _():
        copies[4].wait()
        copies[5].wait()
        for copy in cot_copies + cross_copies:
            copy.start()

    @pl.when(step == 2)
    def _():
        for i, copy in enumerate(cot_copies):
            copy.wait()
            cot_low[i : i + 1, :] = cot_rows[i, 0:8, :].astype(F32)[0:1]
        packed[0] = cot_low[...].astype(BF16)
        pl.semaphore_wait(barrier, devices - 1)
        for send in sends(0):
            send.start()

    bias = bias_ref[...].astype(F32)[:, 0]
    gain = gain_ref[0].astype(F32)
    up_bias = bup_ref[0:1, :].astype(F32)
    inners = wup.shape[1]
    chunks = [slice(c * ff_chunk, (c + 1) * ff_chunk) for c in range(inners // ff_chunk)]
    items = [(seg, pair) for seg in range(rows // SEGLEN) for pair in range(width // LANES)]
    every = range(len(items))
    at = [slice(seg * SEGLEN, (seg + 1) * SEGLEN) for seg, _ in items]

    def front(state, loading):
        def project_part(part):
            if loading:
                copies[part].wait()
                if part == 0:
                    copies[4].start()
                    copies[5].start()
            x = x_ref[...]
            out = mm(x, wqkv[:, part * width : (part + 1) * width])
            if part == 0:
                out = out + bias[0:1]
            if part == 2:
                out = out + bias[1:2]
            out = out.astype(BF16)
            for group in range(width // GROUP):
                qkv_ref[group, :, part * GROUP : (part + 1) * GROUP] = out[:, group * GROUP : (group + 1) * GROUP]

        def piece(e, part):
            pair = items[e][1]
            return qkv_ref[pair // 2, at[e], pair_lanes(pair % 2)[part]]

        def scores():
            xt_ref[...] = x_ref[...].T
            state["scores"] = [mm_nt(piece(e, 1), stack_heads(piece(e, 0) * HDIM**-0.5)) for e in every]

        def softmax(part):
            for e in every[part :: 2]:
                score = state["scores"][e]
                ex = jnp.exp(score - jnp.max(score, axis=0, keepdims=True))
                p = (ex * (1.0 / jnp.sum(ex, axis=0, keepdims=True))).astype(BF16)
                probs_ref[items[e][0], items[e][1]] = p
                state[e] = jnp.concatenate([p[:, :SEGLEN].T, p[:, SEGLEN:].T], axis=1)

        def mix():
            for e, (_, pair) in enumerate(items):
                mixed_ref[at[e], pair * LANES : (pair + 1) * LANES] = mm(state[e], stack_heads(piece(e, 2))).astype(BF16)

        def project_out():
            if loading:
                copies[3].wait()
            mixed = mixed_ref[...]
            mixedt_ref[...] = mixed.T
            state["resid"] = x_ref[...].astype(F32) + mm(mixed, wout[...]) + bias[2:3]

        def norm():
            n1, r1 = norm_stats(state["resid"])
            n1_ref[...] = n1.astype(BF16)
            r1_ref[...] = jnp.broadcast_to(r1, r1_ref.shape)
            first = (n1 * gain[0:1] + bias[3:4]).astype(BF16)
            firstt_ref[...] = first.T
            state["first"] = first

        return [lambda part=part: project_part(part) for part in range(3)] + [scores, lambda: softmax(0), lambda: softmax(1), mix, project_out, norm]

    def back(state):
        first = first_ref[...]
        state["total"] = first.astype(F32) + bias[4:5]

        def up(c):
            state["inner", c] = mm(first, wup[:, chunks[c]])

        def gelu(c):
            cols = chunks[c]
            hidden, slope = gelu_both(state["inner", c] + up_bias[:, cols])
            hidden = hidden.astype(BF16)
            hiddent_ref[cols, :] = hidden.T
            slope_ref[:, cols] = slope.astype(BF16)
            state["hidden", c] = hidden

        def down(c):
            state["total"] = state["total"] + mm(state["hidden", c], wdown[chunks[c], :])

        def norm():
            n2, r2 = norm_stats(state["total"])
            n2_ref[...] = n2.astype(BF16)
            r2_ref[...] = jnp.broadcast_to(r2, r2_ref.shape)
            y = (n2 * gain[1:2] + bias[5:6]).astype(BF16)
            y_ref[...] = y
            segs = rows // SEGLEN
            for seg in range(segs):
                cls_ref[pl.ds((step - 1) * segs + seg, 1), :] = y[seg * SEGLEN : seg * SEGLEN + 8].astype(F32)[0:1]

        pieces = [lambda: up(0)]
        for c in range(len(chunks)):
            if c + 1 < len(chunks):
                pieces.append(lambda c=c: up(c + 1))
            pieces += [lambda c=c: gelu(c), lambda c=c: down(c)]
        return pieces + [norm]

    def run(with_front, with_back):
        state = {}
        lists = ([back(state)] if with_back else []) + ([front(state, not with_back)] if with_front else [])
        turns = sorted((((i + 0.5) / len(pieces), k, i) for k, pieces in enumerate(lists) for i in range(len(pieces))))
        for _, k, i in turns:
            lists[k][i]()
        if with_front:
            first_ref[...] = state["first"]

    @pl.when(step == 0)
    def _():
        run(True, False)

    @pl.when((step > 0) & (step < last))
    def _():
        run(True, True)

    @pl.when(step == last)
    def _():
        run(False, True)
        packed[1] = cls_ref[...].astype(BF16)
        for send in sends(1):
            send.start()
        arrived(0, cross_scratch[-1])
        arrived(1, cross_scratch[-1])
        cross_part(
            me, doc_ref, table_ref, bias_ref, gain_ref, bup_ref, outs, writes,
            cross_weights, cross_copies, cross_scratch, ff_chunk,
        )


def forward_blocks(x, cot, w_qkv, w_out, w_up, w_down, bias, gain, bup, docs, table, devices, tile=256, ff_chunk=768):
    total, width = x.shape
    inners = w_up.shape[-1]
    segs = tile // SEGLEN
    pairs = width // LANES
    any_spec = pl.BlockSpec(memory_space=pl.ANY)

    steps = total // tile

    def rows_of(cols, late):
        return pl.BlockSpec((tile, cols), lambda i: (jnp.maximum(i - 1, 0) if late else jnp.minimum(i, steps - 1), 0))

    def whole(a):
        return pl.BlockSpec(a.shape, lambda i: (0,) * a.ndim)

    def cols_of(rows, late):
        return pl.BlockSpec((rows, tile), lambda i: (0, jnp.maximum(i - 1, 0) if late else jnp.minimum(i, steps - 1)))

    outs = [
        ((width // GROUP, total, 3 * GROUP), BF16, pl.BlockSpec((width // GROUP, tile, 3 * GROUP), lambda i: (0, jnp.minimum(i, steps - 1), 0))),
        ((total // SEGLEN, pairs, SEGLEN, 2 * SEGLEN), BF16, pl.BlockSpec((segs, pairs, SEGLEN, 2 * SEGLEN), lambda i: (jnp.minimum(i, steps - 1), 0, 0, 0))),
        ((total, width), BF16, rows_of(width, False)),
        ((total, LANES), F32, rows_of(LANES, False)),
        ((total, inners), BF16, rows_of(inners, True)),
        ((total, width), BF16, rows_of(width, True)),
        ((total, LANES), F32, rows_of(LANES, True)),
        ((total, width), BF16, rows_of(width, True)),
        ((width, total), BF16, cols_of(width, False)),
        ((width, total), BF16, cols_of(width, False)),
        ((width, total), BF16, cols_of(width, False)),
        ((inners, total), BF16, cols_of(inners, True)),
    ]
    own = total // SEGLEN
    rows = own * devices
    cross_outs = [
        ((own, width), F32), ((own, width), F32), ((8, width), F32), ((1, inners), F32), (table.shape, F32),
        ((width, rows), BF16), ((width, rows), BF16), ((width, rows), BF16), ((inners, rows), BF16),
        ((rows, 3 * width), BF16), ((rows, width), BF16), ((rows, inners), BF16), ((rows, width), BF16),
    ]
    bias = bias.transpose(1, 0, 2)
    dma = pltpu.SemaphoreType.DMA
    return pl.pallas_call(
        functools.partial(forward_kernel, ff_chunk=ff_chunk, devices=devices),
        grid=(steps + 1,),
        in_specs=[rows_of(width, False), any_spec, any_spec, any_spec, any_spec, any_spec]
        + [whole(a) for a in (bias, gain, bup, docs, table)],
        out_specs=[o[2] for o in outs] + [pl.BlockSpec(memory_space=pltpu.HBM)] * OUTS,
        out_shape=[jax.ShapeDtypeStruct(o[0], o[1]) for o in outs + cross_outs],
        scratch_shapes=[pltpu.VMEM(*o) for o in cross_outs]
        + [
            pltpu.VMEM(w_qkv.shape[1:], BF16),
            pltpu.VMEM(w_out.shape[1:], BF16),
            pltpu.VMEM(w_up.shape[1:], BF16),
            pltpu.VMEM(w_down.shape[1:], BF16),
            pltpu.VMEM((tile, width), BF16),
            pltpu.VMEM((tile, width), BF16),
            dma((6,)),
            pltpu.VMEM((own, width), F32),
            pltpu.VMEM((own, 16, width), BF16),
            pltpu.VMEM((own, width), F32),
            pltpu.VMEM((2, own, width), BF16),
            pltpu.VMEM((2, devices, own, width), BF16),
            pltpu.VMEM(w_qkv.shape[1:], BF16),
            pltpu.VMEM(w_out.shape[1:], BF16),
            pltpu.VMEM(w_up.shape[1:], BF16),
            pltpu.VMEM(w_down.shape[1:], BF16),
            pltpu.VMEM((rows, 3 * width), BF16),
            pltpu.VMEM((pairs, rows, 2 * rows), F32),
            pltpu.VMEM((rows, width), BF16),
            pltpu.VMEM((rows, inners), F32),
            pltpu.VMEM((2, rows, width), F32),
            dma((4,)), dma((OUTS,)), dma((own,)), dma((2, devices - 1)), dma((2, devices - 1)),
        ],
        compiler_params=pltpu.CompilerParams(vmem_limit_bytes=63 * 2**20, collective_id=0, has_side_effects=True),
        name="forward_blocks",
    )(x, w_qkv, w_out, w_up, w_down, cot, bias, gain, bup, docs, table)

def fold_rows(values):
    rows, cols = values.shape
    return jnp.sum(values.reshape(rows // 8, 8, cols), axis=0)


def early_kernel(
    gcls_ref, ccls_ref, cot_ref, y_ref, n2_ref, r2_ref, slope_ref, n1_ref, r1_ref, wup_hbm, wdown_hbm, gain_ref,
    out_ref, gsecond_ref, ginner_ref, gbranch_ref, sums_ref, bsums_ref, wup, wdown, two_ref, sems, *, ff_chunk,
):
    step = pl.program_id(0)
    last = pl.num_programs(0) - 1
    inners = wup.shape[1]
    chunks = [slice(c * ff_chunk, (c + 1) * ff_chunk) for c in range(inners // ff_chunk)]
    down_copies = [pltpu.make_async_copy(wdown_hbm.at[0, cols], wdown.at[cols], sems.at[0, c]) for c, cols in enumerate(chunks)]
    up_copies = [pltpu.make_async_copy(wup_hbm.at[0, :, cols], wup.at[:, cols], sems.at[1, c]) for c, cols in enumerate(chunks)]

    queue, order = down_copies[:1], [("down", 0)]
    for c in range(len(chunks)):
        queue += down_copies[c + 1 : c + 2] + [up_copies[c]]
        order += [("down", c + 1)] * (c + 1 < len(chunks)) + [("up", c)]

    def take(kind, c):
        at = order.index((kind, c))
        queue[at].wait()
        if at + 3 < len(queue):
            queue[at + 3].start()

    @pl.when(step == 0)
    def _():
        for copy in queue[:3]:
            copy.start()
        sums_ref[...] = jnp.zeros_like(sums_ref)
        bsums_ref[...] = jnp.zeros_like(bsums_ref)

    rows, width = cot_ref.shape
    segs = rows // SEGLEN
    gain = gain_ref[0].astype(F32)

    def front(state):
        def gradient():
            place = lax.broadcasted_iota(jnp.int32, (rows, width), 0)
            gy = cot_ref[...].astype(F32)
            y = y_ref[...].astype(F32)
            for seg in range(segs):
                at = pl.ds(step * segs + seg, 1)
                gy = jnp.where(place == seg * SEGLEN, gcls_ref[at, :], gy)
                y = jnp.where(place == seg * SEGLEN, ccls_ref[at, :], y)
            out_ref[...] = y.astype(BF16)
            state["gy"] = gy

        def norm():
            gy = state["gy"]
            n2 = n2_ref[...].astype(F32)
            sums_ref[0] += fold_rows(gy * n2)
            sums_ref[1] += fold_rows(gy)
            state["two"] = norm_back(gy, gain[1:2], n2, r2_ref[:, 0:1])

        def store():
            low = state["two"].astype(BF16)
            gsecond_ref[...] = low
            sums_ref[2] += fold_rows(low.astype(F32))

        return [gradient, norm, store]

    def back(state, loading):
        g_two = two_ref[...]
        g_second = g_two.astype(BF16)
        state["first"] = g_two

        def down(c):
            if loading:
                take("down", c)
            state["hidden", c] = mm_nt(g_second, wdown[chunks[c], :])

        def slope(c):
            cols = chunks[c]
            g_low = state["hidden", c].astype(BF16) * slope_ref[:, cols]
            ginner_ref[:, cols] = g_low
            bsums_ref[:, cols] += fold_rows(g_low.astype(F32))
            state["inner", c] = g_low

        def up(c):
            if loading:
                take("up", c)
            state["first"] = state["first"] + mm_nt(state["inner", c], wup[:, chunks[c]])

        def norm():
            g_first = state["first"]
            n1 = n1_ref[...].astype(F32)
            sums_ref[3] += fold_rows(g_first * n1)
            sums_ref[4] += fold_rows(g_first)
            g_branch = norm_back(g_first, gain[0:1], n1, r1_ref[:, 0:1]).astype(BF16)
            gbranch_ref[...] = g_branch
            sums_ref[5] += fold_rows(g_branch.astype(F32))

        pieces = [lambda: down(0)]
        for c in range(len(chunks)):
            if c + 1 < len(chunks):
                pieces.append(lambda c=c: down(c + 1))
            pieces += [lambda c=c: slope(c), lambda c=c: up(c)]
        return pieces + [norm]

    def run(with_front, with_back, loading=False):
        state = {}
        lists = ([back(state, loading)] if with_back else []) + ([front(state)] if with_front else [])
        turns = sorted((((i + 0.5) / len(pieces), k, i) for k, pieces in enumerate(lists) for i in range(len(pieces))))
        for _, k, i in turns:
            lists[k][i]()
        if with_front:
            two_ref[...] = state["two"]

    @pl.when(step == 0)
    def _():
        run(True, False)

    @pl.when(step == 1)
    def _():
        run(True, True, True)

    @pl.when((step > 1) & (step < last))
    def _():
        run(True, True)

    @pl.when(step == last)
    def _():
        run(False, True)


def early_backward(gcls, ccls, cot, y, n2, r2, slope, n1, r1, w_up, w_down, gains, tile=256, ff_chunk=768):
    total, width = cot.shape
    inners = w_up.shape[-1]
    any_spec = pl.BlockSpec(memory_space=pl.ANY)

    steps = total // tile

    def rows_of(cols, late=False):
        return pl.BlockSpec((tile, cols), lambda i: (jnp.maximum(i - 1, 0) if late else jnp.minimum(i, steps - 1), 0))

    def whole(a):
        return pl.BlockSpec(a.shape, lambda i: (0,) * len(a.shape))

    outs = [
        ((total, width), BF16, rows_of(width)),
        ((total, width), BF16, rows_of(width)),
        ((total, inners), BF16, rows_of(inners, True)),
        ((total, width), BF16, rows_of(width, True)),
        ((6, 8, width), F32, pl.BlockSpec((6, 8, width), lambda i: (0, 0, 0))),
        ((8, inners), F32, pl.BlockSpec((8, inners), lambda i: (0, 0))),
    ]
    return pl.pallas_call(
        functools.partial(early_kernel, ff_chunk=ff_chunk),
        grid=(steps + 1,),
        in_specs=[whole(gcls), whole(ccls), rows_of(width), rows_of(width), rows_of(width), rows_of(LANES), rows_of(inners, True),
                  rows_of(width, True), rows_of(LANES, True), any_spec, any_spec, whole(gains)],
        out_specs=[o[2] for o in outs],
        out_shape=[jax.ShapeDtypeStruct(o[0], o[1]) for o in outs],
        scratch_shapes=[pltpu.VMEM(w_up.shape[1:], BF16), pltpu.VMEM(w_down.shape[1:], BF16), pltpu.VMEM((tile, width), F32), pltpu.SemaphoreType.DMA((2, inners // ff_chunk))],
        compiler_params=pltpu.CompilerParams(vmem_limit_bytes=60 * 2**20),
        name="early_backward",
    )(gcls, ccls, cot, y, n2, r2, slope, n1, r1, w_up, w_down, gains)

RING = 4
CROSS_UNITS = 3
SEG_UNITS = 12
UNITS = CROSS_UNITS + SEG_UNITS
CHAINS = UNITS + 1
PART = 48
GROUPS = 3
EARLY = 9
TILES = 4
GROUP_STEPS = TILES + 1
LAST_AT = EARLY + GROUPS * GROUP_STEPS
STEPS = LAST_AT + TILES


CHAIN_TABLE = (
    ("e", 1, 4, 6, 8, 13), ("a", 1, 4, 6, 8, 13), ("e", 2, 6, 8, 11, 16), ("a", 2, 6, 8, 11, 16),
    ("e", 4, 8, 11, 14, 19), ("a", 4, 8, 11, 14, 19), ("b", 6, 11, 14, 17, 21), ("a", 6, 11, 14, 17, 21),
    ("b", 8, 14, 17, 20, 24), ("a", 8, 14, 17, 20, 24), ("b", 11, 17, 20, 23, 26), ("a", 11, 17, 20, 23, 26),
    ("b", 14, 18, 21, 23, 26), ("a", 19, 23, 25, 27, 28), ("b", 24, 26, 27, 28, 28), ("a", 24, 26, 27, 28, 28),
)
SMALL_MOMENTS = (1, 4, 6, 8, 10, 12)
SMALL_LATE = (23, 24, 25, 26, 27, 28)
WAYS = "".join(row[0] for row in CHAIN_TABLE)


def comm_schedule():
    table = {s: [] for s in range(STEPS + 1)}
    for n, (_, *moments) in enumerate(CHAIN_TABLE):
        for action, at in zip(("send", "two", "three", "final", "out"), moments):
            if action != "send" or n not in (1, 3):
                table[at].append((action, n))
    for n, at in ((CROSS_UNITS + EARLY - 1, EARLY + 1), (UNITS - 3, 14), (UNITS - 2, 19), (UNITS - 1, 24)):
        table[at].append(("one", n))
    for d in range(6):
        table[SMALL_MOMENTS[d]].append(("small", d))
        table[SMALL_LATE[d]].append(("late", d))
    order = ("small", "late", "one", "out", "final", "three", "two", "send")
    for at in range(STEPS):
        table[at].sort(key=lambda item: (order.index(item[0]), item[1]))
    rank = {"two": 1, "three": 2, "final": 3, "out": 4}
    table[STEPS].sort(key=lambda item: (rank[item[0]] if item[0] != "late" else item[1] - 2.5, item[1]))
    return table


def add_low(a, b):
    return (a.astype(F32) + b.astype(F32)).astype(BF16)


def late_kernel(
    firstt, ginner, hiddent, gsecond, mixedt, gbranch, xt, qkv, probs, wqkv_hbm, wout_hbm,
    cfirstt, cginner, chiddent, cgsecond, cmixedt, cgbranch, cxt, cgqkv,
    sums, bsums, csums, cbsums, gpos,
    dqkv_ref, dout_ref, dup_ref, ddown_ref, small_ref, gx_ref,
    aslot, bslot, qkv_slot, probs_slot, gbranch_slot, gx_slot, wqkv, wout, fold, csend, crecv, keep, r1, r2, r3, rf, rc, acc, racc, late_acc, late_racc,
    load_sems, tile_sems, store_sems, weight_sems, csend_sems, crecv_sems, s1_sems, q1_sems, s2_sems, q2_sems, s3_sems, q3_sems, sf_sems, qf_sems, sa_sems, qa_sems,
    *, share,
):
    width = bslot.shape[-1]
    line, z = lax.axis_index("row"), lax.axis_index("seg")
    y, x, c = line // 4, (line // 2) % 2, line % 2
    zh, zl = z // 2, z % 2
    flip_c = (y * 4 + x * 2 + 1 - c, z)
    flip_x = (y * 4 + (1 - x) * 2 + c, z)
    flip_y = ((1 - y) * 4 + x * 2 + c, z)
    flip_zl = (line, zh * 2 + 1 - zl)
    flip_zh = (line, (1 - zh) * 2 + zl)
    flip_yzh = ((1 - y) * 4 + x * 2 + c, (1 - zh) * 2 + zl)
    barrier = pltpu.get_barrier_semaphore()
    for peer in (flip_c, flip_x, flip_y, flip_zl, flip_zh, flip_yzh):
        pl.semaphore_signal(barrier, inc=1, device_id=peer, device_id_type=MESH)

    tile = gbranch_slot.shape[1]
    segs = tile // SEGLEN

    def a_slot(u):
        return jnp.where((u < 4) | (u >= EARLY), 0, (u + 1) % 2)

    def b_slot(u):
        return jnp.where(u < 4, u % 2, jnp.where(u < EARLY, u // 8, u - EARLY))

    def load_unit(u, do):
        def act(src, dst, side):
            getattr(pltpu.make_async_copy(src, dst, load_sems.at[side]), do)()

        def columns(ref, j):
            return ref.at[:, pl.ds(pl.multiple_of(j * width, width), width)]

        @pl.when(u == 0)
        def _():
            act(firstt, aslot.at[0], 0)

        @pl.when(u < 4)
        def _():
            act(columns(ginner, u), bslot.at[u % 2], 1)

        @pl.when((u >= 4) & (u < 8))
        def _():
            act(hiddent.at[:, :, :, u - 4], aslot.at[(u + 1) % 2], 0)

        @pl.when(u == 4)
        def _():
            act(gsecond, bslot.at[0], 1)

        @pl.when(u == 8)
        def _():
            act(mixedt, aslot.at[1], 0)
            act(gbranch, bslot.at[1], 1)

        @pl.when(u == EARLY)
        def _():
            act(xt, aslot.at[0], 0)

    def tile_rows(i):
        return pl.ds(pl.multiple_of(i * tile, tile), tile)

    def load_tile(j, i, slot, late, do):
        copies = [pltpu.make_async_copy(gbranch.at[tile_rows(i)], gbranch_slot.at[slot], tile_sems.at[slot, 0])]
        if not late:
            copies.append(pltpu.make_async_copy(qkv.at[j, tile_rows(i)], qkv_slot.at[slot], tile_sems.at[slot, 1]))
            copies.append(
                pltpu.make_async_copy(probs.at[pl.ds(i * segs, segs), pl.ds(2 * j, 2)], probs_slot.at[slot], tile_sems.at[slot, 2])
            )
        for copy in copies:
            getattr(copy, do)()

    def place(s):
        group = (s - EARLY) // GROUP_STEPS
        return group, (s - EARLY) % GROUP_STEPS

    def load(s, do):
        group, part = place(s)
        inside = (s >= EARLY) & (s < LAST_AT)

        @pl.when(s < EARLY)
        def _():
            load_unit(s, do)

        @pl.when(inside & (part < TILES))
        def _():
            load_tile(group, part, part % 2, False, do)

        @pl.when(inside & (part == TILES))
        def _():
            load_unit(EARLY + group, do)

        @pl.when(s >= LAST_AT)
        def _():
            load_tile(0, s - LAST_AT, (s - LAST_AT) % 2, True, do)

    def store_gx(i):
        return pltpu.make_async_copy(gx_slot.at[i % 2], gx_ref.at[tile_rows(i)], store_sems.at[i % 2])

    weight_copies = [pltpu.make_async_copy(wout_hbm.at[0], wout, weight_sems.at[0])]
    for j in range(GROUPS):
        for part in range(3):
            weight_copies.append(
                pltpu.make_async_copy(
                    wqkv_hbm.at[0, :, pl.ds(part * width + j * GROUP, GROUP)],
                    wqkv.at[j, :, pl.ds(part * GROUP, GROUP)],
                    weight_sems.at[1 + 3 * j + part],
                )
            )
    load(0, "start")

    def remote(src, dst, send_sem, recv_sem, peer):
        return pltpu.make_async_remote_copy(
            src_ref=src, dst_ref=dst, send_sem=send_sem, recv_sem=recv_sem, device_id=peer, device_id_type=MESH
        )

    ways = {
        "a": ((x, zl, zh), (flip_x, flip_zl, flip_zh)),
        "b": ((y, x, zl), (flip_y, flip_x, flip_zl)),
        "c": ((zl, x, zh), (flip_zl, flip_x, flip_zh)),
        "e": ((y, x), (flip_y, flip_x)),
        "f": ((x,), (flip_x,)),
    }

    def way(n):
        return ways[WAYS[n]]

    def among(n, kinds, chains):
        return sum((jnp.asarray(n == k).astype(jnp.int32) for k in chains if WAYS[k] in kinds), jnp.int32(0))

    def block_place(in_b, in_c, far, high, low):
        at = {"a": far * 4 + low * 2 + high, "b": high * 4 + far * 2 + low, "c": low * 4 + far * 2 + high}
        return at["a"] + in_b * (at["b"] - at["a"]) + in_c * (at["c"] - at["a"])

    def core_copy(n):
        slot = n % RING
        return remote(csend.at[slot], crecv.at[slot], csend_sems.at[slot], crecv_sems.at[slot], flip_c)

    def part_of(n):
        if n >= UNITS - 1:
            half = width // 2
            return UNITS - 1, slice((n - UNITS + 1) * half, (n - UNITS + 2) * half)
        return n, slice(0, width)

    def copy_one(n):
        (b1, *_), (peer, *_) = way(n)
        m, cols = part_of(n)
        return remote(keep.at[m, pl.ds(4 * (1 - b1), 4), :, cols], r1.at[m, :, :, cols], s1_sems.at[n], q1_sems.at[n], peer)

    def copy_two(n):
        (b1, b2, *_), (_, peer, *_) = way(n)
        m, cols = part_of(n)
        return remote(keep.at[m, pl.ds(4 * b1 + 2 * (1 - b2), 2), :, cols], r2.at[m, :, :, cols], s2_sems.at[n], q2_sems.at[n], peer)

    def copy_three(n):
        (b1, b2, b3), (_, _, peer) = way(n)
        m, cols = part_of(n)
        return remote(keep.at[m, 4 * b1 + 2 * b2 + 1 - b3, :, cols], r3.at[m, :, cols], s3_sems.at[n], q3_sems.at[n], peer)

    def own_block(n):
        (b1, b2, b3), _ = way(n)
        m, cols = part_of(n)
        return keep.at[m, 4 * b1 + 2 * b2 + b3, :, cols]

    def step_one(n):
        core_copy(n).wait_recv()
        keep[n] = add_low(keep[n], crecv[n % RING])

    def step_two(n):
        (b1, *_), _ = way(n)
        copy_one(n).wait()
        m, cols = part_of(n)
        at = pl.ds(4 * b1, 4)
        keep[m, at, :, cols] = add_low(keep[m, at, :, cols], r1[m, :, :, cols])
        if WAYS[n] != "f":
            copy_two(n).start()

    def step_three(n):
        if WAYS[n] == "f":
            return
        (b1, b2, *_), _ = way(n)
        copy_two(n).wait()
        m, cols = part_of(n)
        at = pl.ds(4 * b1 + 2 * b2, 2)
        keep[m, at, :, cols] = add_low(keep[m, at, :, cols], r2[m, :, :, cols])
        if WAYS[n] != "e":
            copy_three(n).start()

    def final_to(n, slot, peer):
        m, cols = part_of(n)
        return remote(own_block(n), rf.at[m, slot, :, cols], sf_sems.at[n], qf_sems.at[n, slot], peer)

    def sends_final(n, act):
        if WAYS[n] != "b":
            @pl.when(y == 1)
            def _():
                act(final_to(n, 0, flip_y))
            return

        @pl.when((y == 1) & (zh == 1))
        def _():
            act(final_to(n, 0, flip_y))

        @pl.when((y == 0) & (zh == 1))
        def _():
            act(final_to(n, 0, flip_zh))

        @pl.when((y == 1) & (zh == 0))
        def _():
            act(final_to(n, 1, flip_yzh))

    def cross_final(n):
        src = keep.at[n, pl.ds(2 * x, 2)] if WAYS[n] == "e" else keep.at[n, pl.ds(4 * x, 4)]
        count = 2 if WAYS[n] == "e" else 4
        return remote(src, rc.at[n // 2, pl.ds(0, count)], sf_sems.at[n], qf_sems.at[n, 0], flip_y)

    def step_final(n):
        if WAYS[n] in "ef":
            @pl.when(y == 0)
            def _():
                cross_final(n).start()
            return
        copy_three(n).wait()
        (b1, b2, b3), _ = way(n)
        m, cols = part_of(n)
        at = 4 * b1 + 2 * b2 + b3
        keep[m, at, :, cols] = add_low(keep[m, at, :, cols], r3[m, :, cols])
        sends_final(n, lambda copy: copy.start())

    def put(u, value, cols=slice(0, 16 * PART)):
        def columns(j):
            return pl.ds(pl.multiple_of(j * width, width), width)

        @pl.when(u < 4)
        def _():
            dup_ref[:, columns(u)] = value

        @pl.when((u >= 4) & (u < 8))
        def _():
            ddown_ref[pl.ds(pl.multiple_of((u - 4) * PART, PART), PART), :] = value

        @pl.when(u == 8)
        def _():
            dout_ref[...] = value

        for j in range(GROUPS):
            @pl.when(u == EARLY + j)
            def _(j=j):
                for part in range(3):
                    first, last = max(part * GROUP, cols.start), min((part + 1) * GROUP, cols.stop)
                    if first < last:
                        to = part * (width - GROUP) + j * GROUP
                        dqkv_ref[:, to + first : to + last] = value[:, first - cols.start : last - cols.start]

    def step_out(n):
        if WAYS[n] in "ef":
            return cross_step_out(n)
        m, cols = part_of(n)
        u = n // 2 if n < 2 * CROSS_UNITS else m - CROSS_UNITS
        sends_final(n, lambda copy: copy.wait_send())

        @pl.when(y == 0)
        def _():
            final_to(n, 0, flip_y).wait_recv()
            straight = (zh == 0) if WAYS[n] == "b" else (y == 0)

            @pl.when(straight)
            def _():
                put(u, own_block(n)[...].astype(F32) + rf[m, 0, :, cols].astype(F32), cols)

            if WAYS[n] == "b":
                @pl.when(zh == 1)
                def _():
                    final_to(n, 1, flip_y).wait_recv()
                    put(u, rf[m, 0, :, cols].astype(F32) + rf[m, 1, :, cols].astype(F32), cols)

    def cross_step_out(n):
        @pl.when(y == 0)
        def _():
            cross_final(n).wait_send()

        @pl.when(y == 1)
        def _():
            cross_final(n).wait_recv()
            for sub in range(4):
                if WAYS[n] == "f":
                    block = keep[n, 4 * x + sub].astype(F32) + rc[n // 2, sub].astype(F32)
                else:
                    block = (rc[n // 2, sub] if sub < 2 else keep[n, 4 + 2 * x + sub - 2]).astype(F32)
                put(2 * n + sub, block)

    small_peers = (flip_c, flip_x, flip_y, flip_zl, flip_zh)

    rounds = ((acc, racc), (late_acc, late_racc))

    def small_copy(late, d):
        own, other = rounds[late]
        return remote(own.at[d], other.at[d], sa_sems.at[late, d], qa_sems.at[late, d], small_peers[d])

    def small_step(late, d):
        own, other = rounds[late]
        small_copy(late, d).wait()
        own[d + 1] = own[d] + other[d]
        if d + 1 < len(small_peers):
            small_copy(late, d + 1).start()
        elif late:
            small_ref[0:8, :] = acc[d + 1, 0:8, :] + own[d + 1]
            small_ref[8:32, :] = acc[d + 1, 8:32, :]

    seg_rows = [jnp.sum(sums[i], axis=0, keepdims=True) for i in range(6)]
    seg_up = jnp.sum(bsums[...], axis=0, keepdims=True)
    order = (6, 7, 5, 4, 2, 1)
    for i, row in enumerate(order):
        if row < 6:
            acc[0, i : i + 1, :] = seg_rows[row]
        acc[0, 6 + i : 7 + i, :] = csums[row : row + 1, :] * share
    for i, row in enumerate((3, 0)):
        acc[0, 12 + i : 13 + i, :] = seg_rows[row]
        acc[0, 14 + i : 15 + i, :] = csums[row : row + 1, :] * share
    for i in range(4):
        acc[0, 16 + i : 17 + i, :] = seg_up[:, i * width : (i + 1) * width]
        acc[0, 20 + i : 21 + i, :] = cbsums[:, i * width : (i + 1) * width] * share
    acc[0, 0:2, :] = jnp.zeros_like(acc[0, 0:2, :])
    acc[0, 24:32, :] = gpos[...] * share
    late_acc[0] = jnp.zeros_like(late_acc[0])

    def cross_unit(n, parts):
        if n >= RING:
            core_copy(n).wait_send()
        for rel in (1, 0):
            core = c if rel == 0 else 1 - c
            for sub, (left, right) in enumerate(parts):
                for far in range(2):
                    value = mm(left(far, core), right).astype(BF16)
                    at = (sub // 2) * 4 + far * 2 + sub % 2 if WAYS[n] == "e" else far * 4 + sub
                    if rel == 1:
                        csend[n % RING, at] = value
                    else:
                        keep[n, at] = value
            if rel == 1:
                if n == 0:
                    pl.semaphore_wait(barrier, 6)
                core_copy(n).start()

    def plain(ref):
        return lambda far, core: ref[far, core, z]

    def nested(ref, j):
        return lambda far, core: ref[far, core, z, j]

    def cut(ref, j):
        return ref[:, j * width : (j + 1) * width]

    def cut_group(ref, j):
        return jnp.concatenate([ref[:, part * width + j * GROUP : part * width + (j + 1) * GROUP] for part in range(3)], axis=1)

    cross_parts = (
        lambda: [(plain(cfirstt), cut(cginner, j)) for j in range(4)],
        lambda: [(nested(chiddent, j), cgsecond[...]) for j in range(4)],
        lambda: [(plain(cmixedt), cgbranch[...])] + [(plain(cxt), cut_group(cgqkv, j)) for j in range(GROUPS)],
    )

    def compute(u):
        n = u + CROSS_UNITS - jnp.maximum(CROSS_UNITS - 1 - u, 0)
        @pl.when(n >= RING)
        def _():
            core_copy(n).wait_send()

        sides = []
        for side in range(2):
            chains, chain = tuple(range(UNITS - 1)) + (UNITS - 1 + side,), n + side * (n // (UNITS - 1))
            sides.append((among(chain, "b", chains), among(chain, "c", chains)))
        right = bslot[b_slot(u)]
        for rel in (1, 0):
            core = c if rel == 0 else 1 - c
            left = aslot[a_slot(u), :, core].reshape(8 * PART, -1)
            value = mm(left, right).astype(BF16)
            for far in range(2):
                for part in range(4):
                    block = value[(far * 4 + part) * PART : (far * 4 + part + 1) * PART]
                    for side in range(2):
                        at = block_place(*sides[side], far, part // 2, part % 2)
                        cols = slice(side * width // 2, (side + 1) * width // 2)
                        if rel == 1:
                            csend[n % RING, at, :, cols] = block[:, cols]
                        else:
                            keep[n, at, :, cols] = block[:, cols]
            if rel == 1:
                core_copy(n).start()

        @pl.when(n < CROSS_UNITS + EARLY)
        def _():
            step_one(n - 1)

    def attention_tile(j, i):
        slot = i % 2
        out_rows = pl.ds(pl.multiple_of(j * GROUP, GROUP), GROUP)
        g_mixed = mm_nt(gbranch_slot[slot], wout[out_rows, :]).astype(BF16)
        items = [(seg, half) for seg in range(segs) for half in range(2)]
        at = [slice(seg * SEGLEN, (seg + 1) * SEGLEN) for seg, _ in items]
        lanes = [pair_lanes(half) for _, half in items]
        to = [pl.ds(pl.multiple_of(i * tile + seg * SEGLEN, SEGLEN), SEGLEN) for seg, _ in items]
        every = range(len(items))
        g_out = [stack_heads(g_mixed[at[e], lanes[e][0]]) for e in every]
        g_p = [mm_nt(qkv_slot[slot, at[e], lanes[e][2]], g_out[e]) for e in every]
        g_v = [mm(probs_slot[slot, seg, half], g_out[e]) for e, (seg, half) in enumerate(items)]
        g_s = []
        for e, (seg, half) in enumerate(items):
            p = probs_slot[slot, seg, half].astype(F32)
            g_s.append((p * (g_p[e] - jnp.sum(g_p[e] * p, axis=0, keepdims=True))).astype(BF16))
        g_k = [mm(g_s[e], stack_heads(qkv_slot[slot, at[e], lanes[e][0]] * HDIM**-0.5)) for e in every]
        g_st = [jnp.concatenate([g_s[e][:, :SEGLEN].T, g_s[e][:, SEGLEN:].T], axis=1) for e in every]
        g_q = [mm(g_st[e], stack_heads(qkv_slot[slot, at[e], lanes[e][1]])) * HDIM**-0.5 for e in every]
        for e in every:
            for part, value in enumerate((g_q[e], g_k[e], g_v[e])):
                value = value.astype(BF16)
                bslot[j, to[e], lanes[e][part]] = value
                if part != 1:
                    fold[part // 2, j, :, lanes[e][0]] += fold_rows(value.astype(F32))

    def last_tile(i):
        slot = i % 2

        @pl.when(i >= 2)
        def _():
            store_gx(i - 2).wait()

        total = gbranch_slot[slot].astype(F32)
        for j in range(GROUPS):
            total = total + mm_nt(bslot[j, tile_rows(i), :], wqkv[j])
        gx_slot[slot] = total.astype(BF16)
        store_gx(i).start()

    def run(action, n):
        if action in ("small", "late"):
            late = int(action == "late")
            if late and n == 0:
                for row in range(2):
                    for j in range(GROUPS):
                        late_acc[0, row : row + 1, j * GROUP : (j + 1) * GROUP] = jnp.sum(fold[row, j], axis=0, keepdims=True)
            if n == 0:
                small_copy(late, 0).start()
            else:
                small_step(late, n - 1)
            return
        {
            "one": step_one, "send": lambda n: copy_one(n).start(), "two": step_two, "three": step_three, "final": step_final, "out": step_out,
        }[action](n)

    schedule = comm_schedule()

    def step(s, carry):
        for at in range(STEPS):
            if schedule[at]:
                @pl.when(s == at)
                def _(at=at):
                    for action, n in schedule[at]:
                        run(action, n)

        @pl.when(s == EARLY)
        def _():
            for copy in weight_copies:
                copy.wait()

        for i in range(1, CROSS_UNITS):
            @pl.when(s == i)
            def _(i=i):
                cross_unit(2 * i, cross_parts[i]())
                step_one(2 * i - 1)
                copy_one(2 * i - 1).start()

        load(s, "wait")

        @pl.when(s == 1)
        def _():
            for copy in weight_copies:
                copy.start()

        @pl.when(s + 1 < STEPS)
        def _():
            load(s + 1, "start")

        group, part = place(s)
        inside = (s >= EARLY) & (s < LAST_AT)
        multiply = (s < EARLY) | (inside & (part == TILES))

        @pl.when(multiply)
        def _():
            compute(jnp.where(s < EARLY, s, EARLY + group))

        @pl.when(inside & (part < TILES))
        def _():
            attention_tile(group, part)

        @pl.when(s >= LAST_AT)
        def _():
            last_tile(s - LAST_AT)

        return carry

    fold[...] = jnp.zeros_like(fold)
    cross_unit(0, cross_parts[0]())
    lax.fori_loop(0, STEPS, step, 0)
    for action, n in schedule[STEPS]:
        run(action, n)
    for i in range(TILES - 2, TILES):
        store_gx(i).wait()
    for n in range(UNITS - RING, UNITS):
        core_copy(n).wait_send()


def late_backward(big, cross, small, attn, share):
    firstt, ginner, hiddent, gsecond, mixedt, gbranch, xt = big
    qkv, probs, w_qkv, w_out = attn
    cfirstt, cginner, chiddent, cgsecond, cmixedt, cgbranch, cxt, cgqkv = cross
    width, depth = firstt.shape
    inners = ginner.shape[1]
    rows = cfirstt.shape[1]
    tile = depth // TILES
    assert width == 16 * PART and inners == 4 * width

    def blocks(a, n):
        return a.reshape((2, 2, 4) + ((n,) if n > 1 else ()) + (PART, a.shape[1]))

    operands = [
        blocks(firstt, 1), ginner, blocks(hiddent, 4), gsecond, blocks(mixedt, 1), gbranch, blocks(xt, 1), qkv, probs, w_qkv, w_out,
        blocks(cfirstt, 1), cginner, blocks(chiddent, 4), cgsecond, blocks(cmixedt, 1), cgbranch, blocks(cxt, 1), cgqkv, *small,
    ]
    vmem = pl.BlockSpec(memory_space=pltpu.VMEM)
    any_spec = pl.BlockSpec(memory_space=pl.ANY)
    outs = [((PART, 3 * width), F32), ((PART, width), F32), ((PART, inners), F32), ((4 * PART, width), F32), ((32, width), F32), ((depth, width), BF16)]
    segs = tile // SEGLEN
    dma = pltpu.SemaphoreType.DMA
    return pl.pallas_call(
        functools.partial(late_kernel, share=share),
        in_specs=[any_spec] * 11 + [vmem] * (len(operands) - 11),
        out_specs=[vmem] * 5 + [any_spec],
        out_shape=[jax.ShapeDtypeStruct(*o) for o in outs],
        scratch_shapes=[
            pltpu.VMEM((2, 2, 2, 4, PART, depth), BF16),
            pltpu.VMEM((GROUPS, depth, width), BF16),
            pltpu.VMEM((2, tile, width), BF16),
            pltpu.VMEM((2, segs, 2, SEGLEN, 2 * SEGLEN), BF16),
            pltpu.VMEM((2, tile, width), BF16),
            pltpu.VMEM((2, tile, width), BF16),
            pltpu.VMEM((GROUPS, width, 3 * GROUP), BF16),
            pltpu.VMEM(w_out.shape[1:], BF16),
            pltpu.VMEM((2, GROUPS, 8, GROUP), F32),
            pltpu.VMEM((RING, 8, PART, width), BF16),
            pltpu.VMEM((RING, 8, PART, width), BF16),
            pltpu.VMEM((UNITS, 8, PART, width), BF16),
            pltpu.VMEM((UNITS, 4, PART, width), BF16),
            pltpu.VMEM((UNITS, 2, PART, width), BF16),
            pltpu.VMEM((UNITS, PART, width), BF16),
            pltpu.VMEM((UNITS, 2, PART, width), BF16),
            pltpu.VMEM((CROSS_UNITS, 4, PART, width), BF16),
            pltpu.VMEM((6, 32, width), F32),
            pltpu.VMEM((5, 32, width), F32),
            pltpu.VMEM((6, 8, width), F32),
            pltpu.VMEM((5, 8, width), F32),
            dma((2,)), dma((2, 3)), dma((2,)), dma((1 + 3 * GROUPS,)), dma((RING,)), dma((RING,)), dma((CHAINS,)), dma((CHAINS,)), dma((CHAINS,)), dma((CHAINS,)),
            dma((CHAINS,)), dma((CHAINS,)), dma((CHAINS,)), dma((CHAINS, 2)), dma((2, 5)), dma((2, 5)),
        ],
        compiler_params=pltpu.CompilerParams(vmem_limit_bytes=63 * 2**20, collective_id=1, has_side_effects=True),
        name="late_backward",
    )(*operands)

def finish_kernel(gx_ref, a_ref, b_ref, c_ref, d_ref, gx_out, a_out, b_out, c_out, d_out):
    gx_out[...] = gx_ref[...].astype(F32)

    @pl.when(pl.program_id(0) == 0)
    def _():
        for src, dst in ((a_ref, a_out), (b_ref, b_out), (c_ref, c_out), (d_ref, d_out)):
            dst[...] = src[...]


def finish(gx, grads, tile=256):
    total, width = gx.shape
    rows = pl.BlockSpec((tile, width), lambda i: (i, 0))
    held = [pl.BlockSpec(g.shape, lambda i: (0, 0)) for g in grads]
    return pl.pallas_call(
        finish_kernel,
        grid=(total // tile,),
        in_specs=[rows] + held,
        out_specs=[rows] + held,
        out_shape=[jax.ShapeDtypeStruct(gx.shape, F32)] + [jax.ShapeDtypeStruct(g.shape, F32) for g in grads],
        name="finish",
    )(gx, *grads)


def small_grads(sums, bsums, csums, cbsums, gpos, bias_sums, cross_share):
    seg_rows = jnp.concatenate([jnp.sum(sums, axis=1), bias_sums])
    cross_rows = csums * cross_share
    order = jnp.array([6, 7, 5, 4, 2, 1])
    biases = jnp.stack([seg_rows[order], cross_rows[order]])
    gains = jnp.stack([seg_rows[jnp.array([3, 0])], cross_rows[jnp.array([3, 0])]])
    ups = jnp.stack([jnp.sum(bsums, axis=0), cbsums[0] * cross_share])
    return biases.reshape(-1), gains.reshape(-1), ups.reshape(-1), (gpos * cross_share).reshape(-1)


def attention_back(qkv, probs, gbranch, w_qkv, w_out):
    total, width = gbranch.shape
    heads = width // HDIM
    segs = total // SEGLEN
    scale = HDIM**-0.5

    def split(a):
        return a.reshape(segs, SEGLEN, heads, HDIM)

    def merge(a):
        return a.reshape(total, width)

    q, k, v = (
        split(qkv[:, :, part * GROUP : (part + 1) * GROUP].transpose(1, 0, 2).reshape(total, width)) for part in range(3)
    )
    p_low = probs.reshape(segs, heads // 2, SEGLEN, 2, SEGLEN).transpose(0, 1, 3, 2, 4).reshape(segs, heads, SEGLEN, SEGLEN)
    g_out = split(mm_nt(gbranch, w_out).astype(BF16))
    p = p_low.astype(F32)
    g_p = jnp.einsum("sqhd,skhd->shkq", g_out, v, preferred_element_type=F32)
    g_s = (p * (g_p - jnp.sum(g_p * p, axis=2, keepdims=True))).astype(BF16)
    g_v = jnp.einsum("shkq,sqhd->skhd", p_low, g_out, preferred_element_type=F32)
    g_k = jnp.einsum("shkq,sqhd->skhd", g_s, q, preferred_element_type=F32) * scale
    g_q = jnp.einsum("shkq,skhd->sqhd", g_s, k, preferred_element_type=F32) * scale
    g_qkv = jnp.concatenate([merge(g_q), merge(g_k), merge(g_v)], axis=1).astype(BF16)
    return g_qkv, gbranch.astype(F32) + mm_nt(g_qkv, w_qkv)


def generic_total(seg_pairs, cross_pairs, small, planes, own):
    axes = ("row", "seg")
    me = lax.axis_index("seg")
    shards = [
        lax.psum_scatter(part, axes, scatter_dimension=0, tiled=True) for part in small_grads(*small, 1.0 / planes)
    ]

    def mine(values, dim):
        return lax.dynamic_slice_in_dim(values, me * own, own, dim)

    big = []
    for at in (6, 4, 0, 2):
        cross = mm(mine(cross_pairs[at], 1), mine(cross_pairs[at + 1], 0))
        both = jnp.concatenate([mm(seg_pairs[at], seg_pairs[at + 1]), cross], axis=0)
        big.append(lax.psum_scatter(both, axes, scatter_dimension=0, tiled=True))
    return big, shards


def per_device(
    tokens, doc_ids, w_qkv, w_out, w_up, w_down, biases, gains, b_up, pos_table, cotangent, *, sizes
):
    lines, planes = sizes
    row_count, local_length, width = tokens.shape
    seg_here = local_length // SEGLEN
    segments = doc_ids.shape[1]
    total = row_count * local_length
    own = row_count * seg_here
    cot = cotangent.reshape(total, width)
    (
        qkv, probs, n1, r1, slope, n2, r2, y, xt, mixedt, firstt, hiddent,
        ccls, gcls, csums, cbsums, gpos, cxt, cmixedt, cfirstt, chiddent, cgqkv, cgbranch, cginner, cgsecond,
    ) = forward_blocks(
        tokens.reshape(total, width), cot, w_qkv, w_out, w_up, w_down, biases, gains, b_up, doc_ids, pos_table, planes,
        tile=256 if planes <= 4 else 128,
    )
    output, gsecond, ginner, gbranch, sums, bsums = early_backward(
        gcls, ccls, cot, y, n2, r2, slope, n1, r1, w_up, w_down, gains
    )
    cross_pairs = (cfirstt, cginner, chiddent, cgsecond, cmixedt, cgbranch, cxt, cgqkv)
    share = 1.0 / planes
    if (lines, planes) == (8, 4) and total == 2048 and width == 16 * PART:
        *grads, small, gx = late_backward(
            (firstt, ginner, hiddent, gsecond, mixedt, gbranch, xt), cross_pairs, (sums, bsums, csums, cbsums, gpos), (qkv, probs, w_qkv, w_out), share
        )
        gx, *grads = finish(gx, grads)
        small = small.reshape(-1)
        index = lax.axis_index("row") * planes + lax.axis_index("seg")
        shards, start = [], 0
        for size in (12 * width, 4 * width, 8 * width, segments * width):
            count = size // (lines * planes)
            shards.append(lax.dynamic_slice_in_dim(small, start + index * count, count, 0))
            start += size
    else:
        gqkv, gx = attention_back(qkv, probs, gbranch, w_qkv[0], w_out[0])
        bias_sums = jnp.stack([jnp.sum(gqkv[:, at : at + width].astype(F32), axis=0) for at in (0, 2 * width)])
        grads, shards = generic_total(
            (firstt, ginner, hiddent, gsecond, mixedt, gbranch, xt, gqkv), cross_pairs, (sums, bsums, csums, cbsums, gpos, bias_sums), planes, own
        )
    return (output.reshape(tokens.shape), gx.reshape(tokens.shape), *grads, *shards)


def solution(mesh):
    sizes = (mesh.shape["row"], mesh.shape["seg"])
    tokens_at = P("row", "seg", None)
    return jax.shard_map(
        functools.partial(per_device, sizes=sizes),
        mesh=mesh,
        in_specs=(tokens_at, P("row", None)) + (P(),) * 8 + (tokens_at,),
        out_specs=(tokens_at, tokens_at) + (P(("row", "seg"), None),) * 4 + (P(("row", "seg")),) * 4,
        check_vma=False,
    )
```

```python
import functools

import jax
import jax.numpy as jnp
from jax import lax
from jax.experimental import pallas as pl
from jax.experimental.pallas import tpu as pltpu
from jax.sharding import PartitionSpec as P


HDIM = 64
SEGLEN = 128
LANES = 128
GROUP = 2 * LANES
EPSILON = 1e-05
GELU_A = 0.7978845608028654
GELU_B = 0.044715 * GELU_A
F32, BF16 = jnp.float32, jnp.bfloat16


def mm(a, b):
    return lax.dot_general(a, b, (((1,), (0,)), ((), ())), preferred_element_type=F32)


def mm_nt(a, b):
    return lax.dot_general(a, b, (((1,), (1,)), ((), ())), preferred_element_type=F32)


def mm_tn(a, b):
    return lax.dot_general(a, b, (((0,), (0,)), ((), ())), preferred_element_type=F32)


def low_lanes(shape):
    return lax.broadcasted_iota(jnp.int32, shape, 1) < HDIM


def stack_heads(pair):
    keep = low_lanes(pair.shape)
    zero = jnp.zeros_like(pair)
    return jnp.concatenate([jnp.where(keep, pair, zero), jnp.where(keep, zero, pair)], axis=0)


def pair_lanes(half):
    return [slice(part * GROUP + half * LANES, part * GROUP + (half + 1) * LANES) for part in range(3)]


def norm_stats(values):
    centered = values - jnp.mean(values, axis=-1, keepdims=True)
    variance = jnp.mean(centered * centered, axis=-1, keepdims=True)
    rstd = lax.rsqrt(variance + EPSILON)
    return centered * rstd, rstd


def gelu_both(u):
    u = u.astype(BF16)
    square = u * u
    bend = GELU_B * square
    half = 0.5 * jnp.tanh(u * (GELU_A + bend))
    gate = half + 0.5
    hidden = u * gate
    slope = gate + hidden * (0.5 - half) * (2.0 * GELU_A + 6.0 * bend)
    return hidden, slope


def norm_back(grad, gain, normal, rstd):
    scaled = grad * gain
    a = jnp.mean(scaled, axis=-1, keepdims=True)
    b = jnp.mean(scaled * normal, axis=-1, keepdims=True)
    return (scaled - a - normal * b) * rstd


OUTS = 13
NEGATIVE = -1000000000.0
MESH = pl.DeviceIdType.MESH


def turned(values):
    return values.astype(F32).T.astype(BF16)


def places(docs, rows, own, kinds):
    lines, segments = docs.shape
    here = own // lines
    count = 2 * rows

    def spread(width, axis):
        return lax.broadcasted_iota(jnp.int32, (count, width), axis)

    def line_of(at):
        return lax.shift_right_logical(at & (own - 1), here.bit_length() - 1)

    in_line = line_of(spread(lines, 0)) == spread(lines, 1)
    row_docs = mm(in_line.astype(BF16), docs.astype(F32).astype(BF16))
    at = spread(segments, 0) & (rows - 1)
    segment = lax.shift_right_logical(at, own.bit_length() - 1) * here + (at & (here - 1))
    across = spread(segments, 1)
    doc = jnp.sum(jnp.where(across == segment, row_docs, 0.0), axis=1, keepdims=True)
    start = jnp.min(jnp.where(row_docs == doc, across.astype(F32), float(segments)), axis=1, keepdims=True)
    place = segment[:, 0:1].astype(F32) - start
    onehot = (place == spread(kinds, 1).astype(F32))[:rows].astype(F32)
    key = doc + segments * line_of(spread(1, 0)).astype(F32)
    keys_across = jnp.broadcast_to(key, (count, max(rows, LANES))).T[:rows]
    return onehot, key[:rows] == keys_across


def cross_part(me, doc_ref, table_ref, bias_ref, gain_ref, bup_ref, outs, writes, weights, copies, scratch, ff_chunk):
    (
        ccls_ref, gcls_ref, sums_ref, bsums_ref, gpos_ref, xt_ref, mixedt_ref, firstt_ref, hiddent_ref,
        gqkv_ref, gbranch_ref, ginner_ref, gsecond_ref,
    ) = outs
    wqkv, wout, wup, wdown = weights
    qkv_ref, probs_ref, mixed_ref, slope_ref, whole_ref = scratch
    own, width = ccls_ref.shape
    rows = whole_ref.shape[1]
    inners = wup.shape[1]
    bias = bias_ref[...].astype(F32)[:, 1]
    gain = gain_ref[1].astype(F32)
    up_bias = bup_ref[1:2, :].astype(F32)
    onehot, allowed = places(doc_ref[...], rows, own, table_ref.shape[0])
    embed = mm(onehot.astype(BF16), table_ref[...])
    x = (whole_ref[0] + embed).astype(BF16)
    gy = whole_ref[1]
    xt_ref[...] = turned(x)
    copies[0].wait()
    for part in range(3):
        cols = slice(part * width, (part + 1) * width)
        out = mm(x, wqkv[:, cols])
        if part == 0:
            out = out + bias[0:1]
        if part == 2:
            out = out + bias[1:2]
        qkv_ref[:, cols] = out.astype(BF16)
    low = low_lanes((rows, LANES))
    pairs = range(width // LANES)
    lanes = [[slice(part * width + pair * LANES, part * width + (pair + 1) * LANES) for part in range(3)] for pair in pairs]
    scores = [
        jnp.where(allowed, mm_nt(qkv_ref[:, at[1]], stack_heads(qkv_ref[:, at[0]] * HDIM**-0.5)), NEGATIVE) for at in lanes
    ]
    pt = []
    for pair in pairs:
        e = jnp.exp(scores[pair] - jnp.max(scores[pair], axis=0, keepdims=True))
        p = e * (1.0 / jnp.sum(e, axis=0, keepdims=True))
        probs_ref[pair] = p
        pt.append(p.T.astype(BF16))
    for pair, at in enumerate(lanes):
        v = qkv_ref[:, at[2]]
        mixed_ref[:, at[0]] = jnp.where(low, mm(pt[pair][:rows], v), mm(pt[pair][rows:], v)).astype(BF16)
    copies[1].wait()
    mixed = mixed_ref[...]
    mixedt_ref[...] = turned(mixed)
    n1, r1 = norm_stats(x.astype(F32) + mm(mixed, wout[...]) + bias[2:3])
    first = (n1 * gain[0:1] + bias[3:4]).astype(BF16)
    firstt_ref[...] = turned(first)
    copies[2].wait()
    copies[3].wait()
    total = first.astype(F32) + bias[4:5]
    chunks = [slice(c * ff_chunk, (c + 1) * ff_chunk) for c in range(inners // ff_chunk)]
    inner = [mm(first, wup[:, cols]) for cols in chunks]
    for c, cols in enumerate(chunks):
        hidden, slope = gelu_both(inner[c] + up_bias[:, cols])
        hidden = hidden.astype(BF16)
        hiddent_ref[cols, :] = turned(hidden)
        slope_ref[:, cols] = slope.astype(F32)
        total = total + mm(hidden, wdown[cols, :])
    n2, r2 = norm_stats(total)
    mine = pl.ds(pl.multiple_of(me * own, own), own)
    whole_ref[0] = (n2 * gain[1:2] + bias[5:6]).astype(BF16).astype(F32)
    ccls_ref[...] = whole_ref[0, mine, :]
    for i in (0, 5, 6, 7, 8):
        writes[i].start()

    def row_sum(values):
        return jnp.sum(values.astype(F32), axis=0, keepdims=True)

    sums_ref[0:1, :] = row_sum(gy * n2)
    sums_ref[1:2, :] = row_sum(gy)
    g_two = norm_back(gy, gain[1:2], n2, r2)
    g_second = g_two.astype(BF16)
    gsecond_ref[...] = g_second
    sums_ref[2:3, :] = row_sum(g_second)
    g_first = g_two
    g_hidden = [mm_nt(g_second, wdown[cols, :]) for cols in chunks]
    for c, cols in enumerate(chunks):
        g_inner = (g_hidden[c] * slope_ref[:, cols]).astype(BF16)
        ginner_ref[:, cols] = g_inner
        bsums_ref[:, cols] = row_sum(g_inner)
        g_first = g_first + mm_nt(g_inner, wup[:, cols])
    sums_ref[3:4, :] = row_sum(g_first * n1)
    sums_ref[4:5, :] = row_sum(g_first)
    g_one = norm_back(g_first, gain[0:1], n1, r1)
    g_branch = g_one.astype(BF16)
    gbranch_ref[...] = g_branch
    sums_ref[5:6, :] = row_sum(g_branch)
    for i in (10, 11, 12):
        writes[i].start()
    g_mixed = mm_nt(g_branch, wout[...]).astype(BF16)
    g_out = [stack_heads(g_mixed[:, at[0]]) for at in lanes]
    g_p = [mm_nt(qkv_ref[:, at[2]], g_out[pair]) for pair, at in enumerate(lanes)]
    g_s, g_st = [], []
    for pair in pairs:
        p = probs_ref[pair]
        g = p * (g_p[pair] - jnp.sum(g_p[pair] * p, axis=0, keepdims=True))
        g_s.append(g.astype(BF16))
        g_st.append(g.T.astype(BF16))
    for pair, at in enumerate(lanes):
        q, k, _ = (qkv_ref[:, part] for part in at)
        g_q = jnp.where(low, mm(g_st[pair][:rows], k), mm(g_st[pair][rows:], k)) * HDIM**-0.5
        gqkv_ref[:, at[0]] = g_q.astype(BF16)
        gqkv_ref[:, at[1]] = mm(g_s[pair], stack_heads(q * HDIM**-0.5)).astype(BF16)
        gqkv_ref[:, at[2]] = mm(probs_ref[pair].astype(BF16), g_out[pair]).astype(BF16)
    g_qkv = gqkv_ref[...]
    sums_ref[6:7, :] = row_sum(g_qkv[:, :width])
    sums_ref[7:8, :] = row_sum(g_qkv[:, 2 * width :])
    g_x = g_one + mm_nt(g_qkv, wqkv[...])
    whole_ref[1] = g_x
    gcls_ref[...] = whole_ref[1, mine, :]
    gpos_ref[...] = lax.dot_general(onehot, g_x, (((0,), (0,)), ((), ())), preferred_element_type=F32, precision=lax.Precision.HIGHEST)
    for i in (1, 2, 3, 4, 9):
        writes[i].start()
    for write in writes:
        write.wait()


def forward_kernel(
    x_ref, wqkv_hbm, wout_hbm, wup_hbm, wdown_hbm, cot_hbm, bias_ref, gain_ref, bup_ref, doc_ref, table_ref,
    qkv_ref, probs_ref, n1_ref, r1_ref, slope_ref, n2_ref, r2_ref, y_ref, xt_ref, mixedt_ref, firstt_ref, hiddent_ref,
    *refs, ff_chunk, devices,
):
    homes, outs, refs = refs[:OUTS], refs[OUTS : 2 * OUTS], refs[2 * OUTS :]
    wqkv, wout, wup, wdown, mixed_ref, first_ref, sems, cls_ref, cot_rows, cot_low, packed, gathered = refs[:12]
    cross_weights, cross_scratch = refs[12:16], refs[16:21]
    cross_sems, out_sems, cot_sems, send_sems, recv_sems = refs[21:]
    step = pl.program_id(0)
    last = pl.num_programs(0) - 1
    rows, width = x_ref.shape
    parts = [slice(part * width, (part + 1) * width) for part in range(3)]
    part_copies = [pltpu.make_async_copy(wqkv_hbm.at[0, :, cols], wqkv.at[:, cols], sems.at[3 + i]) for i, cols in enumerate(parts)]
    copies = part_copies + [
        pltpu.make_async_copy(src.at[0], dst, sems.at[i])
        for i, (src, dst) in enumerate(((wout_hbm, wout), (wup_hbm, wup), (wdown_hbm, wdown)))
    ]

    own = cls_ref.shape[0]
    line, me = lax.axis_index("row"), lax.axis_index("seg")
    peers = [(line, lax.rem(me + hop, devices)) for hop in range(1, devices)]
    cot_copies = [
        pltpu.make_async_copy(cot_hbm.at[pl.ds(i * SEGLEN, 16)], cot_rows.at[i], cot_sems.at[i]) for i in range(own)
    ]
    cross_copies = [
        pltpu.make_async_copy(src.at[1], dst, cross_sems.at[i])
        for i, (src, dst) in enumerate(zip((wqkv_hbm, wout_hbm, wup_hbm, wdown_hbm), cross_weights))
    ]
    writes = [pltpu.make_async_copy(src, dst, out_sems.at[i]) for i, (src, dst) in enumerate(zip(outs, homes))]
    barrier = pltpu.get_barrier_semaphore()

    def sends(kind):
        return [
            pltpu.make_async_remote_copy(
                src_ref=packed.at[kind], dst_ref=gathered.at[kind, hop + 1], send_sem=send_sems.at[kind, hop],
                recv_sem=recv_sems.at[kind, hop], device_id=peer, device_id_type=MESH,
            )
            for hop, peer in enumerate(peers)
        ]

    def arrived(kind, whole_ref):
        for send in sends(kind):
            send.wait()
        gathered[kind, 0] = packed[kind]
        for hop in range(devices):
            rows_at = pl.ds(pl.multiple_of(lax.rem(me - hop + devices, devices) * own, own), own)
            whole_ref[1 - kind, rows_at, :] = gathered[kind, hop].astype(F32)

    @pl.when(step == 0)
    def _():
        for peer in peers:
            pl.semaphore_signal(barrier, inc=1, device_id=peer, device_id_type=MESH)
        for copy in copies[:4]:
            copy.start()

    @pl.when(step == 1)
    def _():
        copies[4].wait()
        copies[5].wait()
        for copy in cot_copies + cross_copies:
            copy.start()

    @pl.when(step == 2)
    def _():
        for i, copy in enumerate(cot_copies):
            copy.wait()
            cot_low[i : i + 1, :] = cot_rows[i, 0:8, :].astype(F32)[0:1]
        packed[0] = cot_low[...].astype(BF16)
        pl.semaphore_wait(barrier, devices - 1)
        for send in sends(0):
            send.start()

    bias = bias_ref[...].astype(F32)[:, 0]
    gain = gain_ref[0].astype(F32)
    up_bias = bup_ref[0:1, :].astype(F32)
    inners = wup.shape[1]
    chunks = [slice(c * ff_chunk, (c + 1) * ff_chunk) for c in range(inners // ff_chunk)]
    items = [(seg, pair) for seg in range(rows // SEGLEN) for pair in range(width // LANES)]
    every = range(len(items))
    at = [slice(seg * SEGLEN, (seg + 1) * SEGLEN) for seg, _ in items]

    def front(state, loading):
        def project_part(part):
            if loading:
                copies[part].wait()
                if part == 0:
                    copies[4].start()
                    copies[5].start()
            x = x_ref[...]
            out = mm(x, wqkv[:, part * width : (part + 1) * width])
            if part == 0:
                out = out + bias[0:1]
            if part == 2:
                out = out + bias[1:2]
            out = out.astype(BF16)
            for group in range(width // GROUP):
                qkv_ref[group, :, part * GROUP : (part + 1) * GROUP] = out[:, group * GROUP : (group + 1) * GROUP]

        def piece(e, part):
            pair = items[e][1]
            return qkv_ref[pair // 2, at[e], pair_lanes(pair % 2)[part]]

        def scores():
            xt_ref[...] = x_ref[...].T
            state["scores"] = [mm_nt(piece(e, 1), stack_heads(piece(e, 0) * HDIM**-0.5)) for e in every]

        def softmax(part):
            for e in every[part :: 2]:
                score = state["scores"][e]
                ex = jnp.exp(score - jnp.max(score, axis=0, keepdims=True))
                p = (ex * (1.0 / jnp.sum(ex, axis=0, keepdims=True))).astype(BF16)
                probs_ref[items[e][0], items[e][1]] = p
                state[e] = jnp.concatenate([p[:, :SEGLEN].T, p[:, SEGLEN:].T], axis=1)

        def mix():
            for e, (_, pair) in enumerate(items):
                mixed_ref[at[e], pair * LANES : (pair + 1) * LANES] = mm(state[e], stack_heads(piece(e, 2))).astype(BF16)

        def project_out():
            if loading:
                copies[3].wait()
            mixed = mixed_ref[...]
            mixedt_ref[...] = mixed.T
            state["resid"] = x_ref[...].astype(F32) + mm(mixed, wout[...]) + bias[2:3]

        def norm():
            n1, r1 = norm_stats(state["resid"])
            n1_ref[...] = n1.astype(BF16)
            r1_ref[...] = jnp.broadcast_to(r1, r1_ref.shape)
            first = (n1 * gain[0:1] + bias[3:4]).astype(BF16)
            firstt_ref[...] = first.T
            state["first"] = first

        return [lambda part=part: project_part(part) for part in range(3)] + [scores, lambda: softmax(0), lambda: softmax(1), mix, project_out, norm]

    def back(state):
        first = first_ref[...]
        state["total"] = first.astype(F32) + bias[4:5]

        def up(c):
            state["inner", c] = mm(first, wup[:, chunks[c]])

        def gelu(c):
            cols = chunks[c]
            hidden, slope = gelu_both(state["inner", c] + up_bias[:, cols])
            hidden = hidden.astype(BF16)
            hiddent_ref[cols, :] = hidden.T
            slope_ref[:, cols] = slope.astype(BF16)
            state["hidden", c] = hidden

        def down(c):
            state["total"] = state["total"] + mm(state["hidden", c], wdown[chunks[c], :])

        def norm():
            n2, r2 = norm_stats(state["total"])
            n2_ref[...] = n2.astype(BF16)
            r2_ref[...] = jnp.broadcast_to(r2, r2_ref.shape)
            y = (n2 * gain[1:2] + bias[5:6]).astype(BF16)
            y_ref[...] = y
            segs = rows // SEGLEN
            for seg in range(segs):
                cls_ref[pl.ds((step - 1) * segs + seg, 1), :] = y[seg * SEGLEN : seg * SEGLEN + 8].astype(F32)[0:1]

        pieces = [lambda: up(0)]
        for c in range(len(chunks)):
            if c + 1 < len(chunks):
                pieces.append(lambda c=c: up(c + 1))
            pieces += [lambda c=c: gelu(c), lambda c=c: down(c)]
        return pieces + [norm]

    def run(with_front, with_back):
        state = {}
        lists = ([back(state)] if with_back else []) + ([front(state, not with_back)] if with_front else [])
        turns = sorted((((i + 0.5) / len(pieces), k, i) for k, pieces in enumerate(lists) for i in range(len(pieces))))
        for _, k, i in turns:
            lists[k][i]()
        if with_front:
            first_ref[...] = state["first"]

    @pl.when(step == 0)
    def _():
        run(True, False)

    @pl.when((step > 0) & (step < last))
    def _():
        run(True, True)

    @pl.when(step == last)
    def _():
        run(False, True)
        packed[1] = cls_ref[...].astype(BF16)
        for send in sends(1):
            send.start()
        arrived(0, cross_scratch[-1])
        arrived(1, cross_scratch[-1])
        cross_part(
            me, doc_ref, table_ref, bias_ref, gain_ref, bup_ref, outs, writes,
            cross_weights, cross_copies, cross_scratch, ff_chunk,
        )


def forward_blocks(x, cot, w_qkv, w_out, w_up, w_down, bias, gain, bup, docs, table, devices, tile=256, ff_chunk=768):
    total, width = x.shape
    inners = w_up.shape[-1]
    segs = tile // SEGLEN
    pairs = width // LANES
    any_spec = pl.BlockSpec(memory_space=pl.ANY)

    steps = total // tile

    def rows_of(cols, late):
        return pl.BlockSpec((tile, cols), lambda i: (jnp.maximum(i - 1, 0) if late else jnp.minimum(i, steps - 1), 0))

    def whole(a):
        return pl.BlockSpec(a.shape, lambda i: (0,) * a.ndim)

    def cols_of(rows, late):
        return pl.BlockSpec((rows, tile), lambda i: (0, jnp.maximum(i - 1, 0) if late else jnp.minimum(i, steps - 1)))

    outs = [
        ((width // GROUP, total, 3 * GROUP), BF16, pl.BlockSpec((width // GROUP, tile, 3 * GROUP), lambda i: (0, jnp.minimum(i, steps - 1), 0))),
        ((total // SEGLEN, pairs, SEGLEN, 2 * SEGLEN), BF16, pl.BlockSpec((segs, pairs, SEGLEN, 2 * SEGLEN), lambda i: (jnp.minimum(i, steps - 1), 0, 0, 0))),
        ((total, width), BF16, rows_of(width, False)),
        ((total, LANES), F32, rows_of(LANES, False)),
        ((total, inners), BF16, rows_of(inners, True)),
        ((total, width), BF16, rows_of(width, True)),
        ((total, LANES), F32, rows_of(LANES, True)),
        ((total, width), BF16, rows_of(width, True)),
        ((width, total), BF16, cols_of(width, False)),
        ((width, total), BF16, cols_of(width, False)),
        ((width, total), BF16, cols_of(width, False)),
        ((inners, total), BF16, cols_of(inners, True)),
    ]
    own = total // SEGLEN
    rows = own * devices
    cross_outs = [
        ((own, width), F32), ((own, width), F32), ((8, width), F32), ((1, inners), F32), (table.shape, F32),
        ((width, rows), BF16), ((width, rows), BF16), ((width, rows), BF16), ((inners, rows), BF16),
        ((rows, 3 * width), BF16), ((rows, width), BF16), ((rows, inners), BF16), ((rows, width), BF16),
    ]
    bias = bias.transpose(1, 0, 2)
    dma = pltpu.SemaphoreType.DMA
    return pl.pallas_call(
        functools.partial(forward_kernel, ff_chunk=ff_chunk, devices=devices),
        grid=(steps + 1,),
        in_specs=[rows_of(width, False), any_spec, any_spec, any_spec, any_spec, any_spec]
        + [whole(a) for a in (bias, gain, bup, docs, table)],
        out_specs=[o[2] for o in outs] + [pl.BlockSpec(memory_space=pltpu.HBM)] * OUTS,
        out_shape=[jax.ShapeDtypeStruct(o[0], o[1]) for o in outs + cross_outs],
        scratch_shapes=[pltpu.VMEM(*o) for o in cross_outs]
        + [
            pltpu.VMEM(w_qkv.shape[1:], BF16),
            pltpu.VMEM(w_out.shape[1:], BF16),
            pltpu.VMEM(w_up.shape[1:], BF16),
            pltpu.VMEM(w_down.shape[1:], BF16),
            pltpu.VMEM((tile, width), BF16),
            pltpu.VMEM((tile, width), BF16),
            dma((6,)),
            pltpu.VMEM((own, width), F32),
            pltpu.VMEM((own, 16, width), BF16),
            pltpu.VMEM((own, width), F32),
            pltpu.VMEM((2, own, width), BF16),
            pltpu.VMEM((2, devices, own, width), BF16),
            pltpu.VMEM(w_qkv.shape[1:], BF16),
            pltpu.VMEM(w_out.shape[1:], BF16),
            pltpu.VMEM(w_up.shape[1:], BF16),
            pltpu.VMEM(w_down.shape[1:], BF16),
            pltpu.VMEM((rows, 3 * width), BF16),
            pltpu.VMEM((pairs, rows, 2 * rows), F32),
            pltpu.VMEM((rows, width), BF16),
            pltpu.VMEM((rows, inners), F32),
            pltpu.VMEM((2, rows, width), F32),
            dma((4,)), dma((OUTS,)), dma((own,)), dma((2, devices - 1)), dma((2, devices - 1)),
        ],
        compiler_params=pltpu.CompilerParams(vmem_limit_bytes=63 * 2**20, collective_id=0, has_side_effects=True),
        name="forward_blocks",
    )(x, w_qkv, w_out, w_up, w_down, cot, bias, gain, bup, docs, table)

def fold_rows(values):
    rows, cols = values.shape
    return jnp.sum(values.reshape(rows // 8, 8, cols), axis=0)


def early_kernel(
    gcls_ref, ccls_ref, cot_ref, y_ref, n2_ref, r2_ref, slope_ref, n1_ref, r1_ref, wup_hbm, wdown_hbm, gain_ref,
    out_ref, gsecond_ref, ginner_ref, gbranch_ref, sums_ref, bsums_ref, wup, wdown, two_ref, sems, *, ff_chunk,
):
    step = pl.program_id(0)
    last = pl.num_programs(0) - 1
    copies = [
        pltpu.make_async_copy(src.at[0], dst, sems.at[i]) for i, (src, dst) in enumerate(((wdown_hbm, wdown), (wup_hbm, wup)))
    ]

    @pl.when(step == 0)
    def _():
        for copy in copies:
            copy.start()
        sums_ref[...] = jnp.zeros_like(sums_ref)
        bsums_ref[...] = jnp.zeros_like(bsums_ref)

    @pl.when(step == 1)
    def _():
        for copy in copies:
            copy.wait()

    rows, width = cot_ref.shape
    segs = rows // SEGLEN
    inners = wup.shape[1]
    gain = gain_ref[0].astype(F32)
    chunks = [slice(c * ff_chunk, (c + 1) * ff_chunk) for c in range(inners // ff_chunk)]

    def front(state):
        def gradient():
            place = lax.broadcasted_iota(jnp.int32, (rows, width), 0)
            gy = cot_ref[...].astype(F32)
            y = y_ref[...].astype(F32)
            for seg in range(segs):
                at = pl.ds(step * segs + seg, 1)
                gy = jnp.where(place == seg * SEGLEN, gcls_ref[at, :], gy)
                y = jnp.where(place == seg * SEGLEN, ccls_ref[at, :], y)
            out_ref[...] = y.astype(BF16)
            state["gy"] = gy

        def norm():
            gy = state["gy"]
            n2 = n2_ref[...].astype(F32)
            sums_ref[0] += fold_rows(gy * n2)
            sums_ref[1] += fold_rows(gy)
            state["two"] = norm_back(gy, gain[1:2], n2, r2_ref[:, 0:1])

        def store():
            low = state["two"].astype(BF16)
            gsecond_ref[...] = low
            sums_ref[2] += fold_rows(low.astype(F32))

        return [gradient, norm, store]

    def back(state):
        g_two = two_ref[...]
        g_second = g_two.astype(BF16)
        state["first"] = g_two

        def down(c):
            state["hidden", c] = mm_nt(g_second, wdown[chunks[c], :])

        def slope(c):
            cols = chunks[c]
            g_low = state["hidden", c].astype(BF16) * slope_ref[:, cols]
            ginner_ref[:, cols] = g_low
            bsums_ref[:, cols] += fold_rows(g_low.astype(F32))
            state["inner", c] = g_low

        def up(c):
            state["first"] = state["first"] + mm_nt(state["inner", c], wup[:, chunks[c]])

        def norm():
            g_first = state["first"]
            n1 = n1_ref[...].astype(F32)
            sums_ref[3] += fold_rows(g_first * n1)
            sums_ref[4] += fold_rows(g_first)
            g_branch = norm_back(g_first, gain[0:1], n1, r1_ref[:, 0:1]).astype(BF16)
            gbranch_ref[...] = g_branch
            sums_ref[5] += fold_rows(g_branch.astype(F32))

        pieces = [lambda: down(0)]
        for c in range(len(chunks)):
            if c + 1 < len(chunks):
                pieces.append(lambda c=c: down(c + 1))
            pieces += [lambda c=c: slope(c), lambda c=c: up(c)]
        return pieces + [norm]

    def run(with_front, with_back):
        state = {}
        lists = ([back(state)] if with_back else []) + ([front(state)] if with_front else [])
        turns = sorted((((i + 0.5) / len(pieces), k, i) for k, pieces in enumerate(lists) for i in range(len(pieces))))
        for _, k, i in turns:
            lists[k][i]()
        if with_front:
            two_ref[...] = state["two"]

    @pl.when(step == 0)
    def _():
        run(True, False)

    @pl.when((step > 0) & (step < last))
    def _():
        run(True, True)

    @pl.when(step == last)
    def _():
        run(False, True)


def early_backward(gcls, ccls, cot, y, n2, r2, slope, n1, r1, w_up, w_down, gains, tile=256, ff_chunk=768):
    total, width = cot.shape
    inners = w_up.shape[-1]
    any_spec = pl.BlockSpec(memory_space=pl.ANY)

    steps = total // tile

    def rows_of(cols, late=False):
        return pl.BlockSpec((tile, cols), lambda i: (jnp.maximum(i - 1, 0) if late else jnp.minimum(i, steps - 1), 0))

    def whole(a):
        return pl.BlockSpec(a.shape, lambda i: (0,) * len(a.shape))

    outs = [
        ((total, width), BF16, rows_of(width)),
        ((total, width), BF16, rows_of(width)),
        ((total, inners), BF16, rows_of(inners, True)),
        ((total, width), BF16, rows_of(width, True)),
        ((6, 8, width), F32, pl.BlockSpec((6, 8, width), lambda i: (0, 0, 0))),
        ((8, inners), F32, pl.BlockSpec((8, inners), lambda i: (0, 0))),
    ]
    return pl.pallas_call(
        functools.partial(early_kernel, ff_chunk=ff_chunk),
        grid=(steps + 1,),
        in_specs=[whole(gcls), whole(ccls), rows_of(width), rows_of(width), rows_of(width), rows_of(LANES), rows_of(inners, True),
                  rows_of(width, True), rows_of(LANES, True), any_spec, any_spec, whole(gains)],
        out_specs=[o[2] for o in outs],
        out_shape=[jax.ShapeDtypeStruct(o[0], o[1]) for o in outs],
        scratch_shapes=[pltpu.VMEM(w_up.shape[1:], BF16), pltpu.VMEM(w_down.shape[1:], BF16), pltpu.VMEM((tile, width), F32), pltpu.SemaphoreType.DMA((2,))],
        compiler_params=pltpu.CompilerParams(vmem_limit_bytes=60 * 2**20),
        name="early_backward",
    )(gcls, ccls, cot, y, n2, r2, slope, n1, r1, w_up, w_down, gains)

RING = 4
CROSS_UNITS = 3
SEG_UNITS = 12
UNITS = CROSS_UNITS + SEG_UNITS
CHAINS = UNITS + 1
PART = 48
GROUPS = 3
EARLY = 9
TILES = 4
GROUP_STEPS = TILES + 1
LAST_AT = EARLY + GROUPS * GROUP_STEPS
STEPS = LAST_AT + TILES


CHAIN_TABLE = (
    ("e", 1, 4, 6, 8, 13), ("a", 1, 4, 6, 8, 13), ("e", 2, 6, 8, 11, 16), ("a", 2, 6, 8, 11, 16),
    ("e", 4, 8, 11, 14, 19), ("a", 4, 8, 11, 14, 19), ("b", 6, 11, 14, 17, 21), ("a", 6, 11, 14, 17, 21),
    ("b", 8, 14, 17, 20, 24), ("a", 8, 14, 17, 20, 24), ("b", 11, 17, 20, 23, 26), ("a", 11, 17, 20, 23, 26),
    ("b", 14, 18, 21, 23, 26), ("a", 19, 23, 25, 27, 28), ("b", 24, 26, 27, 28, 28), ("a", 24, 26, 27, 28, 28),
)
SMALL_MOMENTS = (1, 4, 6, 8, 10, 12)
SMALL_LATE = (23, 24, 25, 26, 27, 28)
WAYS = "".join(row[0] for row in CHAIN_TABLE)


def comm_schedule():
    table = {s: [] for s in range(STEPS + 1)}
    for n, (_, *moments) in enumerate(CHAIN_TABLE):
        for action, at in zip(("send", "two", "three", "final", "out"), moments):
            if action != "send" or n not in (1, 3):
                table[at].append((action, n))
    for n, at in ((CROSS_UNITS + EARLY - 1, EARLY + 1), (UNITS - 3, 14), (UNITS - 2, 19), (UNITS - 1, 24)):
        table[at].append(("one", n))
    for d in range(6):
        table[SMALL_MOMENTS[d]].append(("small", d))
        table[SMALL_LATE[d]].append(("late", d))
    order = ("small", "late", "one", "out", "final", "three", "two", "send")
    for at in range(STEPS):
        table[at].sort(key=lambda item: (order.index(item[0]), item[1]))
    rank = {"two": 1, "three": 2, "final": 3, "out": 4}
    table[STEPS].sort(key=lambda item: (rank[item[0]] if item[0] != "late" else item[1] - 2.5, item[1]))
    return table


def add_low(a, b):
    return (a.astype(F32) + b.astype(F32)).astype(BF16)


def late_kernel(
    firstt, ginner, hiddent, gsecond, mixedt, gbranch, xt, qkv, probs, wqkv_hbm, wout_hbm,
    cfirstt, cginner, chiddent, cgsecond, cmixedt, cgbranch, cxt, cgqkv,
    sums, bsums, csums, cbsums, gpos,
    dqkv_ref, dout_ref, dup_ref, ddown_ref, small_ref, gx_ref,
    aslot, bslot, qkv_slot, probs_slot, gbranch_slot, gx_slot, wqkv, wout, fold, csend, crecv, keep, r1, r2, r3, rf, rc, acc, racc, late_acc, late_racc,
    load_sems, tile_sems, store_sems, weight_sems, csend_sems, crecv_sems, s1_sems, q1_sems, s2_sems, q2_sems, s3_sems, q3_sems, sf_sems, qf_sems, sa_sems, qa_sems,
    *, share,
):
    width = bslot.shape[-1]
    line, z = lax.axis_index("row"), lax.axis_index("seg")
    y, x, c = line // 4, (line // 2) % 2, line % 2
    zh, zl = z // 2, z % 2
    flip_c = (y * 4 + x * 2 + 1 - c, z)
    flip_x = (y * 4 + (1 - x) * 2 + c, z)
    flip_y = ((1 - y) * 4 + x * 2 + c, z)
    flip_zl = (line, zh * 2 + 1 - zl)
    flip_zh = (line, (1 - zh) * 2 + zl)
    flip_yzh = ((1 - y) * 4 + x * 2 + c, (1 - zh) * 2 + zl)
    barrier = pltpu.get_barrier_semaphore()
    for peer in (flip_c, flip_x, flip_y, flip_zl, flip_zh, flip_yzh):
        pl.semaphore_signal(barrier, inc=1, device_id=peer, device_id_type=MESH)

    tile = gbranch_slot.shape[1]
    segs = tile // SEGLEN

    def a_slot(u):
        return jnp.where((u < 4) | (u >= EARLY), 0, (u + 1) % 2)

    def b_slot(u):
        return jnp.where(u < 4, u % 2, jnp.where(u < EARLY, u // 8, u - EARLY))

    def load_unit(u, do):
        def act(src, dst, side):
            getattr(pltpu.make_async_copy(src, dst, load_sems.at[side]), do)()

        def columns(ref, j):
            return ref.at[:, pl.ds(pl.multiple_of(j * width, width), width)]

        @pl.when(u == 0)
        def _():
            act(firstt, aslot.at[0], 0)

        @pl.when(u < 4)
        def _():
            act(columns(ginner, u), bslot.at[u % 2], 1)

        @pl.when((u >= 4) & (u < 8))
        def _():
            act(hiddent.at[:, :, :, u - 4], aslot.at[(u + 1) % 2], 0)

        @pl.when(u == 4)
        def _():
            act(gsecond, bslot.at[0], 1)

        @pl.when(u == 8)
        def _():
            act(mixedt, aslot.at[1], 0)
            act(gbranch, bslot.at[1], 1)

        @pl.when(u == EARLY)
        def _():
            act(xt, aslot.at[0], 0)

    def tile_rows(i):
        return pl.ds(pl.multiple_of(i * tile, tile), tile)

    def load_tile(j, i, slot, late, do):
        copies = [pltpu.make_async_copy(gbranch.at[tile_rows(i)], gbranch_slot.at[slot], tile_sems.at[slot, 0])]
        if not late:
            copies.append(pltpu.make_async_copy(qkv.at[j, tile_rows(i)], qkv_slot.at[slot], tile_sems.at[slot, 1]))
            copies.append(
                pltpu.make_async_copy(probs.at[pl.ds(i * segs, segs), pl.ds(2 * j, 2)], probs_slot.at[slot], tile_sems.at[slot, 2])
            )
        for copy in copies:
            getattr(copy, do)()

    def place(s):
        group = (s - EARLY) // GROUP_STEPS
        return group, (s - EARLY) % GROUP_STEPS

    def load(s, do):
        group, part = place(s)
        inside = (s >= EARLY) & (s < LAST_AT)

        @pl.when(s < EARLY)
        def _():
            load_unit(s, do)

        @pl.when(inside & (part < TILES))
        def _():
            load_tile(group, part, part % 2, False, do)

        @pl.when(inside & (part == TILES))
        def _():
            load_unit(EARLY + group, do)

        @pl.when(s >= LAST_AT)
        def _():
            load_tile(0, s - LAST_AT, (s - LAST_AT) % 2, True, do)

    def store_gx(i):
        return pltpu.make_async_copy(gx_slot.at[i % 2], gx_ref.at[tile_rows(i)], store_sems.at[i % 2])

    weight_copies = [pltpu.make_async_copy(wout_hbm.at[0], wout, weight_sems.at[0])]
    for j in range(GROUPS):
        for part in range(3):
            weight_copies.append(
                pltpu.make_async_copy(
                    wqkv_hbm.at[0, :, pl.ds(part * width + j * GROUP, GROUP)],
                    wqkv.at[j, :, pl.ds(part * GROUP, GROUP)],
                    weight_sems.at[1 + 3 * j + part],
                )
            )
    load(0, "start")

    def remote(src, dst, send_sem, recv_sem, peer):
        return pltpu.make_async_remote_copy(
            src_ref=src, dst_ref=dst, send_sem=send_sem, recv_sem=recv_sem, device_id=peer, device_id_type=MESH
        )

    ways = {
        "a": ((x, zl, zh), (flip_x, flip_zl, flip_zh)),
        "b": ((y, x, zl), (flip_y, flip_x, flip_zl)),
        "c": ((zl, x, zh), (flip_zl, flip_x, flip_zh)),
        "e": ((y, x), (flip_y, flip_x)),
        "f": ((x,), (flip_x,)),
    }

    def way(n):
        return ways[WAYS[n]]

    def among(n, kinds, chains):
        return sum((jnp.asarray(n == k).astype(jnp.int32) for k in chains if WAYS[k] in kinds), jnp.int32(0))

    def block_place(in_b, in_c, far, high, low):
        at = {"a": far * 4 + low * 2 + high, "b": high * 4 + far * 2 + low, "c": low * 4 + far * 2 + high}
        return at["a"] + in_b * (at["b"] - at["a"]) + in_c * (at["c"] - at["a"])

    def core_copy(n):
        slot = n % RING
        return remote(csend.at[slot], crecv.at[slot], csend_sems.at[slot], crecv_sems.at[slot], flip_c)

    def part_of(n):
        if n >= UNITS - 1:
            half = width // 2
            return UNITS - 1, slice((n - UNITS + 1) * half, (n - UNITS + 2) * half)
        return n, slice(0, width)

    def copy_one(n):
        (b1, *_), (peer, *_) = way(n)
        m, cols = part_of(n)
        return remote(keep.at[m, pl.ds(4 * (1 - b1), 4), :, cols], r1.at[m, :, :, cols], s1_sems.at[n], q1_sems.at[n], peer)

    def copy_two(n):
        (b1, b2, *_), (_, peer, *_) = way(n)
        m, cols = part_of(n)
        return remote(keep.at[m, pl.ds(4 * b1 + 2 * (1 - b2), 2), :, cols], r2.at[m, :, :, cols], s2_sems.at[n], q2_sems.at[n], peer)

    def copy_three(n):
        (b1, b2, b3), (_, _, peer) = way(n)
        m, cols = part_of(n)
        return remote(keep.at[m, 4 * b1 + 2 * b2 + 1 - b3, :, cols], r3.at[m, :, cols], s3_sems.at[n], q3_sems.at[n], peer)

    def own_block(n):
        (b1, b2, b3), _ = way(n)
        m, cols = part_of(n)
        return keep.at[m, 4 * b1 + 2 * b2 + b3, :, cols]

    def step_one(n):
        core_copy(n).wait_recv()
        keep[n] = add_low(keep[n], crecv[n % RING])

    def step_two(n):
        (b1, *_), _ = way(n)
        copy_one(n).wait()
        m, cols = part_of(n)
        at = pl.ds(4 * b1, 4)
        keep[m, at, :, cols] = add_low(keep[m, at, :, cols], r1[m, :, :, cols])
        if WAYS[n] != "f":
            copy_two(n).start()

    def step_three(n):
        if WAYS[n] == "f":
            return
        (b1, b2, *_), _ = way(n)
        copy_two(n).wait()
        m, cols = part_of(n)
        at = pl.ds(4 * b1 + 2 * b2, 2)
        keep[m, at, :, cols] = add_low(keep[m, at, :, cols], r2[m, :, :, cols])
        if WAYS[n] != "e":
            copy_three(n).start()

    def final_to(n, slot, peer):
        m, cols = part_of(n)
        return remote(own_block(n), rf.at[m, slot, :, cols], sf_sems.at[n], qf_sems.at[n, slot], peer)

    def sends_final(n, act):
        if WAYS[n] != "b":
            @pl.when(y == 1)
            def _():
                act(final_to(n, 0, flip_y))
            return

        @pl.when((y == 1) & (zh == 1))
        def _():
            act(final_to(n, 0, flip_y))

        @pl.when((y == 0) & (zh == 1))
        def _():
            act(final_to(n, 0, flip_zh))

        @pl.when((y == 1) & (zh == 0))
        def _():
            act(final_to(n, 1, flip_yzh))

    def cross_final(n):
        src = keep.at[n, pl.ds(2 * x, 2)] if WAYS[n] == "e" else keep.at[n, pl.ds(4 * x, 4)]
        count = 2 if WAYS[n] == "e" else 4
        return remote(src, rc.at[n // 2, pl.ds(0, count)], sf_sems.at[n], qf_sems.at[n, 0], flip_y)

    def step_final(n):
        if WAYS[n] in "ef":
            @pl.when(y == 0)
            def _():
                cross_final(n).start()
            return
        copy_three(n).wait()
        (b1, b2, b3), _ = way(n)
        m, cols = part_of(n)
        at = 4 * b1 + 2 * b2 + b3
        keep[m, at, :, cols] = add_low(keep[m, at, :, cols], r3[m, :, cols])
        sends_final(n, lambda copy: copy.start())

    def put(u, value, cols=slice(0, 16 * PART)):
        def columns(j):
            return pl.ds(pl.multiple_of(j * width, width), width)

        @pl.when(u < 4)
        def _():
            dup_ref[:, columns(u)] = value

        @pl.when((u >= 4) & (u < 8))
        def _():
            ddown_ref[pl.ds(pl.multiple_of((u - 4) * PART, PART), PART), :] = value

        @pl.when(u == 8)
        def _():
            dout_ref[...] = value

        for j in range(GROUPS):
            @pl.when(u == EARLY + j)
            def _(j=j):
                for part in range(3):
                    first, last = max(part * GROUP, cols.start), min((part + 1) * GROUP, cols.stop)
                    if first < last:
                        to = part * (width - GROUP) + j * GROUP
                        dqkv_ref[:, to + first : to + last] = value[:, first - cols.start : last - cols.start]

    def step_out(n):
        if WAYS[n] in "ef":
            return cross_step_out(n)
        m, cols = part_of(n)
        u = n // 2 if n < 2 * CROSS_UNITS else m - CROSS_UNITS
        sends_final(n, lambda copy: copy.wait_send())

        @pl.when(y == 0)
        def _():
            final_to(n, 0, flip_y).wait_recv()
            straight = (zh == 0) if WAYS[n] == "b" else (y == 0)

            @pl.when(straight)
            def _():
                put(u, own_block(n)[...].astype(F32) + rf[m, 0, :, cols].astype(F32), cols)

            if WAYS[n] == "b":
                @pl.when(zh == 1)
                def _():
                    final_to(n, 1, flip_y).wait_recv()
                    put(u, rf[m, 0, :, cols].astype(F32) + rf[m, 1, :, cols].astype(F32), cols)

    def cross_step_out(n):
        @pl.when(y == 0)
        def _():
            cross_final(n).wait_send()

        @pl.when(y == 1)
        def _():
            cross_final(n).wait_recv()
            for sub in range(4):
                if WAYS[n] == "f":
                    block = keep[n, 4 * x + sub].astype(F32) + rc[n // 2, sub].astype(F32)
                else:
                    block = (rc[n // 2, sub] if sub < 2 else keep[n, 4 + 2 * x + sub - 2]).astype(F32)
                put(2 * n + sub, block)

    small_peers = (flip_c, flip_x, flip_y, flip_zl, flip_zh)

    rounds = ((acc, racc), (late_acc, late_racc))

    def small_copy(late, d):
        own, other = rounds[late]
        return remote(own.at[d], other.at[d], sa_sems.at[late, d], qa_sems.at[late, d], small_peers[d])

    def small_step(late, d):
        own, other = rounds[late]
        small_copy(late, d).wait()
        own[d + 1] = own[d] + other[d]
        if d + 1 < len(small_peers):
            small_copy(late, d + 1).start()
        elif late:
            small_ref[0:8, :] = acc[d + 1, 0:8, :] + own[d + 1]
            small_ref[8:32, :] = acc[d + 1, 8:32, :]

    seg_rows = [jnp.sum(sums[i], axis=0, keepdims=True) for i in range(6)]
    seg_up = jnp.sum(bsums[...], axis=0, keepdims=True)
    order = (6, 7, 5, 4, 2, 1)
    for i, row in enumerate(order):
        if row < 6:
            acc[0, i : i + 1, :] = seg_rows[row]
        acc[0, 6 + i : 7 + i, :] = csums[row : row + 1, :] * share
    for i, row in enumerate((3, 0)):
        acc[0, 12 + i : 13 + i, :] = seg_rows[row]
        acc[0, 14 + i : 15 + i, :] = csums[row : row + 1, :] * share
    for i in range(4):
        acc[0, 16 + i : 17 + i, :] = seg_up[:, i * width : (i + 1) * width]
        acc[0, 20 + i : 21 + i, :] = cbsums[:, i * width : (i + 1) * width] * share
    acc[0, 0:2, :] = jnp.zeros_like(acc[0, 0:2, :])
    acc[0, 24:32, :] = gpos[...] * share
    late_acc[0] = jnp.zeros_like(late_acc[0])

    def cross_unit(n, parts):
        if n >= RING:
            core_copy(n).wait_send()
        for rel in (1, 0):
            core = c if rel == 0 else 1 - c
            for sub, (left, right) in enumerate(parts):
                for far in range(2):
                    value = mm(left(far, core), right).astype(BF16)
                    at = (sub // 2) * 4 + far * 2 + sub % 2 if WAYS[n] == "e" else far * 4 + sub
                    if rel == 1:
                        csend[n % RING, at] = value
                    else:
                        keep[n, at] = value
            if rel == 1:
                if n == 0:
                    pl.semaphore_wait(barrier, 6)
                core_copy(n).start()

    def plain(ref):
        return lambda far, core: ref[far, core, z]

    def nested(ref, j):
        return lambda far, core: ref[far, core, z, j]

    def cut(ref, j):
        return ref[:, j * width : (j + 1) * width]

    def cut_group(ref, j):
        return jnp.concatenate([ref[:, part * width + j * GROUP : part * width + (j + 1) * GROUP] for part in range(3)], axis=1)

    cross_parts = (
        lambda: [(plain(cfirstt), cut(cginner, j)) for j in range(4)],
        lambda: [(nested(chiddent, j), cgsecond[...]) for j in range(4)],
        lambda: [(plain(cmixedt), cgbranch[...])] + [(plain(cxt), cut_group(cgqkv, j)) for j in range(GROUPS)],
    )

    def compute(u):
        n = u + CROSS_UNITS - jnp.maximum(CROSS_UNITS - 1 - u, 0)
        @pl.when(n >= RING)
        def _():
            core_copy(n).wait_send()

        sides = []
        for side in range(2):
            chains, chain = tuple(range(UNITS - 1)) + (UNITS - 1 + side,), n + side * (n // (UNITS - 1))
            sides.append((among(chain, "b", chains), among(chain, "c", chains)))
        right = bslot[b_slot(u)]
        for rel in (1, 0):
            core = c if rel == 0 else 1 - c
            left = aslot[a_slot(u), :, core].reshape(8 * PART, -1)
            value = mm(left, right).astype(BF16)
            for far in range(2):
                for part in range(4):
                    block = value[(far * 4 + part) * PART : (far * 4 + part + 1) * PART]
                    for side in range(2):
                        at = block_place(*sides[side], far, part // 2, part % 2)
                        cols = slice(side * width // 2, (side + 1) * width // 2)
                        if rel == 1:
                            csend[n % RING, at, :, cols] = block[:, cols]
                        else:
                            keep[n, at, :, cols] = block[:, cols]
            if rel == 1:
                core_copy(n).start()

        @pl.when(n < CROSS_UNITS + EARLY)
        def _():
            step_one(n - 1)

    def attention_tile(j, i):
        slot = i % 2
        out_rows = pl.ds(pl.multiple_of(j * GROUP, GROUP), GROUP)
        g_mixed = mm_nt(gbranch_slot[slot], wout[out_rows, :]).astype(BF16)
        items = [(seg, half) for seg in range(segs) for half in range(2)]
        at = [slice(seg * SEGLEN, (seg + 1) * SEGLEN) for seg, _ in items]
        lanes = [pair_lanes(half) for _, half in items]
        to = [pl.ds(pl.multiple_of(i * tile + seg * SEGLEN, SEGLEN), SEGLEN) for seg, _ in items]
        every = range(len(items))
        g_out = [stack_heads(g_mixed[at[e], lanes[e][0]]) for e in every]
        g_p = [mm_nt(qkv_slot[slot, at[e], lanes[e][2]], g_out[e]) for e in every]
        g_v = [mm(probs_slot[slot, seg, half], g_out[e]) for e, (seg, half) in enumerate(items)]
        g_s = []
        for e, (seg, half) in enumerate(items):
            p = probs_slot[slot, seg, half].astype(F32)
            g_s.append((p * (g_p[e] - jnp.sum(g_p[e] * p, axis=0, keepdims=True))).astype(BF16))
        g_k = [mm(g_s[e], stack_heads(qkv_slot[slot, at[e], lanes[e][0]] * HDIM**-0.5)) for e in every]
        g_st = [jnp.concatenate([g_s[e][:, :SEGLEN].T, g_s[e][:, SEGLEN:].T], axis=1) for e in every]
        g_q = [mm(g_st[e], stack_heads(qkv_slot[slot, at[e], lanes[e][1]])) * HDIM**-0.5 for e in every]
        for e in every:
            for part, value in enumerate((g_q[e], g_k[e], g_v[e])):
                value = value.astype(BF16)
                bslot[j, to[e], lanes[e][part]] = value
                if part != 1:
                    fold[part // 2, j, :, lanes[e][0]] += fold_rows(value.astype(F32))

    def last_tile(i):
        slot = i % 2

        @pl.when(i >= 2)
        def _():
            store_gx(i - 2).wait()

        total = gbranch_slot[slot].astype(F32)
        for j in range(GROUPS):
            total = total + mm_nt(bslot[j, tile_rows(i), :], wqkv[j])
        gx_slot[slot] = total.astype(BF16)
        store_gx(i).start()

    def run(action, n):
        if action in ("small", "late"):
            late = int(action == "late")
            if late and n == 0:
                for row in range(2):
                    for j in range(GROUPS):
                        late_acc[0, row : row + 1, j * GROUP : (j + 1) * GROUP] = jnp.sum(fold[row, j], axis=0, keepdims=True)
            if n == 0:
                small_copy(late, 0).start()
            else:
                small_step(late, n - 1)
            return
        {
            "one": step_one, "send": lambda n: copy_one(n).start(), "two": step_two, "three": step_three, "final": step_final, "out": step_out,
        }[action](n)

    schedule = comm_schedule()

    def step(s, carry):
        for at in range(STEPS):
            if schedule[at]:
                @pl.when(s == at)
                def _(at=at):
                    for action, n in schedule[at]:
                        run(action, n)

        @pl.when(s == EARLY)
        def _():
            for copy in weight_copies:
                copy.wait()

        for i in range(1, CROSS_UNITS):
            @pl.when(s == i)
            def _(i=i):
                cross_unit(2 * i, cross_parts[i]())
                step_one(2 * i - 1)
                copy_one(2 * i - 1).start()

        load(s, "wait")

        @pl.when(s == 1)
        def _():
            for copy in weight_copies:
                copy.start()

        @pl.when(s + 1 < STEPS)
        def _():
            load(s + 1, "start")

        group, part = place(s)
        inside = (s >= EARLY) & (s < LAST_AT)
        multiply = (s < EARLY) | (inside & (part == TILES))

        @pl.when(multiply)
        def _():
            compute(jnp.where(s < EARLY, s, EARLY + group))

        @pl.when(inside & (part < TILES))
        def _():
            attention_tile(group, part)

        @pl.when(s >= LAST_AT)
        def _():
            last_tile(s - LAST_AT)

        return carry

    fold[...] = jnp.zeros_like(fold)
    cross_unit(0, cross_parts[0]())
    lax.fori_loop(0, STEPS, step, 0)
    for action, n in schedule[STEPS]:
        run(action, n)
    for i in range(TILES - 2, TILES):
        store_gx(i).wait()
    for n in range(UNITS - RING, UNITS):
        core_copy(n).wait_send()


def late_backward(big, cross, small, attn, share):
    firstt, ginner, hiddent, gsecond, mixedt, gbranch, xt = big
    qkv, probs, w_qkv, w_out = attn
    cfirstt, cginner, chiddent, cgsecond, cmixedt, cgbranch, cxt, cgqkv = cross
    width, depth = firstt.shape
    inners = ginner.shape[1]
    rows = cfirstt.shape[1]
    tile = depth // TILES
    assert width == 16 * PART and inners == 4 * width

    def blocks(a, n):
        return a.reshape((2, 2, 4) + ((n,) if n > 1 else ()) + (PART, a.shape[1]))

    operands = [
        blocks(firstt, 1), ginner, blocks(hiddent, 4), gsecond, blocks(mixedt, 1), gbranch, blocks(xt, 1), qkv, probs, w_qkv, w_out,
        blocks(cfirstt, 1), cginner, blocks(chiddent, 4), cgsecond, blocks(cmixedt, 1), cgbranch, blocks(cxt, 1), cgqkv, *small,
    ]
    vmem = pl.BlockSpec(memory_space=pltpu.VMEM)
    any_spec = pl.BlockSpec(memory_space=pl.ANY)
    outs = [((PART, 3 * width), F32), ((PART, width), F32), ((PART, inners), F32), ((4 * PART, width), F32), ((32, width), F32), ((depth, width), BF16)]
    segs = tile // SEGLEN
    dma = pltpu.SemaphoreType.DMA
    return pl.pallas_call(
        functools.partial(late_kernel, share=share),
        in_specs=[any_spec] * 11 + [vmem] * (len(operands) - 11),
        out_specs=[vmem] * 5 + [any_spec],
        out_shape=[jax.ShapeDtypeStruct(*o) for o in outs],
        scratch_shapes=[
            pltpu.VMEM((2, 2, 2, 4, PART, depth), BF16),
            pltpu.VMEM((GROUPS, depth, width), BF16),
            pltpu.VMEM((2, tile, width), BF16),
            pltpu.VMEM((2, segs, 2, SEGLEN, 2 * SEGLEN), BF16),
            pltpu.VMEM((2, tile, width), BF16),
            pltpu.VMEM((2, tile, width), BF16),
            pltpu.VMEM((GROUPS, width, 3 * GROUP), BF16),
            pltpu.VMEM(w_out.shape[1:], BF16),
            pltpu.VMEM((2, GROUPS, 8, GROUP), F32),
            pltpu.VMEM((RING, 8, PART, width), BF16),
            pltpu.VMEM((RING, 8, PART, width), BF16),
            pltpu.VMEM((UNITS, 8, PART, width), BF16),
            pltpu.VMEM((UNITS, 4, PART, width), BF16),
            pltpu.VMEM((UNITS, 2, PART, width), BF16),
            pltpu.VMEM((UNITS, PART, width), BF16),
            pltpu.VMEM((UNITS, 2, PART, width), BF16),
            pltpu.VMEM((CROSS_UNITS, 4, PART, width), BF16),
            pltpu.VMEM((6, 32, width), F32),
            pltpu.VMEM((5, 32, width), F32),
            pltpu.VMEM((6, 8, width), F32),
            pltpu.VMEM((5, 8, width), F32),
            dma((2,)), dma((2, 3)), dma((2,)), dma((1 + 3 * GROUPS,)), dma((RING,)), dma((RING,)), dma((CHAINS,)), dma((CHAINS,)), dma((CHAINS,)), dma((CHAINS,)),
            dma((CHAINS,)), dma((CHAINS,)), dma((CHAINS,)), dma((CHAINS, 2)), dma((2, 5)), dma((2, 5)),
        ],
        compiler_params=pltpu.CompilerParams(vmem_limit_bytes=63 * 2**20, collective_id=1, has_side_effects=True),
        name="late_backward",
    )(*operands)

def finish_kernel(gx_ref, a_ref, b_ref, c_ref, d_ref, gx_out, a_out, b_out, c_out, d_out):
    gx_out[...] = gx_ref[...].astype(F32)

    @pl.when(pl.program_id(0) == 0)
    def _():
        for src, dst in ((a_ref, a_out), (b_ref, b_out), (c_ref, c_out), (d_ref, d_out)):
            dst[...] = src[...]


def finish(gx, grads, tile=1024):
    total, width = gx.shape
    rows = pl.BlockSpec((tile, width), lambda i: (i, 0))
    held = [pl.BlockSpec(g.shape, lambda i: (0, 0)) for g in grads]
    return pl.pallas_call(
        finish_kernel,
        grid=(total // tile,),
        in_specs=[rows] + held,
        out_specs=[rows] + held,
        out_shape=[jax.ShapeDtypeStruct(gx.shape, F32)] + [jax.ShapeDtypeStruct(g.shape, F32) for g in grads],
        name="finish",
    )(gx, *grads)


def small_grads(sums, bsums, csums, cbsums, gpos, bias_sums, cross_share):
    seg_rows = jnp.concatenate([jnp.sum(sums, axis=1), bias_sums])
    cross_rows = csums * cross_share
    order = jnp.array([6, 7, 5, 4, 2, 1])
    biases = jnp.stack([seg_rows[order], cross_rows[order]])
    gains = jnp.stack([seg_rows[jnp.array([3, 0])], cross_rows[jnp.array([3, 0])]])
    ups = jnp.stack([jnp.sum(bsums, axis=0), cbsums[0] * cross_share])
    return biases.reshape(-1), gains.reshape(-1), ups.reshape(-1), (gpos * cross_share).reshape(-1)


def attention_back(qkv, probs, gbranch, w_qkv, w_out):
    total, width = gbranch.shape
    heads = width // HDIM
    segs = total // SEGLEN
    scale = HDIM**-0.5

    def split(a):
        return a.reshape(segs, SEGLEN, heads, HDIM)

    def merge(a):
        return a.reshape(total, width)

    q, k, v = (
        split(qkv[:, :, part * GROUP : (part + 1) * GROUP].transpose(1, 0, 2).reshape(total, width)) for part in range(3)
    )
    p_low = probs.reshape(segs, heads // 2, SEGLEN, 2, SEGLEN).transpose(0, 1, 3, 2, 4).reshape(segs, heads, SEGLEN, SEGLEN)
    g_out = split(mm_nt(gbranch, w_out).astype(BF16))
    p = p_low.astype(F32)
    g_p = jnp.einsum("sqhd,skhd->shkq", g_out, v, preferred_element_type=F32)
    g_s = (p * (g_p - jnp.sum(g_p * p, axis=2, keepdims=True))).astype(BF16)
    g_v = jnp.einsum("shkq,sqhd->skhd", p_low, g_out, preferred_element_type=F32)
    g_k = jnp.einsum("shkq,sqhd->skhd", g_s, q, preferred_element_type=F32) * scale
    g_q = jnp.einsum("shkq,skhd->sqhd", g_s, k, preferred_element_type=F32) * scale
    g_qkv = jnp.concatenate([merge(g_q), merge(g_k), merge(g_v)], axis=1).astype(BF16)
    return g_qkv, gbranch.astype(F32) + mm_nt(g_qkv, w_qkv)


def generic_total(seg_pairs, cross_pairs, small, planes, own):
    axes = ("row", "seg")
    me = lax.axis_index("seg")
    shards = [
        lax.psum_scatter(part, axes, scatter_dimension=0, tiled=True) for part in small_grads(*small, 1.0 / planes)
    ]

    def mine(values, dim):
        return lax.dynamic_slice_in_dim(values, me * own, own, dim)

    big = []
    for at in (6, 4, 0, 2):
        cross = mm(mine(cross_pairs[at], 1), mine(cross_pairs[at + 1], 0))
        both = jnp.concatenate([mm(seg_pairs[at], seg_pairs[at + 1]), cross], axis=0)
        big.append(lax.psum_scatter(both, axes, scatter_dimension=0, tiled=True))
    return big, shards


def per_device(
    tokens, doc_ids, w_qkv, w_out, w_up, w_down, biases, gains, b_up, pos_table, cotangent, *, sizes
):
    lines, planes = sizes
    row_count, local_length, width = tokens.shape
    seg_here = local_length // SEGLEN
    segments = doc_ids.shape[1]
    total = row_count * local_length
    own = row_count * seg_here
    cot = cotangent.reshape(total, width)
    (
        qkv, probs, n1, r1, slope, n2, r2, y, xt, mixedt, firstt, hiddent,
        ccls, gcls, csums, cbsums, gpos, cxt, cmixedt, cfirstt, chiddent, cgqkv, cgbranch, cginner, cgsecond,
    ) = forward_blocks(
        tokens.reshape(total, width), cot, w_qkv, w_out, w_up, w_down, biases, gains, b_up, doc_ids, pos_table, planes,
        tile=256 if planes <= 4 else 128,
    )
    output, gsecond, ginner, gbranch, sums, bsums = early_backward(
        gcls, ccls, cot, y, n2, r2, slope, n1, r1, w_up, w_down, gains
    )
    cross_pairs = (cfirstt, cginner, chiddent, cgsecond, cmixedt, cgbranch, cxt, cgqkv)
    share = 1.0 / planes
    if (lines, planes) == (8, 4) and total == 2048 and width == 16 * PART:
        *grads, small, gx = late_backward(
            (firstt, ginner, hiddent, gsecond, mixedt, gbranch, xt), cross_pairs, (sums, bsums, csums, cbsums, gpos), (qkv, probs, w_qkv, w_out), share
        )
        gx, *grads = finish(gx, grads)
        small = small.reshape(-1)
        index = lax.axis_index("row") * planes + lax.axis_index("seg")
        shards, start = [], 0
        for size in (12 * width, 4 * width, 8 * width, segments * width):
            count = size // (lines * planes)
            shards.append(lax.dynamic_slice_in_dim(small, start + index * count, count, 0))
            start += size
    else:
        gqkv, gx = attention_back(qkv, probs, gbranch, w_qkv[0], w_out[0])
        bias_sums = jnp.stack([jnp.sum(gqkv[:, at : at + width].astype(F32), axis=0) for at in (0, 2 * width)])
        grads, shards = generic_total(
            (firstt, ginner, hiddent, gsecond, mixedt, gbranch, xt, gqkv), cross_pairs, (sums, bsums, csums, cbsums, gpos, bias_sums), planes, own
        )
    return (output.reshape(tokens.shape), gx.reshape(tokens.shape), *grads, *shards)


def solution(mesh):
    sizes = (mesh.shape["row"], mesh.shape["seg"])
    tokens_at = P("row", "seg", None)
    return jax.shard_map(
        functools.partial(per_device, sizes=sizes),
        mesh=mesh,
        in_specs=(tokens_at, P("row", None)) + (P(),) * 8 + (tokens_at,),
        out_specs=(tokens_at, tokens_at) + (P(("row", "seg"), None),) * 4 + (P(("row", "seg")),) * 4,
        check_vma=False,
    )
```

```python
import functools

import jax
import jax.numpy as jnp
from jax import lax
from jax.experimental import pallas as pl
from jax.experimental.pallas import tpu as pltpu
from jax.sharding import PartitionSpec as P


HDIM = 64
SEGLEN = 128
LANES = 128
GROUP = 2 * LANES
EPSILON = 1e-05
GELU_A = 0.7978845608028654
GELU_B = 0.044715 * GELU_A
F32, BF16 = jnp.float32, jnp.bfloat16


def mm(a, b):
    return lax.dot_general(a, b, (((1,), (0,)), ((), ())), preferred_element_type=F32)


def mm_nt(a, b):
    return lax.dot_general(a, b, (((1,), (1,)), ((), ())), preferred_element_type=F32)


def mm_tn(a, b):
    return lax.dot_general(a, b, (((0,), (0,)), ((), ())), preferred_element_type=F32)


def low_lanes(shape):
    return lax.broadcasted_iota(jnp.int32, shape, 1) < HDIM


def stack_heads(pair):
    keep = low_lanes(pair.shape)
    zero = jnp.zeros_like(pair)
    return jnp.concatenate([jnp.where(keep, pair, zero), jnp.where(keep, zero, pair)], axis=0)


def pair_lanes(half):
    return [slice(part * GROUP + half * LANES, part * GROUP + (half + 1) * LANES) for part in range(3)]


def norm_stats(values):
    centered = values - jnp.mean(values, axis=-1, keepdims=True)
    variance = jnp.mean(centered * centered, axis=-1, keepdims=True)
    rstd = lax.rsqrt(variance + EPSILON)
    return centered * rstd, rstd


def gelu_both(u):
    u = u.astype(BF16)
    square = u * u
    bend = GELU_B * square
    half = 0.5 * jnp.tanh(u * (GELU_A + bend))
    gate = half + 0.5
    hidden = u * gate
    slope = gate + hidden * (0.5 - half) * (2.0 * GELU_A + 6.0 * bend)
    return hidden, slope


def norm_back(grad, gain, normal, rstd):
    scaled = grad * gain
    a = jnp.mean(scaled, axis=-1, keepdims=True)
    b = jnp.mean(scaled * normal, axis=-1, keepdims=True)
    return (scaled - a - normal * b) * rstd


OUTS = 13
NEGATIVE = -1000000000.0
MESH = pl.DeviceIdType.MESH


def turned(values):
    return values.astype(F32).T.astype(BF16)


def places(docs, rows, own, kinds):
    lines, segments = docs.shape
    here = own // lines
    count = 2 * rows

    def spread(width, axis):
        return lax.broadcasted_iota(jnp.int32, (count, width), axis)

    def line_of(at):
        return lax.shift_right_logical(at & (own - 1), here.bit_length() - 1)

    in_line = line_of(spread(lines, 0)) == spread(lines, 1)
    row_docs = mm(in_line.astype(BF16), docs.astype(F32).astype(BF16))
    at = spread(segments, 0) & (rows - 1)
    segment = lax.shift_right_logical(at, own.bit_length() - 1) * here + (at & (here - 1))
    across = spread(segments, 1)
    doc = jnp.sum(jnp.where(across == segment, row_docs, 0.0), axis=1, keepdims=True)
    start = jnp.min(jnp.where(row_docs == doc, across.astype(F32), float(segments)), axis=1, keepdims=True)
    place = segment[:, 0:1].astype(F32) - start
    onehot = (place == spread(kinds, 1).astype(F32))[:rows].astype(F32)
    key = doc + segments * line_of(spread(1, 0)).astype(F32)
    keys_across = jnp.broadcast_to(key, (count, max(rows, LANES))).T[:rows]
    return onehot, key[:rows] == keys_across


def cross_part(me, onehot, allowed, embed, bias_ref, gain_ref, bup_ref, outs, writes, weights, copies, scratch, ff_chunk):
    (
        ccls_ref, gcls_ref, sums_ref, bsums_ref, gpos_ref, xt_ref, mixedt_ref, firstt_ref, hiddent_ref,
        gqkv_ref, gbranch_ref, ginner_ref, gsecond_ref,
    ) = outs
    wqkv, wout, wup, wdown = weights
    qkv_ref, probs_ref, mixed_ref, slope_ref, whole_ref = scratch
    own, width = ccls_ref.shape
    rows = whole_ref.shape[1]
    inners = wup.shape[1]
    bias = bias_ref[...].astype(F32)[:, 1]
    gain = gain_ref[1].astype(F32)
    up_bias = bup_ref[1:2, :].astype(F32)
    x = (whole_ref[0] + embed).astype(BF16)
    gy = whole_ref[1]
    xt_ref[...] = turned(x)
    copies[0].wait()
    for part in range(3):
        cols = slice(part * width, (part + 1) * width)
        out = mm(x, wqkv[:, cols])
        if part == 0:
            out = out + bias[0:1]
        if part == 2:
            out = out + bias[1:2]
        qkv_ref[:, cols] = out.astype(BF16)
    low = low_lanes((rows, LANES))
    pairs = range(width // LANES)
    lanes = [[slice(part * width + pair * LANES, part * width + (pair + 1) * LANES) for part in range(3)] for pair in pairs]
    scores = [
        jnp.where(allowed, mm_nt(qkv_ref[:, at[1]], stack_heads(qkv_ref[:, at[0]] * HDIM**-0.5)), NEGATIVE) for at in lanes
    ]
    pt = []
    for pair in pairs:
        e = jnp.exp(scores[pair] - jnp.max(scores[pair], axis=0, keepdims=True))
        p = e * (1.0 / jnp.sum(e, axis=0, keepdims=True))
        probs_ref[pair] = p
        pt.append(p.T.astype(BF16))
    for pair, at in enumerate(lanes):
        v = qkv_ref[:, at[2]]
        mixed_ref[:, at[0]] = jnp.where(low, mm(pt[pair][:rows], v), mm(pt[pair][rows:], v)).astype(BF16)
    copies[1].wait()
    mixed = mixed_ref[...]
    mixedt_ref[...] = turned(mixed)
    n1, r1 = norm_stats(x.astype(F32) + mm(mixed, wout[...]) + bias[2:3])
    first = (n1 * gain[0:1] + bias[3:4]).astype(BF16)
    firstt_ref[...] = turned(first)
    copies[2].wait()
    copies[3].wait()
    total = first.astype(F32) + bias[4:5]
    chunks = [slice(c * ff_chunk, (c + 1) * ff_chunk) for c in range(inners // ff_chunk)]
    inner = [mm(first, wup[:, cols]) for cols in chunks]
    for c, cols in enumerate(chunks):
        hidden, slope = gelu_both(inner[c] + up_bias[:, cols])
        hidden = hidden.astype(BF16)
        hiddent_ref[cols, :] = turned(hidden)
        slope_ref[:, cols] = slope.astype(F32)
        total = total + mm(hidden, wdown[cols, :])
    n2, r2 = norm_stats(total)
    mine = pl.ds(pl.multiple_of(me * own, own), own)
    whole_ref[0] = (n2 * gain[1:2] + bias[5:6]).astype(BF16).astype(F32)
    ccls_ref[...] = whole_ref[0, mine, :]
    for i in (0, 5, 6, 7, 8):
        writes[i].start()

    def row_sum(values):
        return jnp.sum(values.astype(F32), axis=0, keepdims=True)

    sums_ref[0:1, :] = row_sum(gy * n2)
    sums_ref[1:2, :] = row_sum(gy)
    g_two = norm_back(gy, gain[1:2], n2, r2)
    g_second = g_two.astype(BF16)
    gsecond_ref[...] = g_second
    sums_ref[2:3, :] = row_sum(g_second)
    g_first = g_two
    g_hidden = [mm_nt(g_second, wdown[cols, :]) for cols in chunks]
    for c, cols in enumerate(chunks):
        g_inner = (g_hidden[c] * slope_ref[:, cols]).astype(BF16)
        ginner_ref[:, cols] = g_inner
        bsums_ref[:, cols] = row_sum(g_inner)
        g_first = g_first + mm_nt(g_inner, wup[:, cols])
    sums_ref[3:4, :] = row_sum(g_first * n1)
    sums_ref[4:5, :] = row_sum(g_first)
    g_one = norm_back(g_first, gain[0:1], n1, r1)
    g_branch = g_one.astype(BF16)
    gbranch_ref[...] = g_branch
    sums_ref[5:6, :] = row_sum(g_branch)
    for i in (10, 11, 12):
        writes[i].start()
    g_mixed = mm_nt(g_branch, wout[...]).astype(BF16)
    g_out = [stack_heads(g_mixed[:, at[0]]) for at in lanes]
    g_p = [mm_nt(qkv_ref[:, at[2]], g_out[pair]) for pair, at in enumerate(lanes)]
    g_s, g_st = [], []
    for pair in pairs:
        p = probs_ref[pair]
        g = p * (g_p[pair] - jnp.sum(g_p[pair] * p, axis=0, keepdims=True))
        g_s.append(g.astype(BF16))
        g_st.append(g.T.astype(BF16))
    for pair, at in enumerate(lanes):
        q, k, _ = (qkv_ref[:, part] for part in at)
        g_q = jnp.where(low, mm(g_st[pair][:rows], k), mm(g_st[pair][rows:], k)) * HDIM**-0.5
        gqkv_ref[:, at[0]] = g_q.astype(BF16)
        gqkv_ref[:, at[1]] = mm(g_s[pair], stack_heads(q * HDIM**-0.5)).astype(BF16)
        gqkv_ref[:, at[2]] = mm(probs_ref[pair].astype(BF16), g_out[pair]).astype(BF16)
    g_qkv = gqkv_ref[...]
    sums_ref[6:7, :] = row_sum(g_qkv[:, :width])
    sums_ref[7:8, :] = row_sum(g_qkv[:, 2 * width :])
    g_x = g_one + mm_nt(g_qkv, wqkv[...])
    whole_ref[1] = g_x
    gcls_ref[...] = whole_ref[1, mine, :]
    gpos_ref[...] = lax.dot_general(onehot, g_x, (((0,), (0,)), ((), ())), preferred_element_type=F32, precision=lax.Precision.HIGHEST)
    for i in (1, 2, 3, 4, 9):
        writes[i].start()
    for write in writes:
        write.wait()


def forward_kernel(
    x_ref, wqkv_hbm, wout_hbm, wup_hbm, wdown_hbm, cot_hbm, bias_ref, gain_ref, bup_ref, doc_ref, table_ref,
    qkv_ref, probs_ref, n1_ref, r1_ref, slope_ref, n2_ref, r2_ref, y_ref, xt_ref, mixedt_ref, firstt_ref, hiddent_ref,
    *refs, ff_chunk, devices,
):
    homes, outs, refs = refs[:OUTS], refs[OUTS : 2 * OUTS], refs[2 * OUTS :]
    wqkv, wout, wup, wdown, mixed_ref, first_ref, sems, cls_ref, cot_rows, cot_low, packed, gathered = refs[:12]
    cross_weights, cross_scratch = refs[12:16], refs[16:21]
    cross_sems, out_sems, cot_sems, send_sems, recv_sems = refs[21:]
    step = pl.program_id(0)
    last = pl.num_programs(0) - 1
    rows, width = x_ref.shape
    parts = [slice(part * width, (part + 1) * width) for part in range(3)]
    part_copies = [pltpu.make_async_copy(wqkv_hbm.at[0, :, cols], wqkv.at[:, cols], sems.at[3 + i]) for i, cols in enumerate(parts)]
    copies = part_copies + [
        pltpu.make_async_copy(src.at[0], dst, sems.at[i])
        for i, (src, dst) in enumerate(((wout_hbm, wout), (wup_hbm, wup), (wdown_hbm, wdown)))
    ]

    own = cls_ref.shape[0]
    line, me = lax.axis_index("row"), lax.axis_index("seg")
    peers = [(line, lax.rem(me + hop, devices)) for hop in range(1, devices)]
    cot_copies = [
        pltpu.make_async_copy(cot_hbm.at[pl.ds(i * SEGLEN, 16)], cot_rows.at[i], cot_sems.at[i]) for i in range(own)
    ]
    cross_copies = [
        pltpu.make_async_copy(src.at[1], dst, cross_sems.at[i])
        for i, (src, dst) in enumerate(zip((wqkv_hbm, wout_hbm, wup_hbm, wdown_hbm), cross_weights))
    ]
    writes = [pltpu.make_async_copy(src, dst, out_sems.at[i]) for i, (src, dst) in enumerate(zip(outs, homes))]
    barrier = pltpu.get_barrier_semaphore()

    def sends(kind):
        return [
            pltpu.make_async_remote_copy(
                src_ref=packed.at[kind], dst_ref=gathered.at[kind, hop + 1], send_sem=send_sems.at[kind, hop],
                recv_sem=recv_sems.at[kind, hop], device_id=peer, device_id_type=MESH,
            )
            for hop, peer in enumerate(peers)
        ]

    def arrived(kind, whole_ref):
        for send in sends(kind):
            send.wait()
        gathered[kind, 0] = packed[kind]
        for hop in range(devices):
            rows_at = pl.ds(pl.multiple_of(lax.rem(me - hop + devices, devices) * own, own), own)
            whole_ref[1 - kind, rows_at, :] = gathered[kind, hop].astype(F32)

    @pl.when(step == 0)
    def _():
        for peer in peers:
            pl.semaphore_signal(barrier, inc=1, device_id=peer, device_id_type=MESH)
        for copy in copies[:4]:
            copy.start()

    @pl.when(step == 1)
    def _():
        copies[4].wait()
        copies[5].wait()
        for copy in cot_copies + cross_copies:
            copy.start()

    @pl.when(step == 2)
    def _():
        for i, copy in enumerate(cot_copies):
            copy.wait()
            cot_low[i : i + 1, :] = cot_rows[i, 0:8, :].astype(F32)[0:1]
        packed[0] = cot_low[...].astype(BF16)
        pl.semaphore_wait(barrier, devices - 1)
        for send in sends(0):
            send.start()

    bias = bias_ref[...].astype(F32)[:, 0]
    gain = gain_ref[0].astype(F32)
    up_bias = bup_ref[0:1, :].astype(F32)
    inners = wup.shape[1]
    chunks = [slice(c * ff_chunk, (c + 1) * ff_chunk) for c in range(inners // ff_chunk)]
    items = [(seg, pair) for seg in range(rows // SEGLEN) for pair in range(width // LANES)]
    every = range(len(items))
    at = [slice(seg * SEGLEN, (seg + 1) * SEGLEN) for seg, _ in items]

    def front(state, loading):
        def project_part(part):
            if loading:
                copies[part].wait()
                if part == 0:
                    copies[4].start()
                    copies[5].start()
            x = x_ref[...]
            out = mm(x, wqkv[:, part * width : (part + 1) * width])
            if part == 0:
                out = out + bias[0:1]
            if part == 2:
                out = out + bias[1:2]
            out = out.astype(BF16)
            for group in range(width // GROUP):
                qkv_ref[group, :, part * GROUP : (part + 1) * GROUP] = out[:, group * GROUP : (group + 1) * GROUP]

        def piece(e, part):
            pair = items[e][1]
            return qkv_ref[pair // 2, at[e], pair_lanes(pair % 2)[part]]

        def scores():
            xt_ref[...] = x_ref[...].T
            state["scores"] = [mm_nt(piece(e, 1), stack_heads(piece(e, 0) * HDIM**-0.5)) for e in every]

        def softmax(part):
            for e in every[part :: 2]:
                score = state["scores"][e]
                ex = jnp.exp(score - jnp.max(score, axis=0, keepdims=True))
                p = (ex * (1.0 / jnp.sum(ex, axis=0, keepdims=True))).astype(BF16)
                probs_ref[items[e][0], items[e][1]] = p
                state[e] = jnp.concatenate([p[:, :SEGLEN].T, p[:, SEGLEN:].T], axis=1)

        def mix():
            for e, (_, pair) in enumerate(items):
                mixed_ref[at[e], pair * LANES : (pair + 1) * LANES] = mm(state[e], stack_heads(piece(e, 2))).astype(BF16)

        def project_out():
            if loading:
                copies[3].wait()
            mixed = mixed_ref[...]
            mixedt_ref[...] = mixed.T
            state["resid"] = x_ref[...].astype(F32) + mm(mixed, wout[...]) + bias[2:3]

        def norm():
            n1, r1 = norm_stats(state["resid"])
            n1_ref[...] = n1.astype(BF16)
            r1_ref[...] = jnp.broadcast_to(r1, r1_ref.shape)
            first = (n1 * gain[0:1] + bias[3:4]).astype(BF16)
            firstt_ref[...] = first.T
            state["first"] = first

        return [lambda part=part: project_part(part) for part in range(3)] + [scores, lambda: softmax(0), lambda: softmax(1), mix, project_out, norm]

    def back(state):
        first = first_ref[...]
        state["total"] = first.astype(F32) + bias[4:5]

        def up(c):
            state["inner", c] = mm(first, wup[:, chunks[c]])

        def gelu(c):
            cols = chunks[c]
            hidden, slope = gelu_both(state["inner", c] + up_bias[:, cols])
            hidden = hidden.astype(BF16)
            hiddent_ref[cols, :] = hidden.T
            slope_ref[:, cols] = slope.astype(BF16)
            state["hidden", c] = hidden

        def down(c):
            state["total"] = state["total"] + mm(state["hidden", c], wdown[chunks[c], :])

        def norm():
            n2, r2 = norm_stats(state["total"])
            n2_ref[...] = n2.astype(BF16)
            r2_ref[...] = jnp.broadcast_to(r2, r2_ref.shape)
            y = (n2 * gain[1:2] + bias[5:6]).astype(BF16)
            y_ref[...] = y
            segs = rows // SEGLEN
            for seg in range(segs):
                cls_ref[pl.ds((step - 1) * segs + seg, 1), :] = y[seg * SEGLEN : seg * SEGLEN + 8].astype(F32)[0:1]

        pieces = [lambda: up(0)]
        for c in range(len(chunks)):
            if c + 1 < len(chunks):
                pieces.append(lambda c=c: up(c + 1))
            pieces += [lambda c=c: gelu(c), lambda c=c: down(c)]
        return pieces + [norm]

    def run(with_front, with_back):
        state = {}
        lists = ([back(state)] if with_back else []) + ([front(state, not with_back)] if with_front else [])
        turns = sorted((((i + 0.5) / len(pieces), k, i) for k, pieces in enumerate(lists) for i in range(len(pieces))))
        for _, k, i in turns:
            lists[k][i]()
        if with_front:
            first_ref[...] = state["first"]

    @pl.when(step == 0)
    def _():
        run(True, False)

    @pl.when((step > 0) & (step < last))
    def _():
        run(True, True)

    @pl.when(step == last)
    def _():
        run(False, True)
        packed[1] = cls_ref[...].astype(BF16)
        for send in sends(1):
            send.start()
        onehot, allowed = places(doc_ref[...], own * devices, own, table_ref.shape[0])
        embed = mm(onehot.astype(BF16), table_ref[...])
        arrived(0, cross_scratch[-1])
        arrived(1, cross_scratch[-1])
        cross_part(
            me, onehot, allowed, embed, bias_ref, gain_ref, bup_ref, outs, writes,
            cross_weights, cross_copies, cross_scratch, ff_chunk,
        )


def forward_blocks(x, cot, w_qkv, w_out, w_up, w_down, bias, gain, bup, docs, table, devices, tile=256, ff_chunk=768):
    total, width = x.shape
    inners = w_up.shape[-1]
    segs = tile // SEGLEN
    pairs = width // LANES
    any_spec = pl.BlockSpec(memory_space=pl.ANY)

    steps = total // tile

    def rows_of(cols, late):
        return pl.BlockSpec((tile, cols), lambda i: (jnp.maximum(i - 1, 0) if late else jnp.minimum(i, steps - 1), 0))

    def whole(a):
        return pl.BlockSpec(a.shape, lambda i: (0,) * a.ndim)

    def cols_of(rows, late):
        return pl.BlockSpec((rows, tile), lambda i: (0, jnp.maximum(i - 1, 0) if late else jnp.minimum(i, steps - 1)))

    outs = [
        ((width // GROUP, total, 3 * GROUP), BF16, pl.BlockSpec((width // GROUP, tile, 3 * GROUP), lambda i: (0, jnp.minimum(i, steps - 1), 0))),
        ((total // SEGLEN, pairs, SEGLEN, 2 * SEGLEN), BF16, pl.BlockSpec((segs, pairs, SEGLEN, 2 * SEGLEN), lambda i: (jnp.minimum(i, steps - 1), 0, 0, 0))),
        ((total, width), BF16, rows_of(width, False)),
        ((total, LANES), F32, rows_of(LANES, False)),
        ((total, inners), BF16, rows_of(inners, True)),
        ((total, width), BF16, rows_of(width, True)),
        ((total, LANES), F32, rows_of(LANES, True)),
        ((total, width), BF16, rows_of(width, True)),
        ((width, total), BF16, cols_of(width, False)),
        ((width, total), BF16, cols_of(width, False)),
        ((width, total), BF16, cols_of(width, False)),
        ((inners, total), BF16, cols_of(inners, True)),
    ]
    own = total // SEGLEN
    rows = own * devices
    cross_outs = [
        ((own, width), F32), ((own, width), F32), ((8, width), F32), ((1, inners), F32), (table.shape, F32),
        ((width, rows), BF16), ((width, rows), BF16), ((width, rows), BF16), ((inners, rows), BF16),
        ((rows, 3 * width), BF16), ((rows, width), BF16), ((rows, inners), BF16), ((rows, width), BF16),
    ]
    bias = bias.transpose(1, 0, 2)
    dma = pltpu.SemaphoreType.DMA
    return pl.pallas_call(
        functools.partial(forward_kernel, ff_chunk=ff_chunk, devices=devices),
        grid=(steps + 1,),
        in_specs=[rows_of(width, False), any_spec, any_spec, any_spec, any_spec, any_spec]
        + [whole(a) for a in (bias, gain, bup, docs, table)],
        out_specs=[o[2] for o in outs] + [pl.BlockSpec(memory_space=pltpu.HBM)] * OUTS,
        out_shape=[jax.ShapeDtypeStruct(o[0], o[1]) for o in outs + cross_outs],
        scratch_shapes=[pltpu.VMEM(*o) for o in cross_outs]
        + [
            pltpu.VMEM(w_qkv.shape[1:], BF16),
            pltpu.VMEM(w_out.shape[1:], BF16),
            pltpu.VMEM(w_up.shape[1:], BF16),
            pltpu.VMEM(w_down.shape[1:], BF16),
            pltpu.VMEM((tile, width), BF16),
            pltpu.VMEM((tile, width), BF16),
            dma((6,)),
            pltpu.VMEM((own, width), F32),
            pltpu.VMEM((own, 16, width), BF16),
            pltpu.VMEM((own, width), F32),
            pltpu.VMEM((2, own, width), BF16),
            pltpu.VMEM((2, devices, own, width), BF16),
            pltpu.VMEM(w_qkv.shape[1:], BF16),
            pltpu.VMEM(w_out.shape[1:], BF16),
            pltpu.VMEM(w_up.shape[1:], BF16),
            pltpu.VMEM(w_down.shape[1:], BF16),
            pltpu.VMEM((rows, 3 * width), BF16),
            pltpu.VMEM((pairs, rows, 2 * rows), F32),
            pltpu.VMEM((rows, width), BF16),
            pltpu.VMEM((rows, inners), F32),
            pltpu.VMEM((2, rows, width), F32),
            dma((4,)), dma((OUTS,)), dma((own,)), dma((2, devices - 1)), dma((2, devices - 1)),
        ],
        compiler_params=pltpu.CompilerParams(vmem_limit_bytes=63 * 2**20, collective_id=0, has_side_effects=True),
        name="forward_blocks",
    )(x, w_qkv, w_out, w_up, w_down, cot, bias, gain, bup, docs, table)

def fold_rows(values):
    rows, cols = values.shape
    return jnp.sum(values.reshape(rows // 8, 8, cols), axis=0)


def early_kernel(
    gcls_ref, ccls_ref, cot_ref, y_ref, n2_ref, r2_ref, slope_ref, n1_ref, r1_ref, wup_hbm, wdown_hbm, gain_ref,
    out_ref, gsecond_ref, ginner_ref, gbranch_ref, sums_ref, bsums_ref, wup, wdown, two_ref, sems, *, ff_chunk,
):
    step = pl.program_id(0)
    last = pl.num_programs(0) - 1
    copies = [
        pltpu.make_async_copy(src.at[0], dst, sems.at[i]) for i, (src, dst) in enumerate(((wdown_hbm, wdown), (wup_hbm, wup)))
    ]

    @pl.when(step == 0)
    def _():
        for copy in copies:
            copy.start()
        sums_ref[...] = jnp.zeros_like(sums_ref)
        bsums_ref[...] = jnp.zeros_like(bsums_ref)

    @pl.when(step == 1)
    def _():
        for copy in copies:
            copy.wait()

    rows, width = cot_ref.shape
    segs = rows // SEGLEN
    inners = wup.shape[1]
    gain = gain_ref[0].astype(F32)
    chunks = [slice(c * ff_chunk, (c + 1) * ff_chunk) for c in range(inners // ff_chunk)]

    def front(state):
        def gradient():
            place = lax.broadcasted_iota(jnp.int32, (rows, width), 0)
            gy = cot_ref[...].astype(F32)
            y = y_ref[...].astype(F32)
            for seg in range(segs):
                at = pl.ds(step * segs + seg, 1)
                gy = jnp.where(place == seg * SEGLEN, gcls_ref[at, :], gy)
                y = jnp.where(place == seg * SEGLEN, ccls_ref[at, :], y)
            out_ref[...] = y.astype(BF16)
            state["gy"] = gy

        def norm():
            gy = state["gy"]
            n2 = n2_ref[...].astype(F32)
            sums_ref[0] += fold_rows(gy * n2)
            sums_ref[1] += fold_rows(gy)
            state["two"] = norm_back(gy, gain[1:2], n2, r2_ref[:, 0:1])

        def store():
            low = state["two"].astype(BF16)
            gsecond_ref[...] = low
            sums_ref[2] += fold_rows(low.astype(F32))

        return [gradient, norm, store]

    def back(state):
        g_two = two_ref[...]
        g_second = g_two.astype(BF16)
        state["first"] = g_two

        def down(c):
            state["hidden", c] = mm_nt(g_second, wdown[chunks[c], :])

        def slope(c):
            cols = chunks[c]
            g_low = state["hidden", c].astype(BF16) * slope_ref[:, cols]
            ginner_ref[:, cols] = g_low
            bsums_ref[:, cols] += fold_rows(g_low.astype(F32))
            state["inner", c] = g_low

        def up(c):
            state["first"] = state["first"] + mm_nt(state["inner", c], wup[:, chunks[c]])

        def norm():
            g_first = state["first"]
            n1 = n1_ref[...].astype(F32)
            sums_ref[3] += fold_rows(g_first * n1)
            sums_ref[4] += fold_rows(g_first)
            g_branch = norm_back(g_first, gain[0:1], n1, r1_ref[:, 0:1]).astype(BF16)
            gbranch_ref[...] = g_branch
            sums_ref[5] += fold_rows(g_branch.astype(F32))

        pieces = [lambda: down(0)]
        for c in range(len(chunks)):
            if c + 1 < len(chunks):
                pieces.append(lambda c=c: down(c + 1))
            pieces += [lambda c=c: slope(c), lambda c=c: up(c)]
        return pieces + [norm]

    def run(with_front, with_back):
        state = {}
        lists = ([back(state)] if with_back else []) + ([front(state)] if with_front else [])
        turns = sorted((((i + 0.5) / len(pieces), k, i) for k, pieces in enumerate(lists) for i in range(len(pieces))))
        for _, k, i in turns:
            lists[k][i]()
        if with_front:
            two_ref[...] = state["two"]

    @pl.when(step == 0)
    def _():
        run(True, False)

    @pl.when((step > 0) & (step < last))
    def _():
        run(True, True)

    @pl.when(step == last)
    def _():
        run(False, True)


def early_backward(gcls, ccls, cot, y, n2, r2, slope, n1, r1, w_up, w_down, gains, tile=256, ff_chunk=768):
    total, width = cot.shape
    inners = w_up.shape[-1]
    any_spec = pl.BlockSpec(memory_space=pl.ANY)

    steps = total // tile

    def rows_of(cols, late=False):
        return pl.BlockSpec((tile, cols), lambda i: (jnp.maximum(i - 1, 0) if late else jnp.minimum(i, steps - 1), 0))

    def whole(a):
        return pl.BlockSpec(a.shape, lambda i: (0,) * len(a.shape))

    outs = [
        ((total, width), BF16, rows_of(width)),
        ((total, width), BF16, rows_of(width)),
        ((total, inners), BF16, rows_of(inners, True)),
        ((total, width), BF16, rows_of(width, True)),
        ((6, 8, width), F32, pl.BlockSpec((6, 8, width), lambda i: (0, 0, 0))),
        ((8, inners), F32, pl.BlockSpec((8, inners), lambda i: (0, 0))),
    ]
    return pl.pallas_call(
        functools.partial(early_kernel, ff_chunk=ff_chunk),
        grid=(steps + 1,),
        in_specs=[whole(gcls), whole(ccls), rows_of(width), rows_of(width), rows_of(width), rows_of(LANES), rows_of(inners, True),
                  rows_of(width, True), rows_of(LANES, True), any_spec, any_spec, whole(gains)],
        out_specs=[o[2] for o in outs],
        out_shape=[jax.ShapeDtypeStruct(o[0], o[1]) for o in outs],
        scratch_shapes=[pltpu.VMEM(w_up.shape[1:], BF16), pltpu.VMEM(w_down.shape[1:], BF16), pltpu.VMEM((tile, width), F32), pltpu.SemaphoreType.DMA((2,))],
        compiler_params=pltpu.CompilerParams(vmem_limit_bytes=60 * 2**20),
        name="early_backward",
    )(gcls, ccls, cot, y, n2, r2, slope, n1, r1, w_up, w_down, gains)

RING = 4
CROSS_UNITS = 3
SEG_UNITS = 12
UNITS = CROSS_UNITS + SEG_UNITS
CHAINS = UNITS + 1
PART = 48
GROUPS = 3
EARLY = 9
TILES = 4
GROUP_STEPS = TILES + 1
LAST_AT = EARLY + GROUPS * GROUP_STEPS
STEPS = LAST_AT + TILES


CHAIN_TABLE = (
    ("e", 1, 4, 6, 8, 13), ("a", 1, 4, 6, 8, 13), ("e", 2, 6, 8, 11, 16), ("a", 2, 6, 8, 11, 16),
    ("e", 4, 8, 11, 14, 19), ("a", 4, 8, 11, 14, 19), ("b", 6, 11, 14, 17, 21), ("a", 6, 11, 14, 17, 21),
    ("b", 8, 14, 17, 20, 24), ("a", 8, 14, 17, 20, 24), ("b", 11, 17, 20, 23, 26), ("a", 11, 17, 20, 23, 26),
    ("b", 14, 18, 21, 23, 26), ("a", 19, 23, 25, 27, 28), ("b", 24, 26, 27, 28, 28), ("a", 24, 26, 27, 28, 28),
)
SMALL_MOMENTS = (1, 3, 5, 7, 10, 13)
SMALL_LATE = (23, 24, 25, 26, 27, 28)
WAYS = "".join(row[0] for row in CHAIN_TABLE)


def comm_schedule():
    table = {s: [] for s in range(STEPS + 1)}
    for n, (_, *moments) in enumerate(CHAIN_TABLE):
        for action, at in zip(("send", "two", "three", "final", "out"), moments):
            if action != "send" or n not in (1, 3):
                table[at].append((action, n))
    for n, at in ((CROSS_UNITS + EARLY - 1, EARLY + 1), (UNITS - 3, 14), (UNITS - 2, 19), (UNITS - 1, 24)):
        table[at].append(("one", n))
    for d in range(6):
        table[SMALL_MOMENTS[d]].append(("small", d))
        table[SMALL_LATE[d]].append(("late", d))
    order = ("small", "late", "one", "out", "final", "three", "two", "send")
    for at in range(STEPS):
        table[at].sort(key=lambda item: (order.index(item[0]), item[1]))
    rank = {"two": 1, "three": 2, "final": 3, "out": 4}
    table[STEPS].sort(key=lambda item: (rank[item[0]] if item[0] != "late" else item[1] - 2.5, item[1]))
    return table


def add_low(a, b):
    return (a.astype(F32) + b.astype(F32)).astype(BF16)


def late_kernel(
    firstt, ginner, hiddent, gsecond, mixedt, gbranch, xt, qkv, probs, wqkv_hbm, wout_hbm,
    cfirstt, cginner, chiddent, cgsecond, cmixedt, cgbranch, cxt, cgqkv,
    sums, bsums, csums, cbsums, gpos,
    dqkv_ref, dout_ref, dup_ref, ddown_ref, small_ref, gx_ref,
    aslot, bslot, qkv_slot, probs_slot, gbranch_slot, gx_slot, wqkv, wout, fold, csend, crecv, keep, r1, r2, r3, rf, rc, acc, racc, late_acc, late_racc,
    load_sems, tile_sems, store_sems, weight_sems, csend_sems, crecv_sems, s1_sems, q1_sems, s2_sems, q2_sems, s3_sems, q3_sems, sf_sems, qf_sems, sa_sems, qa_sems,
    *, share,
):
    width = bslot.shape[-1]
    line, z = lax.axis_index("row"), lax.axis_index("seg")
    y, x, c = line // 4, (line // 2) % 2, line % 2
    zh, zl = z // 2, z % 2
    flip_c = (y * 4 + x * 2 + 1 - c, z)
    flip_x = (y * 4 + (1 - x) * 2 + c, z)
    flip_y = ((1 - y) * 4 + x * 2 + c, z)
    flip_zl = (line, zh * 2 + 1 - zl)
    flip_zh = (line, (1 - zh) * 2 + zl)
    flip_yzh = ((1 - y) * 4 + x * 2 + c, (1 - zh) * 2 + zl)
    barrier = pltpu.get_barrier_semaphore()
    for peer in (flip_c, flip_x, flip_y, flip_zl, flip_zh, flip_yzh):
        pl.semaphore_signal(barrier, inc=1, device_id=peer, device_id_type=MESH)

    tile = gbranch_slot.shape[1]
    segs = tile // SEGLEN

    def a_slot(u):
        return jnp.where((u < 4) | (u >= EARLY), 0, (u + 1) % 2)

    def b_slot(u):
        return jnp.where(u < 4, u % 2, jnp.where(u < EARLY, u // 8, u - EARLY))

    def load_unit(u, do):
        def act(src, dst, side):
            getattr(pltpu.make_async_copy(src, dst, load_sems.at[side]), do)()

        def columns(ref, j):
            return ref.at[:, pl.ds(pl.multiple_of(j * width, width), width)]

        @pl.when(u == 0)
        def _():
            act(firstt, aslot.at[0], 0)

        @pl.when(u < 4)
        def _():
            act(columns(ginner, u), bslot.at[u % 2], 1)

        @pl.when((u >= 4) & (u < 8))
        def _():
            act(hiddent.at[:, :, :, u - 4], aslot.at[(u + 1) % 2], 0)

        @pl.when(u == 4)
        def _():
            act(gsecond, bslot.at[0], 1)

        @pl.when(u == 8)
        def _():
            act(mixedt, aslot.at[1], 0)
            act(gbranch, bslot.at[1], 1)

        @pl.when(u == EARLY)
        def _():
            act(xt, aslot.at[0], 0)

    def tile_rows(i):
        return pl.ds(pl.multiple_of(i * tile, tile), tile)

    def load_tile(j, i, slot, late, do):
        copies = [pltpu.make_async_copy(gbranch.at[tile_rows(i)], gbranch_slot.at[slot], tile_sems.at[slot, 0])]
        if not late:
            copies.append(pltpu.make_async_copy(qkv.at[j, tile_rows(i)], qkv_slot.at[slot], tile_sems.at[slot, 1]))
            copies.append(
                pltpu.make_async_copy(probs.at[pl.ds(i * segs, segs), pl.ds(2 * j, 2)], probs_slot.at[slot], tile_sems.at[slot, 2])
            )
        for copy in copies:
            getattr(copy, do)()

    def place(s):
        group = (s - EARLY) // GROUP_STEPS
        return group, (s - EARLY) % GROUP_STEPS

    def load(s, do):
        group, part = place(s)
        inside = (s >= EARLY) & (s < LAST_AT)

        @pl.when(s < EARLY)
        def _():
            load_unit(s, do)

        @pl.when(inside & (part < TILES))
        def _():
            load_tile(group, part, part % 2, False, do)

        @pl.when(inside & (part == TILES))
        def _():
            load_unit(EARLY + group, do)

        @pl.when(s >= LAST_AT)
        def _():
            load_tile(0, s - LAST_AT, (s - LAST_AT) % 2, True, do)

    def store_gx(i):
        return pltpu.make_async_copy(gx_slot.at[i % 2], gx_ref.at[tile_rows(i)], store_sems.at[i % 2])

    weight_copies = [pltpu.make_async_copy(wout_hbm.at[0], wout, weight_sems.at[0])]
    for j in range(GROUPS):
        for part in range(3):
            weight_copies.append(
                pltpu.make_async_copy(
                    wqkv_hbm.at[0, :, pl.ds(part * width + j * GROUP, GROUP)],
                    wqkv.at[j, :, pl.ds(part * GROUP, GROUP)],
                    weight_sems.at[1 + 3 * j + part],
                )
            )
    load(0, "start")

    def remote(src, dst, send_sem, recv_sem, peer):
        return pltpu.make_async_remote_copy(
            src_ref=src, dst_ref=dst, send_sem=send_sem, recv_sem=recv_sem, device_id=peer, device_id_type=MESH
        )

    ways = {
        "a": ((x, zl, zh), (flip_x, flip_zl, flip_zh)),
        "b": ((y, x, zl), (flip_y, flip_x, flip_zl)),
        "c": ((zl, x, zh), (flip_zl, flip_x, flip_zh)),
        "e": ((y, x), (flip_y, flip_x)),
        "f": ((x,), (flip_x,)),
    }

    def way(n):
        return ways[WAYS[n]]

    def among(n, kinds, chains):
        return sum((jnp.asarray(n == k).astype(jnp.int32) for k in chains if WAYS[k] in kinds), jnp.int32(0))

    def block_place(in_b, in_c, far, high, low):
        at = {"a": far * 4 + low * 2 + high, "b": high * 4 + far * 2 + low, "c": low * 4 + far * 2 + high}
        return at["a"] + in_b * (at["b"] - at["a"]) + in_c * (at["c"] - at["a"])

    def core_copy(n):
        slot = n % RING
        return remote(csend.at[slot], crecv.at[slot], csend_sems.at[slot], crecv_sems.at[slot], flip_c)

    def part_of(n):
        if n >= UNITS - 1:
            half = width // 2
            return UNITS - 1, slice((n - UNITS + 1) * half, (n - UNITS + 2) * half)
        return n, slice(0, width)

    def copy_one(n):
        (b1, *_), (peer, *_) = way(n)
        m, cols = part_of(n)
        return remote(keep.at[m, pl.ds(4 * (1 - b1), 4), :, cols], r1.at[m, :, :, cols], s1_sems.at[n], q1_sems.at[n], peer)

    def copy_two(n):
        (b1, b2, *_), (_, peer, *_) = way(n)
        m, cols = part_of(n)
        return remote(keep.at[m, pl.ds(4 * b1 + 2 * (1 - b2), 2), :, cols], r2.at[m, :, :, cols], s2_sems.at[n], q2_sems.at[n], peer)

    def copy_three(n):
        (b1, b2, b3), (_, _, peer) = way(n)
        m, cols = part_of(n)
        return remote(keep.at[m, 4 * b1 + 2 * b2 + 1 - b3, :, cols], r3.at[m, :, cols], s3_sems.at[n], q3_sems.at[n], peer)

    def own_block(n):
        (b1, b2, b3), _ = way(n)
        m, cols = part_of(n)
        return keep.at[m, 4 * b1 + 2 * b2 + b3, :, cols]

    def step_one(n):
        core_copy(n).wait_recv()
        keep[n] = add_low(keep[n], crecv[n % RING])

    def step_two(n):
        (b1, *_), _ = way(n)
        copy_one(n).wait()
        m, cols = part_of(n)
        at = pl.ds(4 * b1, 4)
        keep[m, at, :, cols] = add_low(keep[m, at, :, cols], r1[m, :, :, cols])
        if WAYS[n] != "f":
            copy_two(n).start()

    def step_three(n):
        if WAYS[n] == "f":
            return
        (b1, b2, *_), _ = way(n)
        copy_two(n).wait()
        m, cols = part_of(n)
        at = pl.ds(4 * b1 + 2 * b2, 2)
        keep[m, at, :, cols] = add_low(keep[m, at, :, cols], r2[m, :, :, cols])
        if WAYS[n] != "e":
            copy_three(n).start()

    def final_to(n, slot, peer):
        m, cols = part_of(n)
        return remote(own_block(n), rf.at[m, slot, :, cols], sf_sems.at[n], qf_sems.at[n, slot], peer)

    def sends_final(n, act):
        if WAYS[n] != "b":
            @pl.when(y == 1)
            def _():
                act(final_to(n, 0, flip_y))
            return

        @pl.when((y == 1) & (zh == 1))
        def _():
            act(final_to(n, 0, flip_y))

        @pl.when((y == 0) & (zh == 1))
        def _():
            act(final_to(n, 0, flip_zh))

        @pl.when((y == 1) & (zh == 0))
        def _():
            act(final_to(n, 1, flip_yzh))

    def cross_final(n):
        src = keep.at[n, pl.ds(2 * x, 2)] if WAYS[n] == "e" else keep.at[n, pl.ds(4 * x, 4)]
        count = 2 if WAYS[n] == "e" else 4
        return remote(src, rc.at[n // 2, pl.ds(0, count)], sf_sems.at[n], qf_sems.at[n, 0], flip_y)

    def step_final(n):
        if WAYS[n] in "ef":
            @pl.when(y == 0)
            def _():
                cross_final(n).start()
            return
        copy_three(n).wait()
        (b1, b2, b3), _ = way(n)
        m, cols = part_of(n)
        at = 4 * b1 + 2 * b2 + b3
        keep[m, at, :, cols] = add_low(keep[m, at, :, cols], r3[m, :, cols])
        sends_final(n, lambda copy: copy.start())

    def put(u, value, cols=slice(0, 16 * PART)):
        def columns(j):
            return pl.ds(pl.multiple_of(j * width, width), width)

        @pl.when(u < 4)
        def _():
            dup_ref[:, columns(u)] = value

        @pl.when((u >= 4) & (u < 8))
        def _():
            ddown_ref[pl.ds(pl.multiple_of((u - 4) * PART, PART), PART), :] = value

        @pl.when(u == 8)
        def _():
            dout_ref[...] = value

        for j in range(GROUPS):
            @pl.when(u == EARLY + j)
            def _(j=j):
                for part in range(3):
                    first, last = max(part * GROUP, cols.start), min((part + 1) * GROUP, cols.stop)
                    if first < last:
                        to = part * (width - GROUP) + j * GROUP
                        dqkv_ref[:, to + first : to + last] = value[:, first - cols.start : last - cols.start]

    def step_out(n):
        if WAYS[n] in "ef":
            return cross_step_out(n)
        m, cols = part_of(n)
        u = n // 2 if n < 2 * CROSS_UNITS else m - CROSS_UNITS
        sends_final(n, lambda copy: copy.wait_send())

        @pl.when(y == 0)
        def _():
            final_to(n, 0, flip_y).wait_recv()
            straight = (zh == 0) if WAYS[n] == "b" else (y == 0)

            @pl.when(straight)
            def _():
                put(u, own_block(n)[...].astype(F32) + rf[m, 0, :, cols].astype(F32), cols)

            if WAYS[n] == "b":
                @pl.when(zh == 1)
                def _():
                    final_to(n, 1, flip_y).wait_recv()
                    put(u, rf[m, 0, :, cols].astype(F32) + rf[m, 1, :, cols].astype(F32), cols)

    def cross_step_out(n):
        @pl.when(y == 0)
        def _():
            cross_final(n).wait_send()

        @pl.when(y == 1)
        def _():
            cross_final(n).wait_recv()
            for sub in range(4):
                if WAYS[n] == "f":
                    block = keep[n, 4 * x + sub].astype(F32) + rc[n // 2, sub].astype(F32)
                else:
                    block = (rc[n // 2, sub] if sub < 2 else keep[n, 4 + 2 * x + sub - 2]).astype(F32)
                put(2 * n + sub, block)

    small_peers = (flip_c, flip_x, flip_y, flip_zl, flip_zh)

    rounds = ((acc, racc), (late_acc, late_racc))

    def small_copy(late, d):
        own, other = rounds[late]
        return remote(own.at[d], other.at[d], sa_sems.at[late, d], qa_sems.at[late, d], small_peers[d])

    def small_step(late, d):
        own, other = rounds[late]
        small_copy(late, d).wait()
        own[d + 1] = own[d] + other[d]
        if d + 1 < len(small_peers):
            small_copy(late, d + 1).start()
        elif late:
            small_ref[0:8, :] = acc[d + 1, 0:8, :] + own[d + 1]
            small_ref[8:32, :] = acc[d + 1, 8:32, :]

    seg_rows = [jnp.sum(sums[i], axis=0, keepdims=True) for i in range(6)]
    seg_up = jnp.sum(bsums[...], axis=0, keepdims=True)
    order = (6, 7, 5, 4, 2, 1)
    for i, row in enumerate(order):
        if row < 6:
            acc[0, i : i + 1, :] = seg_rows[row]
        acc[0, 6 + i : 7 + i, :] = csums[row : row + 1, :] * share
    for i, row in enumerate((3, 0)):
        acc[0, 12 + i : 13 + i, :] = seg_rows[row]
        acc[0, 14 + i : 15 + i, :] = csums[row : row + 1, :] * share
    for i in range(4):
        acc[0, 16 + i : 17 + i, :] = seg_up[:, i * width : (i + 1) * width]
        acc[0, 20 + i : 21 + i, :] = cbsums[:, i * width : (i + 1) * width] * share
    acc[0, 0:2, :] = jnp.zeros_like(acc[0, 0:2, :])
    acc[0, 24:32, :] = gpos[...] * share
    late_acc[0] = jnp.zeros_like(late_acc[0])

    def cross_unit(n, parts):
        if n >= RING:
            core_copy(n).wait_send()
        for rel in (1, 0):
            core = c if rel == 0 else 1 - c
            for sub, (left, right) in enumerate(parts):
                for far in range(2):
                    value = mm(left(far, core), right).astype(BF16)
                    at = (sub // 2) * 4 + far * 2 + sub % 2 if WAYS[n] == "e" else far * 4 + sub
                    if rel == 1:
                        csend[n % RING, at] = value
                    else:
                        keep[n, at] = value
            if rel == 1:
                if n == 0:
                    pl.semaphore_wait(barrier, 6)
                core_copy(n).start()

    def plain(ref):
        return lambda far, core: ref[far, core, z]

    def nested(ref, j):
        return lambda far, core: ref[far, core, z, j]

    def cut(ref, j):
        return ref[:, j * width : (j + 1) * width]

    def cut_group(ref, j):
        return jnp.concatenate([ref[:, part * width + j * GROUP : part * width + (j + 1) * GROUP] for part in range(3)], axis=1)

    cross_parts = (
        lambda: [(plain(cfirstt), cut(cginner, j)) for j in range(4)],
        lambda: [(nested(chiddent, j), cgsecond[...]) for j in range(4)],
        lambda: [(plain(cmixedt), cgbranch[...])] + [(plain(cxt), cut_group(cgqkv, j)) for j in range(GROUPS)],
    )

    def compute(u):
        n = u + CROSS_UNITS - jnp.maximum(CROSS_UNITS - 1 - u, 0)
        @pl.when(n >= RING)
        def _():
            core_copy(n).wait_send()

        sides = []
        for side in range(2):
            chains, chain = tuple(range(UNITS - 1)) + (UNITS - 1 + side,), n + side * (n // (UNITS - 1))
            sides.append((among(chain, "b", chains), among(chain, "c", chains)))
        right = bslot[b_slot(u)]
        for rel in (1, 0):
            core = c if rel == 0 else 1 - c
            left = aslot[a_slot(u), :, core].reshape(8 * PART, -1)
            value = mm(left, right).astype(BF16)
            for far in range(2):
                for part in range(4):
                    block = value[(far * 4 + part) * PART : (far * 4 + part + 1) * PART]
                    for side in range(2):
                        at = block_place(*sides[side], far, part // 2, part % 2)
                        cols = slice(side * width // 2, (side + 1) * width // 2)
                        if rel == 1:
                            csend[n % RING, at, :, cols] = block[:, cols]
                        else:
                            keep[n, at, :, cols] = block[:, cols]
            if rel == 1:
                core_copy(n).start()

        @pl.when(n < CROSS_UNITS + EARLY)
        def _():
            step_one(n - 1)

    def attention_tile(j, i):
        slot = i % 2
        out_rows = pl.ds(pl.multiple_of(j * GROUP, GROUP), GROUP)
        g_mixed = mm_nt(gbranch_slot[slot], wout[out_rows, :]).astype(BF16)
        items = [(seg, half) for seg in range(segs) for half in range(2)]
        at = [slice(seg * SEGLEN, (seg + 1) * SEGLEN) for seg, _ in items]
        lanes = [pair_lanes(half) for _, half in items]
        to = [pl.ds(pl.multiple_of(i * tile + seg * SEGLEN, SEGLEN), SEGLEN) for seg, _ in items]
        every = range(len(items))
        g_out = [stack_heads(g_mixed[at[e], lanes[e][0]]) for e in every]
        g_p = [mm_nt(qkv_slot[slot, at[e], lanes[e][2]], g_out[e]) for e in every]
        g_v = [mm(probs_slot[slot, seg, half], g_out[e]) for e, (seg, half) in enumerate(items)]
        g_s = []
        for e, (seg, half) in enumerate(items):
            p = probs_slot[slot, seg, half].astype(F32)
            g_s.append((p * (g_p[e] - jnp.sum(g_p[e] * p, axis=0, keepdims=True))).astype(BF16))
        g_k = [mm(g_s[e], stack_heads(qkv_slot[slot, at[e], lanes[e][0]] * HDIM**-0.5)) for e in every]
        g_st = [jnp.concatenate([g_s[e][:, :SEGLEN].T, g_s[e][:, SEGLEN:].T], axis=1) for e in every]
        g_q = [mm(g_st[e], stack_heads(qkv_slot[slot, at[e], lanes[e][1]])) * HDIM**-0.5 for e in every]
        for e in every:
            for part, value in enumerate((g_q[e], g_k[e], g_v[e])):
                value = value.astype(BF16)
                bslot[j, to[e], lanes[e][part]] = value
                if part != 1:
                    fold[part // 2, j, :, lanes[e][0]] += fold_rows(value.astype(F32))

    def last_tile(i):
        slot = i % 2

        @pl.when(i >= 2)
        def _():
            store_gx(i - 2).wait()

        total = gbranch_slot[slot].astype(F32)
        for j in range(GROUPS):
            total = total + mm_nt(bslot[j, tile_rows(i), :], wqkv[j])
        gx_slot[slot] = total.astype(BF16)
        store_gx(i).start()

    def run(action, n):
        if action in ("small", "late"):
            late = int(action == "late")
            if late and n == 0:
                for row in range(2):
                    for j in range(GROUPS):
                        late_acc[0, row : row + 1, j * GROUP : (j + 1) * GROUP] = jnp.sum(fold[row, j], axis=0, keepdims=True)
            if n == 0:
                small_copy(late, 0).start()
            else:
                small_step(late, n - 1)
            return
        {
            "one": step_one, "send": lambda n: copy_one(n).start(), "two": step_two, "three": step_three, "final": step_final, "out": step_out,
        }[action](n)

    schedule = comm_schedule()

    def step(s, carry):
        for at in range(STEPS):
            if schedule[at]:
                @pl.when(s == at)
                def _(at=at):
                    for action, n in schedule[at]:
                        run(action, n)

        @pl.when(s == EARLY)
        def _():
            for copy in weight_copies:
                copy.wait()

        for i in range(1, CROSS_UNITS):
            @pl.when(s == i)
            def _(i=i):
                cross_unit(2 * i, cross_parts[i]())
                step_one(2 * i - 1)
                copy_one(2 * i - 1).start()

        load(s, "wait")

        @pl.when(s == 1)
        def _():
            for copy in weight_copies:
                copy.start()

        @pl.when(s + 1 < STEPS)
        def _():
            load(s + 1, "start")

        group, part = place(s)
        inside = (s >= EARLY) & (s < LAST_AT)
        multiply = (s < EARLY) | (inside & (part == TILES))

        @pl.when(multiply)
        def _():
            compute(jnp.where(s < EARLY, s, EARLY + group))

        @pl.when(inside & (part < TILES))
        def _():
            attention_tile(group, part)

        @pl.when(s >= LAST_AT)
        def _():
            last_tile(s - LAST_AT)

        return carry

    fold[...] = jnp.zeros_like(fold)
    cross_unit(0, cross_parts[0]())
    lax.fori_loop(0, STEPS, step, 0)
    for action, n in schedule[STEPS]:
        run(action, n)
    for i in range(TILES - 2, TILES):
        store_gx(i).wait()
    for n in range(UNITS - RING, UNITS):
        core_copy(n).wait_send()


def late_backward(big, cross, small, attn, share):
    firstt, ginner, hiddent, gsecond, mixedt, gbranch, xt = big
    qkv, probs, w_qkv, w_out = attn
    cfirstt, cginner, chiddent, cgsecond, cmixedt, cgbranch, cxt, cgqkv = cross
    width, depth = firstt.shape
    inners = ginner.shape[1]
    rows = cfirstt.shape[1]
    tile = depth // TILES
    assert width == 16 * PART and inners == 4 * width

    def blocks(a, n):
        return a.reshape((2, 2, 4) + ((n,) if n > 1 else ()) + (PART, a.shape[1]))

    operands = [
        blocks(firstt, 1), ginner, blocks(hiddent, 4), gsecond, blocks(mixedt, 1), gbranch, blocks(xt, 1), qkv, probs, w_qkv, w_out,
        blocks(cfirstt, 1), cginner, blocks(chiddent, 4), cgsecond, blocks(cmixedt, 1), cgbranch, blocks(cxt, 1), cgqkv, *small,
    ]
    vmem = pl.BlockSpec(memory_space=pltpu.VMEM)
    any_spec = pl.BlockSpec(memory_space=pl.ANY)
    outs = [((PART, 3 * width), F32), ((PART, width), F32), ((PART, inners), F32), ((4 * PART, width), F32), ((32, width), F32), ((depth, width), BF16)]
    segs = tile // SEGLEN
    dma = pltpu.SemaphoreType.DMA
    return pl.pallas_call(
        functools.partial(late_kernel, share=share),
        in_specs=[any_spec] * 11 + [vmem] * (len(operands) - 11),
        out_specs=[vmem] * 5 + [any_spec],
        out_shape=[jax.ShapeDtypeStruct(*o) for o in outs],
        scratch_shapes=[
            pltpu.VMEM((2, 2, 2, 4, PART, depth), BF16),
            pltpu.VMEM((GROUPS, depth, width), BF16),
            pltpu.VMEM((2, tile, width), BF16),
            pltpu.VMEM((2, segs, 2, SEGLEN, 2 * SEGLEN), BF16),
            pltpu.VMEM((2, tile, width), BF16),
            pltpu.VMEM((2, tile, width), BF16),
            pltpu.VMEM((GROUPS, width, 3 * GROUP), BF16),
            pltpu.VMEM(w_out.shape[1:], BF16),
            pltpu.VMEM((2, GROUPS, 8, GROUP), F32),
            pltpu.VMEM((RING, 8, PART, width), BF16),
            pltpu.VMEM((RING, 8, PART, width), BF16),
            pltpu.VMEM((UNITS, 8, PART, width), BF16),
            pltpu.VMEM((UNITS, 4, PART, width), BF16),
            pltpu.VMEM((UNITS, 2, PART, width), BF16),
            pltpu.VMEM((UNITS, PART, width), BF16),
            pltpu.VMEM((UNITS, 2, PART, width), BF16),
            pltpu.VMEM((CROSS_UNITS, 4, PART, width), BF16),
            pltpu.VMEM((6, 32, width), F32),
            pltpu.VMEM((5, 32, width), F32),
            pltpu.VMEM((6, 8, width), F32),
            pltpu.VMEM((5, 8, width), F32),
            dma((2,)), dma((2, 3)), dma((2,)), dma((1 + 3 * GROUPS,)), dma((RING,)), dma((RING,)), dma((CHAINS,)), dma((CHAINS,)), dma((CHAINS,)), dma((CHAINS,)),
            dma((CHAINS,)), dma((CHAINS,)), dma((CHAINS,)), dma((CHAINS, 2)), dma((2, 5)), dma((2, 5)),
        ],
        compiler_params=pltpu.CompilerParams(vmem_limit_bytes=63 * 2**20, collective_id=1, has_side_effects=True),
        name="late_backward",
    )(*operands)

def finish_kernel(gx_ref, a_ref, b_ref, c_ref, d_ref, gx_out, a_out, b_out, c_out, d_out):
    gx_out[...] = gx_ref[...].astype(F32)

    @pl.when(pl.program_id(0) == 0)
    def _():
        for src, dst in ((a_ref, a_out), (b_ref, b_out), (c_ref, c_out), (d_ref, d_out)):
            dst[...] = src[...]


def finish(gx, grads, tile=1024):
    total, width = gx.shape
    rows = pl.BlockSpec((tile, width), lambda i: (i, 0))
    held = [pl.BlockSpec(g.shape, lambda i: (0, 0)) for g in grads]
    return pl.pallas_call(
        finish_kernel,
        grid=(total // tile,),
        in_specs=[rows] + held,
        out_specs=[rows] + held,
        out_shape=[jax.ShapeDtypeStruct(gx.shape, F32)] + [jax.ShapeDtypeStruct(g.shape, F32) for g in grads],
        name="finish",
    )(gx, *grads)


def small_grads(sums, bsums, csums, cbsums, gpos, bias_sums, cross_share):
    seg_rows = jnp.concatenate([jnp.sum(sums, axis=1), bias_sums])
    cross_rows = csums * cross_share
    order = jnp.array([6, 7, 5, 4, 2, 1])
    biases = jnp.stack([seg_rows[order], cross_rows[order]])
    gains = jnp.stack([seg_rows[jnp.array([3, 0])], cross_rows[jnp.array([3, 0])]])
    ups = jnp.stack([jnp.sum(bsums, axis=0), cbsums[0] * cross_share])
    return biases.reshape(-1), gains.reshape(-1), ups.reshape(-1), (gpos * cross_share).reshape(-1)


def attention_back(qkv, probs, gbranch, w_qkv, w_out):
    total, width = gbranch.shape
    heads = width // HDIM
    segs = total // SEGLEN
    scale = HDIM**-0.5

    def split(a):
        return a.reshape(segs, SEGLEN, heads, HDIM)

    def merge(a):
        return a.reshape(total, width)

    q, k, v = (
        split(qkv[:, :, part * GROUP : (part + 1) * GROUP].transpose(1, 0, 2).reshape(total, width)) for part in range(3)
    )
    p_low = probs.reshape(segs, heads // 2, SEGLEN, 2, SEGLEN).transpose(0, 1, 3, 2, 4).reshape(segs, heads, SEGLEN, SEGLEN)
    g_out = split(mm_nt(gbranch, w_out).astype(BF16))
    p = p_low.astype(F32)
    g_p = jnp.einsum("sqhd,skhd->shkq", g_out, v, preferred_element_type=F32)
    g_s = (p * (g_p - jnp.sum(g_p * p, axis=2, keepdims=True))).astype(BF16)
    g_v = jnp.einsum("shkq,sqhd->skhd", p_low, g_out, preferred_element_type=F32)
    g_k = jnp.einsum("shkq,sqhd->skhd", g_s, q, preferred_element_type=F32) * scale
    g_q = jnp.einsum("shkq,skhd->sqhd", g_s, k, preferred_element_type=F32) * scale
    g_qkv = jnp.concatenate([merge(g_q), merge(g_k), merge(g_v)], axis=1).astype(BF16)
    return g_qkv, gbranch.astype(F32) + mm_nt(g_qkv, w_qkv)


def generic_total(seg_pairs, cross_pairs, small, planes, own):
    axes = ("row", "seg")
    me = lax.axis_index("seg")
    shards = [
        lax.psum_scatter(part, axes, scatter_dimension=0, tiled=True) for part in small_grads(*small, 1.0 / planes)
    ]

    def mine(values, dim):
        return lax.dynamic_slice_in_dim(values, me * own, own, dim)

    big = []
    for at in (6, 4, 0, 2):
        cross = mm(mine(cross_pairs[at], 1), mine(cross_pairs[at + 1], 0))
        both = jnp.concatenate([mm(seg_pairs[at], seg_pairs[at + 1]), cross], axis=0)
        big.append(lax.psum_scatter(both, axes, scatter_dimension=0, tiled=True))
    return big, shards


def per_device(
    tokens, doc_ids, w_qkv, w_out, w_up, w_down, biases, gains, b_up, pos_table, cotangent, *, sizes
):
    lines, planes = sizes
    row_count, local_length, width = tokens.shape
    seg_here = local_length // SEGLEN
    segments = doc_ids.shape[1]
    total = row_count * local_length
    own = row_count * seg_here
    cot = cotangent.reshape(total, width)
    (
        qkv, probs, n1, r1, slope, n2, r2, y, xt, mixedt, firstt, hiddent,
        ccls, gcls, csums, cbsums, gpos, cxt, cmixedt, cfirstt, chiddent, cgqkv, cgbranch, cginner, cgsecond,
    ) = forward_blocks(
        tokens.reshape(total, width), cot, w_qkv, w_out, w_up, w_down, biases, gains, b_up, doc_ids, pos_table, planes,
        tile=256 if planes <= 4 else 128,
    )
    output, gsecond, ginner, gbranch, sums, bsums = early_backward(
        gcls, ccls, cot, y, n2, r2, slope, n1, r1, w_up, w_down, gains
    )
    cross_pairs = (cfirstt, cginner, chiddent, cgsecond, cmixedt, cgbranch, cxt, cgqkv)
    share = 1.0 / planes
    if (lines, planes) == (8, 4) and total == 2048 and width == 16 * PART:
        *grads, small, gx = late_backward(
            (firstt, ginner, hiddent, gsecond, mixedt, gbranch, xt), cross_pairs, (sums, bsums, csums, cbsums, gpos), (qkv, probs, w_qkv, w_out), share
        )
        gx, *grads = finish(gx, grads)
        small = small.reshape(-1)
        index = lax.axis_index("row") * planes + lax.axis_index("seg")
        shards, start = [], 0
        for size in (12 * width, 4 * width, 8 * width, segments * width):
            count = size // (lines * planes)
            shards.append(lax.dynamic_slice_in_dim(small, start + index * count, count, 0))
            start += size
    else:
        gqkv, gx = attention_back(qkv, probs, gbranch, w_qkv[0], w_out[0])
        bias_sums = jnp.stack([jnp.sum(gqkv[:, at : at + width].astype(F32), axis=0) for at in (0, 2 * width)])
        grads, shards = generic_total(
            (firstt, ginner, hiddent, gsecond, mixedt, gbranch, xt, gqkv), cross_pairs, (sums, bsums, csums, cbsums, gpos, bias_sums), planes, own
        )
    return (output.reshape(tokens.shape), gx.reshape(tokens.shape), *grads, *shards)


def solution(mesh):
    sizes = (mesh.shape["row"], mesh.shape["seg"])
    tokens_at = P("row", "seg", None)
    return jax.shard_map(
        functools.partial(per_device, sizes=sizes),
        mesh=mesh,
        in_specs=(tokens_at, P("row", None)) + (P(),) * 8 + (tokens_at,),
        out_specs=(tokens_at, tokens_at) + (P(("row", "seg"), None),) * 4 + (P(("row", "seg")),) * 4,
        check_vma=False,
    )
```
